32 devices in a mesh: replica: 2 (over y), dp: 4 (over x, core), tp: 4 (over z).
Axes of the slice: x: 2, y: 2, z: 4, core: 2. Of those that a mesh axis runs over, the one named last changes fastest.
Arguments:
- query_nope: bfloat16 [2048, 64, 128], P(('replica', 'dp'), 'tp'), parts along dimension 0, may hold values from -6 to 6
- query_rope: bfloat16 [2048, 4096], P(('replica', 'dp'), 'tp'), parts along dimension 0, may hold values from -8 to 8
- new_latent: bfloat16 [2048, 512], P(('replica', 'dp')), parts along dimension 0, may hold values from -6 to 6
- new_rope: bfloat16 [2048, 64], P(('replica', 'dp')), parts along dimension 0, may hold values from -8 to 8
- cache_latent: bfloat16 [256, 64, 512], P(('replica', 'dp')), parts along dimension 0, may hold values from -6 to 6
- cache_rope: bfloat16 [256, 4096], P(('replica', 'dp')), parts along dimension 0, may hold values from -8 to 8
- absorb_key: bfloat16 [64, 128, 512], P('tp'), may hold values from -0.5 to 0.5
- absorb_value: bfloat16 [64, 512, 128], P('tp'), may hold values from -0.25 to 0.25
- output_weight: bfloat16 [8192, 7168], P('tp', 'dp'), may hold values from -0.5 to 0.5
- send_blocks: int32 [8, 4, 2], P(('replica', 'dp')), parts along dimension 0, may hold values from 0 to 31
- prefill_table: int32 [8, 16], P(('replica', 'dp')), parts along dimension 0, may hold values from 0 to 31, as said below
- prefill_offset: int32 [8], P(('replica', 'dp')), parts along dimension 0, may hold values from 0 to 1024, as said below
- decode_table: int32 [128, 4], P(('replica', 'dp')), parts along dimension 0, may hold values from 0 to 39
- decode_length: int32 [128], P(('replica', 'dp')), parts along dimension 0, may hold values from 1 to 256, as said below
Outputs:
- mixed: bfloat16 [2048, 7168], P(('replica', 'tp'), 'dp'), parts along dimension 0
The draws below stay inside these ranges and needn't reach their ends.
There are 2 independent parts, one for each index of `replica`. The reference program is written for one: setup_inputs(seed, part) draws one part's arguments, and reference() takes and returns one part's arrays. A program takes and returns all parts, laid end to end along the dimension named above; an argument that names none is the same for every part. Nothing has to cross between parts.
Inputs may be any that keep to these rules, and one draw needn't show every extreme that they name: `prefill_table`: each row names 16 different blocks. Some group has prefill_offset 16 * 64. `decode_length`: some request has 256 cached tokens. `decode_table`: numbers below 32 name the group's own blocks; 32 + s * 2 + k names slot k of what group s sends it; numbers may repeat.
All inputs are finite; a program needn't handle non-finite values.
Results may differ from the reference program's by a relative error of at most 0.017.
Values may be sent and summed in bfloat16 or wider, within the bound.
No kernel may reach another device: no remote copies, remote signals or barrier semaphores. Data moves between devices by JAX's collectives and lax.ppermute only.
A program may use at most 192 MiB of HBM per device.

```python
import jax
import jax.numpy as jnp
from jax import lax

D = 7168
H = 64
DN = 128
R = 64
L = 512
DV = 128
BS = 64
CAP = 2
POOL = 32
MAXB = 4
MAXPB = 16
DEC = 16
PRE = 240
GROUPS = 4
HG = 16
T_GRP = 256
TOKENS = 1024
N_TP = 4


def draw_query_rope(key, part):
    key = jax.random.fold_in(key, 11)
    values = jnp.clip(jax.random.normal(key, (TOKENS, H, R), jnp.float32), -6.0, 6.0)
    return values.reshape(TOKENS, H * R).astype(jnp.bfloat16)


def draw_new_rope(key, part):
    key = jax.random.fold_in(key, 12)
    values = jnp.clip(jax.random.normal(key, (TOKENS, R), jnp.float32), -6.0, 6.0)
    return values.astype(jnp.bfloat16)


def draw_cache_rope(key, part):
    key = jax.random.fold_in(key, 13)
    values = jnp.clip(jax.random.normal(key, (GROUPS * POOL, BS, R), jnp.float32), -6.0, 6.0)
    return values.reshape(GROUPS * POOL, BS * R).astype(jnp.bfloat16)


def draw_prefill_table(key, part):
    key = jax.random.fold_in(key, 14)
    group_keys = jax.random.split(key, GROUPS)
    tables = jax.vmap(lambda single: jax.random.permutation(single, POOL)[:MAXPB])(group_keys)
    return tables.astype(jnp.int32)


def draw_prefill_offset(key, part):
    key = jax.random.fold_in(key, 15)
    first_key, second_key = jax.random.split(key)
    offsets = jax.random.randint(first_key, (GROUPS,), 0, MAXPB * BS + 1)
    longest = jax.random.randint(second_key, (), 0, GROUPS)
    return jnp.where(jnp.arange(GROUPS) == longest, MAXPB * BS, offsets).astype(jnp.int32)


def draw_decode_length(key, part):
    key = jax.random.fold_in(key, 16)
    first_key, second_key = jax.random.split(key)
    lengths = jax.random.randint(first_key, (GROUPS * DEC,), 1, MAXB * BS + 1)
    longest = jax.random.randint(second_key, (), 0, GROUPS * DEC)
    return jnp.where(jnp.arange(GROUPS * DEC) == longest, MAXB * BS, lengths).astype(jnp.int32)


def set_ends(values, key, smallest, high):
    longest = values.shape.index(max(values.shape))
    spots = []
    for shift in (0, 1):
        where = [jax.random.randint(jax.random.fold_in(key, axis), (), 0, length) for axis, length in enumerate(values.shape)]
        where[longest] = (where[longest] + shift) % values.shape[longest]
        spots.append(tuple(where))
    return values.at[spots[0]].set(smallest).at[spots[1]].set(high)


def block_levels(own_key, shape, cuts, smallest, largest):
    def one(position, blocks):
        steps = jax.random.uniform(jax.random.fold_in(jax.random.fold_in(own_key, 6), position), (blocks,), jnp.float32, smallest / len(cuts), largest / len(cuts))
        return jnp.repeat(jnp.exp(steps), shape[position] // blocks).reshape((-1,) + (1,) * (len(shape) - position - 1))

    level = one(*cuts[0])
    for cut in cuts[1:]:
        level = level * one(*cut)
    return level


def noise(rng, dims, width, bound, pieces=(), kind=jnp.bfloat16):
    level = block_levels(rng, dims, pieces, -0.22, 0.18) if pieces else 1.0
    values = jax.random.normal(rng, dims, jnp.float32) * width * level
    return jnp.minimum(jnp.maximum(values, -bound), bound).astype(kind)


def setup_inputs(seed: int = 0, part: int = 0) -> dict:
    splits = jax.random.split(jax.random.key(seed), 15)
    own_keys = jax.random.split(jax.random.fold_in(splits[14], part), 15)
    return {
        "query_nope": noise(own_keys[0], (TOKENS, H, DN), 1.0, 6.0, ((0, 4), (1, 4))),
        "query_rope": draw_query_rope(jax.random.fold_in(jax.random.fold_in(splits[14], part), 71), part),
        "new_latent": noise(own_keys[2], (TOKENS, L), 1.0, 6.0, ((0, 4),)),
        "new_rope": draw_new_rope(jax.random.fold_in(jax.random.fold_in(splits[14], part), 71), part),
        "cache_latent": noise(own_keys[4], (GROUPS * POOL, BS, L), 1.0, 6.0, ((0, 4),)),
        "cache_rope": draw_cache_rope(jax.random.fold_in(jax.random.fold_in(splits[14], part), 71), part),
        "absorb_key": noise(splits[6], (H, DN, L), DN ** -0.5, 0.5, ((0, 4),)),
        "absorb_value": noise(splits[7], (H, L, DV), L ** -0.5, 0.25, ((0, 4),)),
        "output_weight": noise(splits[8], (H * DV, D), DV ** -0.5, 0.5, ((0, 4), (1, 4))),
        "send_blocks": set_ends(jax.random.randint(own_keys[9], (GROUPS, GROUPS, CAP), 0, POOL), jax.random.fold_in(own_keys[9], 1), 0, POOL - 1).astype(jnp.int32),
        "prefill_table": draw_prefill_table(jax.random.fold_in(jax.random.fold_in(splits[14], part), 71), part),
        "prefill_offset": draw_prefill_offset(jax.random.fold_in(jax.random.fold_in(splits[14], part), 71), part),
        "decode_table": set_ends(jax.random.randint(own_keys[12], (GROUPS * DEC, MAXB), 0, POOL + GROUPS * CAP), jax.random.fold_in(own_keys[12], 1), 0, (POOL + GROUPS * CAP) - 1).astype(jnp.int32),
        "decode_length": draw_decode_length(jax.random.fold_in(jax.random.fold_in(splits[14], part), 71), part),
    }


def normalized(scores, visible):
    masked = jnp.where(visible, scores, -jnp.inf)
    row_top = jnp.max(masked, axis=-1, keepdims=True)
    exp_terms = jnp.where(visible, jnp.exp(masked - row_top), 0.0)
    return (exp_terms / jnp.sum(exp_terms, axis=-1, keepdims=True)).astype(jnp.bfloat16)


def group_heads(inputs, cache_latent, cache_rope, absorb_key, absorb_value):
    nope_group, rope_group, latent_group, newrope_group, sent_ids, prior_ids, offset, table_ids, lengths, group_index = inputs
    score_scale = (DN + R) ** -0.5
    q_latent = jnp.einsum("thd,hdl->thl", nope_group.astype(jnp.float32), absorb_key.astype(jnp.float32)).astype(jnp.bfloat16)
    rope_query = rope_group.reshape(T_GRP, H, R).astype(jnp.float32)
    own_ids = group_index * POOL + jnp.arange(POOL).astype(jnp.int32)
    flat_ids = (jnp.arange(GROUPS).astype(jnp.int32)[:, None] * POOL + sent_ids.astype(jnp.int32)).reshape(-1)
    ext_ids = jnp.concatenate([own_ids, flat_ids], 0).astype(jnp.int32)
    ext_latent = cache_latent[ext_ids]
    ext_rope = cache_rope[ext_ids]
    prior_len = MAXPB * BS
    key_latent = jnp.concatenate([ext_latent[prior_ids].reshape(prior_len, L), latent_group[:PRE]], 0).astype(jnp.float32)
    key_rope = jnp.concatenate([ext_rope[prior_ids].reshape(prior_len, R), newrope_group[:PRE]], 0).astype(jnp.float32)
    scores = (jnp.einsum("thl,kl->thk", q_latent[:PRE].astype(jnp.float32), key_latent)
              + jnp.einsum("the,ke->thk", rope_query[:PRE], key_rope)) * score_scale
    key_pos = jnp.arange(prior_len + PRE).astype(jnp.int32)
    token_pos = jnp.arange(PRE).astype(jnp.int32)
    visible = jnp.where(key_pos[None, :] < prior_len, key_pos[None, :] < offset, key_pos[None, :] - prior_len <= token_pos[:, None])
    weights = normalized(scores, visible[:, None, :])
    prefill_out = jnp.einsum("thk,kl->thl", weights.astype(jnp.float32), key_latent).astype(jnp.bfloat16)
    dec_span = MAXB * BS
    decode_latent = jnp.concatenate([ext_latent[table_ids].reshape(DEC, dec_span, L), latent_group[PRE:][:, None, :]], 1).astype(jnp.float32)
    decode_rope = jnp.concatenate([ext_rope[table_ids].reshape(DEC, dec_span, R), newrope_group[PRE:][:, None, :]], 1).astype(jnp.float32)
    dec_scores = (jnp.einsum("rhl,rkl->rhk", q_latent[PRE:].astype(jnp.float32), decode_latent)
                  + jnp.einsum("rhe,rke->rhk", rope_query[PRE:], decode_rope)) * score_scale
    slot_pos = jnp.arange(dec_span + 1).astype(jnp.int32)
    dec_visible = (slot_pos[None, :] < lengths[:, None]) | (slot_pos[None, :] == dec_span)
    dec_weights = normalized(dec_scores, dec_visible[:, None, :])
    decode_out = jnp.einsum("rhk,rkl->rhl", dec_weights.astype(jnp.float32), decode_latent).astype(jnp.bfloat16)
    attended = jnp.concatenate([prefill_out, decode_out], 0)
    head_out = jnp.einsum("thl,hlv->thv", attended.astype(jnp.float32), absorb_value.astype(jnp.float32)).astype(jnp.bfloat16)
    return head_out.reshape(T_GRP, H * DV)


def reference(query_nope, query_rope, new_latent, new_rope, cache_latent, cache_rope, absorb_key, absorb_value, output_weight, send_blocks, prefill_table, prefill_offset, decode_table, decode_length):
    rope_cache = cache_rope.reshape(GROUPS * POOL, BS, R)
    inputs = (query_nope.reshape(GROUPS, T_GRP, H, DN), query_rope.reshape(GROUPS, T_GRP, H * R),
              new_latent.reshape(GROUPS, T_GRP, L), new_rope.reshape(GROUPS, T_GRP, R),
              jnp.transpose(send_blocks, (1, 0, 2)), prefill_table, prefill_offset,
              decode_table.reshape(GROUPS, DEC, MAXB), decode_length.reshape(GROUPS, DEC),
              jnp.arange(GROUPS).astype(jnp.int32))
    head_out = lax.map(lambda item: group_heads(item, cache_latent, rope_cache, absorb_key, absorb_value), inputs)
    head_out = head_out.reshape(TOKENS, N_TP, HG * DV).transpose(1, 0, 2)
    weight_blocks = output_weight.reshape(N_TP, HG * DV, D)

    def add_group(total, pair):
        group_part = jnp.dot(pair[0], pair[1], preferred_element_type=jnp.float32).astype(jnp.bfloat16)
        return total + group_part.astype(jnp.float32), None

    total, _ = lax.scan(add_group, jnp.zeros((TOKENS, D), jnp.float32), (head_out, weight_blocks))
    return total.astype(jnp.bfloat16)
```

```python
import functools

import jax
import jax.numpy as jnp
from jax import lax
from jax.experimental import pallas as pl
from jax.experimental.pallas import tpu as pltpu
from jax.sharding import PartitionSpec as P

HIDDEN = -1e30
LANES = 128
VMEM_LIMIT = 48 * 1024 * 1024


def dot_nt(a, b):
    return lax.dot_general(a, b, (((1,), (1,)), ((), ())), preferred_element_type=jnp.float32)


def dot(a, b):
    return jnp.dot(a, b, preferred_element_type=jnp.float32)


def chunk_sizes(tok_group):
    if tok_group == 256:
        return (32, 64, 64, 96)
    return (tok_group,)


def attend_kernel(
    first,
    prefill_len,
    exp_scale,
    with_decode,
    table,
    offset,
    q_nope,
    q_rope,
    wk_hbm,
    wv_hbm,
    cache_latent,
    cache_rope,
    new_latent,
    new_rope,
    *rest,
):
    if with_decode:
        (recv_latent, recv_rope, decode_table, decode_length, out,
         wk, wv, keys, q, att, dkeys, sems, wsems, dsems) = rest
    else:
        out, wk, wv, keys, q, att, sems, wsems = rest
    heads, t, nope_dim = q_nope.shape
    block_len, latent = cache_latent.shape[1:]
    rope_dim = q_rope.shape[1] // heads
    blocks = table.shape[1]
    prior = blocks * block_len
    fresh = keys.shape[0] - prior

    wk_copy = pltpu.make_async_copy(wk_hbm, wk, wsems.at[0])
    wk_copy.start()
    copies = []
    for i in range(blocks):
        b = table[0, i]
        rows = pl.ds(i * block_len, block_len)
        copies.append(pltpu.make_async_copy(
            cache_latent.at[b], keys.at[rows, pl.ds(0, latent)], sems.at[2 * i]))
        copies.append(pltpu.make_async_copy(
            cache_rope.at[b], keys.at[rows, pl.ds(latent, LANES)], sems.at[2 * i + 1]))
    copies.append(pltpu.make_async_copy(
        new_latent.at[pl.ds(0, fresh)], keys.at[pl.ds(prior, fresh), pl.ds(0, latent)],
        sems.at[2 * blocks]))
    copies.append(pltpu.make_async_copy(
        new_rope.at[pl.ds(0, fresh)], keys.at[pl.ds(prior, fresh), pl.ds(latent, LANES)],
        sems.at[2 * blocks + 1]))
    for c in copies:
        c.start()
    wv_copy = pltpu.make_async_copy(wv_hbm, wv, wsems.at[1])
    wv_copy.start()
    dec_copies = []
    if with_decode:
        pool = cache_latent.shape[0]
        for i in range(pool):
            rows = pl.ds(i * block_len, block_len)
            dec_copies.append(pltpu.make_async_copy(
                cache_latent.at[i], dkeys.at[rows, pl.ds(0, latent)], dsems.at[2 * i]))
            dec_copies.append(pltpu.make_async_copy(
                cache_rope.at[i], dkeys.at[rows, pl.ds(latent, LANES)], dsems.at[2 * i + 1]))
        received = recv_latent.shape[0]
        tail = dkeys.shape[0] - pool * block_len - received
        start = new_latent.shape[0] - tail
        n = 2 * pool
        for src_l, src_r, at, size in (
            (recv_latent, recv_rope, pool * block_len, received),
            (new_latent.at[pl.ds(start, tail)], new_rope.at[pl.ds(start, tail)],
             pool * block_len + received, tail),
        ):
            dec_copies.append(pltpu.make_async_copy(
                src_l, dkeys.at[pl.ds(at, size), pl.ds(0, latent)], dsems.at[n]))
            dec_copies.append(pltpu.make_async_copy(
                src_r, dkeys.at[pl.ds(at, size), pl.ds(latent, LANES)], dsems.at[n + 1]))
            n += 2
        for c in dec_copies:
            c.start()

    lane = lax.broadcasted_iota(jnp.int32, (t, LANES), 1)
    one = jnp.where(lane == rope_dim, 1.0, 0.0)
    per_tile = LANES // rope_dim
    for h in range(heads):
        pair = q_rope[:, h // per_tile * LANES:(h // per_tile + 1) * LANES].astype(jnp.float32)
        turn = h % per_tile * rope_dim
        if turn:
            pair = pltpu.roll(pair, LANES - turn, 1)
        q[h * t:(h + 1) * t, latent:] = jnp.where(lane < rope_dim, pair, one).astype(jnp.bfloat16)
    wk_copy.wait()
    for h in range(heads):
        q[h * t:(h + 1) * t, :latent] = dot(q_nope[h], wk[h]).astype(jnp.bfloat16)

    for c in copies:
        c.wait()
    lane_k = lax.broadcasted_iota(jnp.int32, (prior, LANES), 1)
    pos_k = lax.broadcasted_iota(jnp.int32, (prior, LANES), 0)
    hide = jnp.where((lane_k == rope_dim) & (pos_k >= offset[0]), HIDDEN, 0.0)
    keys[:prior, latent:] = (keys[:prior, latent:].astype(jnp.float32) + hide).astype(jnp.bfloat16)

    together = 1
    while together * 2 <= heads and together * 2 * t <= 384:
        together *= 2
    tile = together * t
    token = first + lax.broadcasted_iota(jnp.int32, (t, fresh), 0)
    key_token = lax.broadcasted_iota(jnp.int32, (t, fresh), 1)
    causal = (key_token <= token)[None]

    def scores_of(i):
        rows = q[i * tile:(i + 1) * tile, :]
        return dot_nt(rows, keys[:prior, :]), dot_nt(rows, keys[prior:, :])

    steps = heads // together
    ahead = scores_of(0)
    for i in range(steps):
        s_old, s_new = ahead
        if i + 1 < steps:
            ahead = scores_of(i + 1)
        s_new = jnp.where(causal, s_new.reshape(together, t, fresh), HIDDEN).reshape(tile, fresh)
        top = jnp.maximum(jnp.max(s_old, axis=1, keepdims=True), jnp.max(s_new, axis=1, keepdims=True))
        p_old = jnp.exp2((s_old - top) * exp_scale)
        p_new = jnp.exp2((s_new - top) * exp_scale)
        total = jnp.sum(p_old, axis=1, keepdims=True) + jnp.sum(p_new, axis=1, keepdims=True)
        mixed = dot(p_old.astype(jnp.bfloat16), keys[:prior, :latent]) + dot(
            p_new.astype(jnp.bfloat16), keys[prior:, :latent])
        att[i * tile:(i + 1) * tile, :] = (mixed / total).astype(jnp.bfloat16)

    if with_decode:
        decodes = decode_table.shape[0]
        for c in dec_copies:
            c.wait()
        span = dkeys.shape[0]
        ext = span - tail
        key = lax.broadcasted_iota(jnp.int32, (decodes, span), 1)
        request = lax.broadcasted_iota(jnp.int32, (decodes, span), 0)
        block = key // block_len
        pos = key % block_len
        count = jnp.where(key - ext + start == request + prefill_len, 1.0, 0.0)
        for m in range(decode_table.shape[1]):
            hit = (block == decode_table[:, m:m + 1]) & (
                pos + m * block_len < decode_length[:, 0:1]) & (key < ext)
            count = count + jnp.where(hit, 1.0, 0.0)
        count = count[None]
        at = prefill_len - first
        half = heads // 2 if heads % 2 == 0 else heads
        for lo in range(0, heads, half):
            rows = jnp.concatenate(
                [q[h * t + at:h * t + at + decodes, :] for h in range(lo, lo + half)], axis=0)
            s = dot_nt(rows, dkeys[...]).reshape(half, decodes, span)
            s = jnp.where(count > 0.0, s, HIDDEN)
            top = jnp.max(s, axis=2, keepdims=True)
            p = count * jnp.exp2((s - top) * exp_scale)
            total = jnp.sum(p, axis=2, keepdims=True).reshape(half * decodes, 1)
            p = p.reshape(half * decodes, span).astype(jnp.bfloat16)
            mixed = (dot(p, dkeys[:, :latent]) / total).astype(jnp.bfloat16)
            for h in range(lo, lo + half):
                att[h * t + at:h * t + at + decodes, :] = mixed[(h - lo) * decodes:(h - lo + 1) * decodes]

    wv_copy.wait()
    dv = wv.shape[2]
    for h in range(heads):
        out[:, h * dv:(h + 1) * dv] = dot(att[h * t:(h + 1) * t, :], wv[h]).astype(jnp.bfloat16)


def attend(first, size, prefill_len, exp_scale, q_nope, q_rope, wk, wv, cache_latent, cache_rope,
           new_latent, new_rope, table, offset, decode=None):
    heads, _, latent = wk.shape
    tok_group = new_latent.shape[0]
    block_len = cache_latent.shape[1]
    blocks = table.shape[1]
    prior = blocks * block_len
    seen = min(first + size, prefill_len)
    fresh = min(-(-seen // LANES) * LANES, tok_group)
    width = latent + LANES
    dv = wv.shape[2]
    smem = pl.BlockSpec(memory_space=pltpu.SMEM)
    vmem = pl.BlockSpec(memory_space=pltpu.VMEM)
    hbm = pl.BlockSpec(memory_space=pl.ANY)
    args = [table, offset, q_nope, q_rope, wk, wv, cache_latent, cache_rope, new_latent, new_rope]
    in_specs = [smem, smem, vmem, vmem] + [hbm] * 6
    scratch = [
        pltpu.VMEM(wk.shape, jnp.bfloat16),
        pltpu.VMEM(wv.shape, jnp.bfloat16),
        pltpu.VMEM((prior + fresh, width), jnp.bfloat16),
        pltpu.VMEM((heads * size, width), jnp.bfloat16),
        pltpu.VMEM((heads * size, latent), jnp.bfloat16),
    ]
    flops = 2 * heads * size * ((prior + fresh) * (width + latent) + latent * 2 * LANES)
    if decode is not None:
        args += list(decode)
        in_specs += [hbm, hbm, vmem, vmem]
        received = decode[0].shape[0]
        pool = cache_latent.shape[0]
        span = pool * block_len + received + min(LANES, tok_group)
        scratch.append(pltpu.VMEM((span, width), jnp.bfloat16))
        flops += 2 * heads * decode[2].shape[0] * span * (width + latent)
    scratch += [pltpu.SemaphoreType.DMA((2 * blocks + 2,)), pltpu.SemaphoreType.DMA((2,))]
    if decode is not None:
        scratch.append(pltpu.SemaphoreType.DMA((2 * pool + 4,)))
    return pl.pallas_call(
        functools.partial(attend_kernel, first, prefill_len, exp_scale, decode is not None),
        out_shape=jax.ShapeDtypeStruct((size, heads * dv), jnp.bfloat16),
        in_specs=in_specs,
        out_specs=vmem,
        scratch_shapes=scratch,
        name="attend",
        compiler_params=pltpu.CompilerParams(vmem_limit_bytes=VMEM_LIMIT),
        cost_estimate=pl.CostEstimate(
            flops=2 * flops, bytes_accessed=6_000_000, transcendentals=heads * size * (prior + fresh)),
    )(*args)


def project_kernel(x, w, out):
    groups, t, depth = x.shape
    out[...] = dot(x[...].reshape(groups * t, depth), w[...]).astype(jnp.bfloat16).reshape(out.shape)


def project(x, w):
    groups, t, depth = x.shape
    columns = w.shape[1]
    step = 256 if columns % 256 == 0 else columns
    return pl.pallas_call(
        project_kernel,
        out_shape=jax.ShapeDtypeStruct((groups, t, columns), jnp.bfloat16),
        grid=(columns // step,),
        in_specs=[
            pl.BlockSpec((groups, t, depth), lambda j: (0, 0, 0)),
            pl.BlockSpec((depth, step), lambda j: (0, j)),
        ],
        out_specs=pl.BlockSpec((groups, t, step), lambda j: (0, 0, j)),
        name="project",
        compiler_params=pltpu.CompilerParams(vmem_limit_bytes=VMEM_LIMIT),
        cost_estimate=pl.CostEstimate(
            flops=2 * groups * t * depth * columns, bytes_accessed=2 * depth * columns, transcendentals=0),
    )(x, w)


def body(
    query_nope,
    query_rope,
    new_latent,
    new_rope,
    cache_latent,
    cache_rope,
    absorb_key,
    absorb_value,
    output_weight,
    send_blocks,
    prefill_table,
    prefill_offset,
    decode_table,
    decode_length,
):
    tok_group, heads, nope_dim = query_nope.shape
    pool_blocks, block_len, latent_dim = cache_latent.shape
    rope_dim = new_rope.shape[1]
    capacity = send_blocks.shape[2]
    group_count = lax.axis_size("dp")
    prefill_len = tok_group - decode_length.shape[0]
    exp_scale = float((nope_dim + rope_dim) ** (-0.5) * 1.4426950408889634)

    padded_rope = jnp.pad(
        cache_rope.reshape(pool_blocks, block_len, rope_dim), ((0, 0), (0, 0), (0, LANES - rope_dim)))
    padded_new = jnp.pad(new_rope, ((0, 0), (0, LANES - rope_dim)))

    outgoing = send_blocks[0]
    send = jnp.concatenate([cache_latent[outgoing], padded_rope[outgoing]], axis=3)
    me = lax.axis_index("dp")
    parts = [lax.dynamic_index_in_dim(send, me, 0, keepdims=False)]
    for shift in range(1, group_count):
        there = lax.rem(me + shift, group_count)
        parts.append(lax.ppermute(
            lax.dynamic_index_in_dim(send, there, 0, keepdims=False), "dp",
            [(i, (i + shift) % group_count) for i in range(group_count)]))
    received = jnp.stack(parts[::-1], axis=0)
    received = jnp.roll(received, me + 1, axis=0)
    received = received.reshape(group_count * capacity * block_len, latent_dim + LANES)

    first = 0
    outs = []
    sizes = chunk_sizes(tok_group)
    for n, size in enumerate(sizes):
        decode = None
        if n == len(sizes) - 1:
            decode = (received[:, :latent_dim], received[:, latent_dim:], decode_table,
                      decode_length[:, None])
        head_out = attend(
            first, size, prefill_len, exp_scale,
            query_nope[first:first + size].transpose(1, 0, 2), query_rope[first:first + size],
            absorb_key, absorb_value, cache_latent, padded_rope, new_latent, padded_new,
            prefill_table, prefill_offset, decode)
        gathered = lax.all_gather(head_out, "dp", axis=0, tiled=False)
        partials = project(gathered, output_weight)
        outs.append(lax.psum_scatter(partials, "tp", scatter_dimension=0, tiled=False))
        first += size
    return jnp.concatenate(outs, axis=0)


def solution(mesh):
    return jax.shard_map(
        body,
        mesh=mesh,
        in_specs=(
            P(("replica", "dp"), "tp", None),
            P(("replica", "dp"), "tp"),
            P(("replica", "dp"), None),
            P(("replica", "dp"), None),
            P(("replica", "dp"), None, None),
            P(("replica", "dp"), None),
            P("tp", None, None),
            P("tp", None, None),
            P("tp", "dp"),
            P(("replica", "dp"), None, None),
            P(("replica", "dp"), None),
            P(("replica", "dp")),
            P(("replica", "dp"), None),
            P(("replica", "dp")),
        ),
        out_specs=P(("replica", "tp"), "dp"),
        check_vma=False,
    )
```

```python
import functools

import jax
import jax.numpy as jnp
import numpy as np
from jax import lax
from jax.experimental import pallas as pl
from jax.experimental.pallas import tpu as pltpu
from jax.sharding import PartitionSpec as P

HIDDEN = -1e30
LANES = 128
VMEM_LIMIT = 32 * 1024 * 1024


def dot_nt(a, b):
    return lax.dot_general(a, b, (((1,), (1,)), ((), ())), preferred_element_type=jnp.float32)


def dot(a, b):
    return jnp.dot(a, b, preferred_element_type=jnp.float32)


def chunk_sizes(tok_group):
    if tok_group == 256:
        return (32, 64, 64, 96)
    return (tok_group,)


def attend_kernel(
    first,
    prefill_len,
    exp_scale,
    with_decode,
    table,
    offset,
    q_nope,
    q_rope,
    wk,
    wv,
    cache_latent,
    cache_rope,
    new_latent,
    new_rope,
    *rest,
):
    if with_decode:
        (recv_latent, recv_rope, decode_table, decode_length, out,
         keys, q, att, dkeys, sems, dsems) = rest
    else:
        out, keys, q, att, sems = rest
    heads, t, nope_dim = q_nope.shape
    block_len, latent = cache_latent.shape[1:]
    rope_dim = q_rope.shape[1] // heads
    blocks = table.shape[1]
    prior = blocks * block_len
    fresh = keys.shape[0] - prior

    copies = []
    for i in range(blocks):
        b = table[0, i]
        rows = pl.ds(i * block_len, block_len)
        copies.append(pltpu.make_async_copy(
            cache_latent.at[b], keys.at[rows, pl.ds(0, latent)], sems.at[2 * i]))
        copies.append(pltpu.make_async_copy(
            cache_rope.at[b], keys.at[rows, pl.ds(latent, LANES)], sems.at[2 * i + 1]))
    copies.append(pltpu.make_async_copy(
        new_latent.at[pl.ds(0, fresh)], keys.at[pl.ds(prior, fresh), pl.ds(0, latent)],
        sems.at[2 * blocks]))
    copies.append(pltpu.make_async_copy(
        new_rope.at[pl.ds(0, fresh)], keys.at[pl.ds(prior, fresh), pl.ds(latent, LANES)],
        sems.at[2 * blocks + 1]))
    for c in copies:
        c.start()
    dec_copies = []
    if with_decode:
        pool = cache_latent.shape[0]
        for i in range(pool):
            rows = pl.ds(i * block_len, block_len)
            dec_copies.append(pltpu.make_async_copy(
                cache_latent.at[i], dkeys.at[rows, pl.ds(0, latent)], dsems.at[2 * i]))
            dec_copies.append(pltpu.make_async_copy(
                cache_rope.at[i], dkeys.at[rows, pl.ds(latent, LANES)], dsems.at[2 * i + 1]))
        received = recv_latent.shape[0]
        tail = dkeys.shape[0] - pool * block_len - received
        start = new_latent.shape[0] - tail
        n = 2 * pool
        for src_l, src_r, at, size in (
            (recv_latent, recv_rope, pool * block_len, received),
            (new_latent.at[pl.ds(start, tail)], new_rope.at[pl.ds(start, tail)],
             pool * block_len + received, tail),
        ):
            dec_copies.append(pltpu.make_async_copy(
                src_l, dkeys.at[pl.ds(at, size), pl.ds(0, latent)], dsems.at[n]))
            dec_copies.append(pltpu.make_async_copy(
                src_r, dkeys.at[pl.ds(at, size), pl.ds(latent, LANES)], dsems.at[n + 1]))
            n += 2
        for c in dec_copies:
            c.start()

    lane = lax.broadcasted_iota(jnp.int32, (t, LANES), 1)
    one = jnp.where(lane == rope_dim, 1.0, 0.0)
    per_tile = LANES // rope_dim
    for h in range(heads):
        pair = q_rope[:, h // per_tile * LANES:(h // per_tile + 1) * LANES].astype(jnp.float32)
        turn = h % per_tile * rope_dim
        if turn:
            pair = pltpu.roll(pair, LANES - turn, 1)
        q[h * t:(h + 1) * t, latent:] = jnp.where(lane < rope_dim, pair, one).astype(jnp.bfloat16)
    for h in range(heads):
        q[h * t:(h + 1) * t, :latent] = dot(q_nope[h], wk[h]).astype(jnp.bfloat16)

    for c in copies:
        c.wait()
    lane_k = lax.broadcasted_iota(jnp.int32, (prior, LANES), 1)
    pos_k = lax.broadcasted_iota(jnp.int32, (prior, LANES), 0)
    hide = jnp.where((lane_k == rope_dim) & (pos_k >= offset[0]), HIDDEN, 0.0)
    keys[:prior, latent:] = (keys[:prior, latent:].astype(jnp.float32) + hide).astype(jnp.bfloat16)

    together = 1
    while together * 2 <= heads and together * 2 * t <= 384:
        together *= 2
    tile = together * t
    token = first + lax.broadcasted_iota(jnp.int32, (t, fresh), 0)
    key_token = lax.broadcasted_iota(jnp.int32, (t, fresh), 1)
    causal = (key_token <= token)[None]

    def scores_of(i):
        rows = q[i * tile:(i + 1) * tile, :]
        return dot_nt(rows, keys[:prior, :]), dot_nt(rows, keys[prior:, :])

    steps = heads // together
    ahead = scores_of(0)
    for i in range(steps):
        s_old, s_new = ahead
        if i + 1 < steps:
            ahead = scores_of(i + 1)
        s_new = jnp.where(causal, s_new.reshape(together, t, fresh), HIDDEN).reshape(tile, fresh)
        top = jnp.maximum(jnp.max(s_old, axis=1, keepdims=True), jnp.max(s_new, axis=1, keepdims=True))
        p_old = jnp.exp2((s_old - top) * exp_scale)
        p_new = jnp.exp2((s_new - top) * exp_scale)
        total = jnp.sum(p_old, axis=1, keepdims=True) + jnp.sum(p_new, axis=1, keepdims=True)
        mixed = dot(p_old.astype(jnp.bfloat16), keys[:prior, :latent]) + dot(
            p_new.astype(jnp.bfloat16), keys[prior:, :latent])
        att[i * tile:(i + 1) * tile, :] = (mixed / total).astype(jnp.bfloat16)

    if with_decode:
        decodes = decode_table.shape[0]
        for c in dec_copies:
            c.wait()
        span = dkeys.shape[0]
        ext = span - tail
        key = lax.broadcasted_iota(jnp.int32, (decodes, span), 1)
        request = lax.broadcasted_iota(jnp.int32, (decodes, span), 0)
        block = key // block_len
        pos = key % block_len
        count = jnp.where(key - ext + start == request + prefill_len, 1.0, 0.0)
        for m in range(decode_table.shape[1]):
            hit = (block == decode_table[:, m:m + 1]) & (
                pos + m * block_len < decode_length[:, 0:1]) & (key < ext)
            count = count + jnp.where(hit, 1.0, 0.0)
        count = count[None]
        at = prefill_len - first
        half = heads // 2 if heads % 2 == 0 else heads
        for lo in range(0, heads, half):
            rows = jnp.concatenate(
                [q[h * t + at:h * t + at + decodes, :] for h in range(lo, lo + half)], axis=0)
            s = dot_nt(rows, dkeys[...]).reshape(half, decodes, span)
            s = jnp.where(count > 0.0, s, HIDDEN)
            top = jnp.max(s, axis=2, keepdims=True)
            p = count * jnp.exp2((s - top) * exp_scale)
            total = jnp.sum(p, axis=2, keepdims=True).reshape(half * decodes, 1)
            p = p.reshape(half * decodes, span).astype(jnp.bfloat16)
            mixed = (dot(p, dkeys[:, :latent]) / total).astype(jnp.bfloat16)
            for h in range(lo, lo + half):
                att[h * t + at:h * t + at + decodes, :] = mixed[(h - lo) * decodes:(h - lo + 1) * decodes]

    dv = wv.shape[2]
    for h in range(heads):
        out[:, h * dv:(h + 1) * dv] = dot(att[h * t:(h + 1) * t, :], wv[h]).astype(jnp.bfloat16)


def attend(first, size, prefill_len, exp_scale, q_nope, q_rope, wk, wv, cache_latent, cache_rope,
           new_latent, new_rope, table, offset, decode=None):
    heads, _, latent = wk.shape
    tok_group = new_latent.shape[0]
    block_len = cache_latent.shape[1]
    blocks = table.shape[1]
    prior = blocks * block_len
    seen = min(first + size, prefill_len)
    fresh = min(-(-seen // LANES) * LANES, tok_group)
    width = latent + LANES
    dv = wv.shape[2]
    smem = pl.BlockSpec(memory_space=pltpu.SMEM)
    vmem = pl.BlockSpec(memory_space=pltpu.VMEM)
    hbm = pl.BlockSpec(memory_space=pl.ANY)
    args = [table, offset, q_nope, q_rope, wk, wv, cache_latent, cache_rope, new_latent, new_rope]
    in_specs = [smem, smem, vmem, vmem, vmem, vmem] + [hbm] * 4
    scratch = [
        pltpu.VMEM((prior + fresh, width), jnp.bfloat16),
        pltpu.VMEM((heads * size, width), jnp.bfloat16),
        pltpu.VMEM((heads * size, latent), jnp.bfloat16),
    ]
    flops = 2 * heads * size * ((prior + fresh) * (width + latent) + latent * 2 * LANES)
    if decode is not None:
        args += list(decode)
        in_specs += [hbm, hbm, vmem, vmem]
        received = decode[0].shape[0]
        pool = cache_latent.shape[0]
        span = pool * block_len + received + min(LANES, tok_group)
        scratch.append(pltpu.VMEM((span, width), jnp.bfloat16))
        flops += 2 * heads * decode[2].shape[0] * span * (width + latent)
    scratch.append(pltpu.SemaphoreType.DMA((2 * blocks + 2,)))
    if decode is not None:
        scratch.append(pltpu.SemaphoreType.DMA((2 * pool + 4,)))
    return pl.pallas_call(
        functools.partial(attend_kernel, first, prefill_len, exp_scale, decode is not None),
        out_shape=jax.ShapeDtypeStruct((size, heads * dv), jnp.bfloat16),
        in_specs=in_specs,
        out_specs=vmem,
        scratch_shapes=scratch,
        name="attend",
        compiler_params=pltpu.CompilerParams(vmem_limit_bytes=VMEM_LIMIT),
        cost_estimate=pl.CostEstimate(
            flops=2 * flops, bytes_accessed=6_000_000, transcendentals=heads * size * (prior + fresh)),
    )(*args)


def project_kernel(place, w, *rest):
    groups = (len(rest) - 1) // 2
    parts, outs, x = rest[:groups], rest[groups:2 * groups], rest[-1]
    t = parts[0].shape[0]
    for i in range(groups):
        x[pl.ds(pl.multiple_of(place[i] * t, t), t), :] = parts[i][...]
    columns = w.shape[1]
    step = 256 if columns % 256 == 0 else columns
    for at in range(0, columns, step):
        y = dot(x[...], w[:, at:at + step]).astype(jnp.bfloat16)
        for i in range(groups):
            outs[i][:, at:at + step] = y[i * t:(i + 1) * t]


def project(place, parts, w):
    groups = len(parts)
    t, depth = parts[0].shape
    columns = w.shape[1]
    vmem = pl.BlockSpec(memory_space=pltpu.VMEM)
    return pl.pallas_call(
        project_kernel,
        out_shape=[jax.ShapeDtypeStruct((t, columns), jnp.bfloat16)] * groups,
        in_specs=[pl.BlockSpec(memory_space=pltpu.SMEM)] + [vmem] * (groups + 1),
        out_specs=[vmem] * groups,
        scratch_shapes=[pltpu.VMEM((groups * t, depth), jnp.bfloat16)],
        name="project",
        compiler_params=pltpu.CompilerParams(vmem_limit_bytes=VMEM_LIMIT),
        cost_estimate=pl.CostEstimate(
            flops=2 * groups * t * depth * columns, bytes_accessed=4 * groups * t * columns,
            transcendentals=0),
    )(place, w, *parts)


def gather_groups(x):
    groups = lax.axis_size("dp")
    if groups % 2:
        return [x] + [lax.ppermute(x, "dp", [(i, (i + s) % groups) for i in range(groups)])
                      for s in range(1, groups)]
    mine = [x] + [lax.ppermute(x, "dp", [(i, (i + 2 * s) % groups) for i in range(groups)])
                  for s in range(1, groups // 2)]
    swap = [(i, i ^ 1) for i in range(groups)]
    return mine + [lax.ppermute(y, "dp", swap) for y in mine]


def gathered_ids(groups, me):
    if groups % 2:
        return [(me - s) % groups for s in range(groups)]
    return [(who - 2 * s) % groups for who in (me, me ^ 1) for s in range(groups // 2)]


LINE_ORDER = ((0, 3, 2, 1), (1, 3, 2, 0), (2, 0, 1, 3), (3, 0, 1, 2))


def add(*terms):
    return sum(x.astype(jnp.float32) for x in terms).astype(jnp.bfloat16)


def reduce_line(own, far, mid, near):
    inward = [(0, 1), (3, 2)]
    across = [(1, 2), (2, 1)]
    outward = [(1, 0), (2, 3)]
    far_in = lax.ppermute(far, "tp", inward)
    mid_in = lax.ppermute(mid, "tp", inward)
    near_in = lax.ppermute(near, "tp", inward)
    far_on = lax.ppermute(add(far, far_in), "tp", across)
    mid_on = lax.ppermute(add(mid, mid_in), "tp", across)
    last = lax.ppermute(add(near, far_on), "tp", outward)
    return add(own, near_in, mid_on, last)


def body(
    query_nope,
    query_rope,
    new_latent,
    new_rope,
    cache_latent,
    cache_rope,
    absorb_key,
    absorb_value,
    output_weight,
    send_blocks,
    prefill_table,
    prefill_offset,
    decode_table,
    decode_length,
):
    tok_group, heads, nope_dim = query_nope.shape
    pool_blocks, block_len, latent_dim = cache_latent.shape
    rope_dim = new_rope.shape[1]
    capacity = send_blocks.shape[2]
    group_count = lax.axis_size("dp")
    prefill_len = tok_group - decode_length.shape[0]
    exp_scale = float((nope_dim + rope_dim) ** (-0.5) * 1.4426950408889634)

    padded_rope = jnp.pad(
        cache_rope.reshape(pool_blocks, block_len, rope_dim), ((0, 0), (0, 0), (0, LANES - rope_dim)))
    padded_new = jnp.pad(new_rope, ((0, 0), (0, LANES - rope_dim)))

    outgoing = send_blocks[0]
    send = jnp.concatenate([cache_latent[outgoing], padded_rope[outgoing]], axis=3)
    me = lax.axis_index("dp")
    parts = [lax.dynamic_index_in_dim(send, me, 0, keepdims=False)]
    for shift in range(1, group_count):
        there = lax.rem(me + shift, group_count)
        parts.append(lax.ppermute(
            lax.dynamic_index_in_dim(send, there, 0, keepdims=False), "dp",
            [(i, (i + shift) % group_count) for i in range(group_count)]))
    received = jnp.stack(parts[::-1], axis=0)
    received = jnp.roll(received, me + 1, axis=0)
    received = received.reshape(group_count * capacity * block_len, latent_dim + LANES)

    on_line = lax.axis_size("tp") == 4 and group_count == 4
    ids = np.array([gathered_ids(group_count, g) for g in range(group_count)], np.int32)
    if on_line:
        places = np.argsort(np.array(LINE_ORDER), axis=1)[None, :, :]
        places = np.take_along_axis(
            np.broadcast_to(places, (4, 4, 4)), np.broadcast_to(ids[:, None, :], (4, 4, 4)), axis=2)
        place = jnp.asarray(places.astype(np.int32))[me, lax.axis_index("tp")]
    else:
        place = jnp.asarray(ids)[me]

    first = 0
    outs = []
    sizes = chunk_sizes(tok_group)
    for n, size in enumerate(sizes):
        decode = None
        if n == len(sizes) - 1:
            decode = (received[:, :latent_dim], received[:, latent_dim:], decode_table,
                      decode_length[:, None])
        head_out = attend(
            first, size, prefill_len, exp_scale,
            query_nope[first:first + size].transpose(1, 0, 2), query_rope[first:first + size],
            absorb_key, absorb_value, cache_latent, padded_rope, new_latent, padded_new,
            prefill_table, prefill_offset, decode)
        partials = project(place, gather_groups(head_out), output_weight)
        if on_line:
            outs.append(reduce_line(*partials))
        else:
            outs.append(lax.psum_scatter(jnp.stack(partials), "tp", scatter_dimension=0, tiled=False))
        first += size
    return jnp.concatenate(outs, axis=0)


def solution(mesh):
    return jax.shard_map(
        body,
        mesh=mesh,
        in_specs=(
            P(("replica", "dp"), "tp", None),
            P(("replica", "dp"), "tp"),
            P(("replica", "dp"), None),
            P(("replica", "dp"), None),
            P(("replica", "dp"), None, None),
            P(("replica", "dp"), None),
            P("tp", None, None),
            P("tp", None, None),
            P("tp", "dp"),
            P(("replica", "dp"), None, None),
            P(("replica", "dp"), None),
            P(("replica", "dp")),
            P(("replica", "dp"), None),
            P(("replica", "dp")),
        ),
        out_specs=P(("replica", "tp"), "dp"),
        check_vma=False,
    )
```

```python
import functools

import jax
import jax.numpy as jnp
import numpy as np
from jax import lax
from jax.experimental import pallas as pl
from jax.experimental.pallas import tpu as pltpu
from jax.sharding import PartitionSpec as P

HIDDEN = -1e30
LANES = 128
MIB = 1024 * 1024

SMEM = pl.BlockSpec(memory_space=pltpu.SMEM)
VMEM = pl.BlockSpec(memory_space=pltpu.VMEM)
HBM = pl.BlockSpec(memory_space=pltpu.HBM)
ANY = pl.BlockSpec(memory_space=pl.ANY)


def params(mib):
    return pltpu.CompilerParams(vmem_limit_bytes=mib * MIB)


def dot_nt(a, b):
    return lax.dot_general(a, b, (((1,), (1,)), ((), ())), preferred_element_type=jnp.float32)


def dot(a, b):
    return jnp.dot(a, b, preferred_element_type=jnp.float32)


def chunk_sizes(tok_group):
    if tok_group == 256:
        return (48, 64, 64, 80)
    return (tok_group,)


def rope_rows(rope_t):
    rows = jnp.transpose(rope_t.astype(jnp.float32), (1, 0))
    return jnp.concatenate(
        [rows, jnp.zeros((rows.shape[0], LANES - rows.shape[1]), jnp.float32)], axis=1
    ).astype(jnp.bfloat16)


def build_queries(q, q_nope, q_rope, wk, ready=None):
    heads, t, _ = q_nope.shape
    latent = wk.shape[2]
    rope_dim = q_rope.shape[1] // heads
    lane = lax.broadcasted_iota(jnp.int32, (t, LANES), 1)
    one = jnp.where(lane == rope_dim, 1.0, 0.0)
    per_tile = LANES // rope_dim
    for h in range(heads):
        pair = q_rope[:, h // per_tile * LANES:(h // per_tile + 1) * LANES].astype(jnp.float32)
        turn = h % per_tile * rope_dim
        if turn:
            pair = pltpu.roll(pair, LANES - turn, 1)
        q[h * t:(h + 1) * t, latent:] = jnp.where(lane < rope_dim, pair, one).astype(jnp.bfloat16)
    for h in range(heads):
        if ready is not None:
            ready(h)
        q[h * t:(h + 1) * t, :latent] = dot(q_nope[h], wk[h]).astype(jnp.bfloat16)


def prefill(q, keys, att, heads, t, first, prior, fresh, exp_scale):
    latent = att.shape[1]
    together = 1
    while together * 2 <= heads and together * 2 * t <= 384:
        together *= 2
    tile = together * t
    token = first + lax.broadcasted_iota(jnp.int32, (t, fresh), 0)
    key_token = lax.broadcasted_iota(jnp.int32, (t, fresh), 1)
    causal = (key_token <= token)[None]
    end = prior + fresh

    def scores_of(i):
        rows = q[i * tile:(i + 1) * tile, :]
        return dot_nt(rows, keys[:prior, :]), dot_nt(rows, keys[prior:end, :])

    steps = heads // together
    ahead = scores_of(0)
    for i in range(steps):
        s_old, s_new = ahead
        if i + 1 < steps:
            ahead = scores_of(i + 1)
        s_new = jnp.where(causal, s_new.reshape(together, t, fresh), HIDDEN).reshape(tile, fresh)
        top = jnp.maximum(jnp.max(s_old, axis=1, keepdims=True), jnp.max(s_new, axis=1, keepdims=True))
        p_old = jnp.exp2((s_old - top) * exp_scale)
        p_new = jnp.exp2((s_new - top) * exp_scale)
        total = jnp.sum(p_old, axis=1, keepdims=True) + jnp.sum(p_new, axis=1, keepdims=True)
        mixed = dot(p_old.astype(jnp.bfloat16), keys[:prior, :latent]) + dot(
            p_new.astype(jnp.bfloat16), keys[prior:end, :latent])
        att[i * tile:(i + 1) * tile, :] = (mixed / total).astype(jnp.bfloat16)


def head_outputs(out, att, wv, t):
    heads, _, dv = wv.shape
    for h in range(heads):
        out[:, h * dv:(h + 1) * dv] = dot(att[h * t:(h + 1) * t, :], wv[h]).astype(jnp.bfloat16)


def first_kernel(fresh, exp_scale, table, offset, q_nope, q_rope_hbm, wk_hbm, wv_hbm, cache_latent,
                 cache_rope, new_latent, new_rope_t, out, keys, wk, wv, q_rope, q, att, sems, wsems):
    heads, t, _ = q_nope.shape
    block_len, latent = cache_latent.shape[1:]
    rope_dim = new_rope_t.shape[0]
    blocks = table.shape[1]
    prior = blocks * block_len
    tok_group = new_latent.shape[0]

    rope_copy = pltpu.make_async_copy(q_rope_hbm.at[pl.ds(0, t)], q_rope, wsems.at[0])
    rope_copy.start()
    wk_copies = [pltpu.make_async_copy(wk_hbm.at[h], wk.at[h], wsems.at[1 + h]) for h in range(heads)]
    for c in wk_copies:
        c.start()
    copies = []
    for i in range(blocks):
        b = table[0, i]
        rows = pl.ds(i * block_len, block_len)
        copies.append(pltpu.make_async_copy(
            cache_latent.at[b], keys.at[rows, pl.ds(0, latent)], sems.at[2 * i]))
        copies.append(pltpu.make_async_copy(
            cache_rope.at[b], keys.at[rows, pl.ds(latent, LANES)], sems.at[2 * i + 1]))
    copies.append(pltpu.make_async_copy(
        new_latent, keys.at[pl.ds(prior, tok_group), pl.ds(0, latent)], sems.at[2 * blocks]))
    for c in copies:
        c.start()
    wv_copy = pltpu.make_async_copy(wv_hbm, wv, sems.at[2 * blocks + 1])
    wv_copy.start()

    keys[prior:, latent:] = rope_rows(new_rope_t[...])
    rope_copy.wait()
    build_queries(q, q_nope, q_rope, wk, lambda h: wk_copies[h].wait())

    for c in copies:
        c.wait()
    lane = lax.broadcasted_iota(jnp.int32, (prior, LANES), 1)
    pos = lax.broadcasted_iota(jnp.int32, (prior, LANES), 0)
    hide = jnp.where((lane == rope_dim) & (pos >= offset[0]), HIDDEN, 0.0)
    keys[:prior, latent:] = (keys[:prior, latent:].astype(jnp.float32) + hide).astype(jnp.bfloat16)
    prefill(q, keys, att, heads, t, 0, prior, fresh, exp_scale)
    wv_copy.wait()
    head_outputs(out, att, wv, t)


def later_kernel(first, fresh, prior, exp_scale, n_after, q_nope, q_rope, wk, wv, keys, *rest):
    out, q, att = rest[n_after:]
    heads, t, _ = q_nope.shape
    build_queries(q, q_nope, q_rope, wk)
    prefill(q, keys, att, heads, t, first, prior, fresh, exp_scale)
    head_outputs(out, att, wv, t)


def last_kernel(first, fresh, prior, prefill_len, exp_scale, n_after, q_nope, q_rope, wk, wv, keys,
                cache_latent, cache_rope, received, decode_table, decode_length, *rest):
    out, q, att, dkeys, sems = rest[n_after:]
    heads, t, _ = q_nope.shape
    pool, block_len, latent = cache_latent.shape
    got = received.shape[0]
    ext = pool * block_len + got
    tail = dkeys.shape[0] - ext
    start = keys.shape[0] - tail
    copies = []
    for i in range(pool):
        rows = pl.ds(i * block_len, block_len)
        copies.append(pltpu.make_async_copy(
            cache_latent.at[i], dkeys.at[rows, pl.ds(0, latent)], sems.at[2 * i]))
        copies.append(pltpu.make_async_copy(
            cache_rope.at[i], dkeys.at[rows, pl.ds(latent, LANES)], sems.at[2 * i + 1]))
    copies.append(pltpu.make_async_copy(
        received, dkeys.at[pl.ds(pool * block_len, got)], sems.at[2 * pool]))
    for c in copies:
        c.start()
    dkeys[ext:, :] = keys[start:, :]

    build_queries(q, q_nope, q_rope, wk)
    prefill(q, keys, att, heads, t, first, prior, fresh, exp_scale)

    decodes = decode_table.shape[0]
    for c in copies:
        c.wait()
    span = dkeys.shape[0]
    key = lax.broadcasted_iota(jnp.int32, (decodes, span), 1)
    request = lax.broadcasted_iota(jnp.int32, (decodes, span), 0)
    block = key // block_len
    pos = key % block_len
    own_key = key - ext + (start - prior) == request + prefill_len
    count = jnp.where(own_key, 1.0, 0.0)
    for m in range(decode_table.shape[1]):
        hit = (block == decode_table[:, m:m + 1]) & (
            pos + m * block_len < decode_length[:, 0:1]) & (key < ext)
        count = count + jnp.where(hit, 1.0, 0.0)
    count = count[None]
    at = prefill_len - first
    half = heads // 2 if heads % 2 == 0 else heads
    for lo in range(0, heads, half):
        rows = jnp.concatenate(
            [q[h * t + at:h * t + at + decodes, :] for h in range(lo, lo + half)], axis=0)
        s = dot_nt(rows, dkeys[...]).reshape(half, decodes, span)
        s = jnp.where(count > 0.0, s, HIDDEN)
        top = jnp.max(s, axis=2, keepdims=True)
        p = count * jnp.exp2((s - top) * exp_scale)
        total = jnp.sum(p, axis=2, keepdims=True).reshape(half * decodes, 1)
        p = p.reshape(half * decodes, span).astype(jnp.bfloat16)
        mixed = (dot(p, dkeys[:, :latent]) / total).astype(jnp.bfloat16)
        for h in range(lo, lo + half):
            att[h * t + at:h * t + at + decodes, :] = mixed[(h - lo) * decodes:(h - lo + 1) * decodes]
    head_outputs(out, att, wv, t)


COST = pl.CostEstimate(flops=1000, bytes_accessed=1000, transcendentals=0)
LONG = pl.CostEstimate(flops=40_000_000_000, bytes_accessed=1000, transcendentals=0)


def in_hbm(x):
    return pltpu.with_memory_space_constraint(x, pltpu.HBM)


def pack_kernel(ids, cache_latent, cache_rope, out, sems):
    latent = cache_latent.shape[2]
    _, groups, capacity = ids.shape
    copies = []
    for g in range(groups):
        for k in range(capacity):
            n = g * capacity + k
            b = ids[0, g, k]
            copies.append(pltpu.make_async_copy(
                cache_latent.at[b], out.at[n, :, pl.ds(0, latent)], sems.at[2 * n]))
            copies.append(pltpu.make_async_copy(
                cache_rope.at[b], out.at[n, :, pl.ds(latent, LANES)], sems.at[2 * n + 1]))
    for c in copies:
        c.start()
    for c in copies:
        c.wait()


def project_kernel(n_after, place, w, *rest):
    parts, (own, others, x) = rest[:-3 - n_after], rest[-3:]
    t = own.shape[0]
    i = 0
    for part in parts:
        for at in range(0, part.shape[0], t):
            x[pl.ds(pl.multiple_of(place[i] * t, t), t), :] = part[at:at + t, :]
            i += 1
    columns = w.shape[1]
    step = 256 if columns % 256 == 0 else columns
    for at in range(0, columns, step):
        y = dot(x[...], w[:, at:at + step]).astype(jnp.bfloat16)
        own[:, at:at + step] = y[:t]
        others[:, at:at + step] = y[t:]


def project(place, parts, w, t, after=()):
    depth, columns = w.shape
    rows = sum(p.shape[0] for p in parts)
    return pl.pallas_call(
        functools.partial(project_kernel, len(after)),
        out_shape=[jax.ShapeDtypeStruct((t, columns), jnp.bfloat16),
                   jax.ShapeDtypeStruct((rows - t, columns), jnp.bfloat16)],
        in_specs=[SMEM, VMEM] + [VMEM] * len(parts) + [ANY] * len(after),
        out_specs=[VMEM, VMEM],
        scratch_shapes=[pltpu.VMEM((rows, depth), jnp.bfloat16)],
        name="project",
        compiler_params=params(12),
        cost_estimate=COST,
    )(place, w, *parts, *after)


def add_kernel(spans, n_after, *refs):
    out = refs[-1]
    n = out.shape[0]
    total = None
    for ref, at in zip(refs, spans):
        x = ref[at:at + n, :].astype(jnp.float32)
        total = x if total is None else total + x
    out[...] = total.astype(jnp.bfloat16)


def add(rows, terms, after=()):
    return pl.pallas_call(
        functools.partial(add_kernel, [at for _, at in terms], len(after)),
        out_shape=jax.ShapeDtypeStruct((rows, terms[0][0].shape[1]), jnp.bfloat16),
        in_specs=[VMEM] * len(terms) + [ANY] * len(after),
        out_specs=VMEM,
        name="add",
        compiler_params=params(8),
        cost_estimate=COST,
    )(*[x for x, _ in terms], *after)


def gathered_ids(groups, me):
    if groups % 2:
        return [(me - s) % groups for s in range(groups)]
    return [(who - 2 * s) % groups for who in (me, me ^ 1) for s in range(groups // 2)]


def shift_groups(x):
    groups = lax.axis_size("dp")
    step = 1 if groups % 2 else 2
    return [x] + [lax.ppermute(x, "dp", [(i, (i + s) % groups) for i in range(groups)])
                  for s in range(step, groups, step)]


def stack_kernel(count, *refs):
    out, at = refs[-1], 0
    for ref in refs[:count]:
        out[at:at + ref.shape[0], :] = ref[...]
        at += ref.shape[0]


def stack(parts, after=()):
    rows = sum(p.shape[0] for p in parts)
    return pl.pallas_call(
        functools.partial(stack_kernel, len(parts)),
        out_shape=jax.ShapeDtypeStruct((rows, parts[0].shape[1]), parts[0].dtype),
        in_specs=[VMEM] * len(parts) + [ANY] * len(after),
        out_specs=VMEM,
        name="stack",
        compiler_params=params(4),
        cost_estimate=COST,
    )(*parts, *after)


def swap_cores(x):
    return lax.ppermute(x, "dp", [(i, i ^ 1) for i in range(lax.axis_size("dp"))])


LINE_ORDER = ((0, 3, 2, 1), (1, 3, 2, 0), (2, 0, 1, 3), (3, 0, 1, 2))
INWARD = [(0, 1), (3, 2)]
ACROSS = [(1, 2), (2, 1)]
OUTWARD = [(1, 0), (2, 3)]


def body(
    query_nope,
    query_rope,
    new_latent,
    new_rope,
    cache_latent,
    cache_rope,
    absorb_key,
    absorb_value,
    output_weight,
    send_blocks,
    prefill_table,
    prefill_offset,
    decode_table,
    decode_length,
):
    tok_group, heads, nope_dim = query_nope.shape
    pool, block_len, latent = cache_latent.shape
    rope_dim = new_rope.shape[1]
    capacity = send_blocks.shape[2]
    groups = lax.axis_size("dp")
    decodes = decode_length.shape[0]
    prefill_len = tok_group - decodes
    dv = absorb_value.shape[2]
    columns = output_weight.shape[1]
    exp_scale = float((nope_dim + rope_dim) ** (-0.5) * 1.4426950408889634)
    blocks = prefill_table.shape[1]
    prior = blocks * block_len
    width = latent + LANES
    on_line = lax.axis_size("tp") == 4 and groups == 4
    bf16 = jnp.bfloat16

    me = lax.axis_index("dp")
    ids = np.array([gathered_ids(groups, g) for g in range(groups)], np.int32)
    if on_line:
        places = np.argsort(np.array(LINE_ORDER), axis=1)[None, :, :]
        places = np.take_along_axis(
            np.broadcast_to(places, (4, 4, 4)), np.broadcast_to(ids[:, None, :], (4, 4, 4)), axis=2)
        place = jnp.asarray(places.astype(np.int32))[me, lax.axis_index("tp")]
    else:
        place = jnp.asarray(ids)[me]

    padded_rope = jnp.pad(
        cache_rope.reshape(pool, block_len, rope_dim), ((0, 0), (0, 0), (0, LANES - rope_dim)))
    sizes = chunk_sizes(tok_group)
    starts = [sum(sizes[:i]) for i in range(len(sizes))]

    def fresh_of(n):
        seen = min(starts[n] + sizes[n], prefill_len)
        return min(-(-seen // LANES) * LANES, tok_group)

    def scratch(t):
        return [pltpu.VMEM((heads * t, width), bf16), pltpu.VMEM((heads * t, latent), bf16)]

    def nope_of(n):
        return query_nope[starts[n]:starts[n] + sizes[n]].transpose(1, 0, 2)

    def first_chunk():
        t = sizes[0]
        return pl.pallas_call(
            functools.partial(first_kernel, fresh_of(0), exp_scale),
            out_shape=[jax.ShapeDtypeStruct((t, heads * dv), bf16),
                       jax.ShapeDtypeStruct((prior + tok_group, width), bf16)],
            in_specs=[SMEM, SMEM, VMEM, HBM, HBM, HBM, HBM, ANY, HBM, VMEM],
            out_specs=[VMEM, VMEM],
            scratch_shapes=[
                pltpu.VMEM(absorb_key.shape, bf16),
                pltpu.VMEM(absorb_value.shape, bf16),
                pltpu.VMEM((t, query_rope.shape[1]), bf16),
                *scratch(t),
                pltpu.SemaphoreType.DMA((2 * blocks + 2,)),
                pltpu.SemaphoreType.DMA((heads + 1,)),
            ],
            name="attend_first",
            compiler_params=params(20),
            cost_estimate=LONG,
        )(prefill_table, prefill_offset, nope_of(0), in_hbm(query_rope), in_hbm(absorb_key),
          in_hbm(absorb_value), in_hbm(cache_latent), padded_rope, in_hbm(new_latent), new_rope.T)

    def later_chunk(n, keys, after, decode=None):
        t = sizes[n]
        args = [nope_of(n), query_rope[starts[n]:starts[n] + t], absorb_key, absorb_value, keys]
        specs = [VMEM] * 5
        scratches = scratch(t)
        if decode is None:
            kernel = functools.partial(
                later_kernel, starts[n], fresh_of(n), prior, exp_scale, len(after))
            limit = 20
        else:
            kernel = functools.partial(
                last_kernel, starts[n], fresh_of(n), prior, prefill_len, exp_scale, len(after))
            args += [in_hbm(cache_latent), padded_rope, *decode]
            specs += [HBM, ANY, ANY, VMEM, VMEM]
            span = pool * block_len + decode[0].shape[0] + min(LANES, tok_group)
            scratches += [pltpu.VMEM((span, width), bf16), pltpu.SemaphoreType.DMA((2 * pool + 1,))]
            limit = 26
        return pl.pallas_call(
            kernel,
            out_shape=jax.ShapeDtypeStruct((t, heads * dv), bf16),
            in_specs=specs + [ANY] * len(after),
            out_specs=VMEM,
            scratch_shapes=scratches,
            name="attend",
            compiler_params=params(limit),
            cost_estimate=LONG,
        )(*args, *after)

    def pack():
        return pl.pallas_call(
            pack_kernel,
            out_shape=jax.ShapeDtypeStruct((groups * capacity, block_len, width), bf16),
            in_specs=[SMEM, HBM, ANY],
            out_specs=VMEM,
            scratch_shapes=[pltpu.SemaphoreType.DMA((2 * groups * capacity,))],
            name="pack",
            compiler_params=params(8),
            cost_estimate=COST,
        )(send_blocks, in_hbm(cache_latent), padded_rope)

    def migrate(packed):
        got = lax.all_to_all(packed, "dp", split_axis=0, concat_axis=0, tiled=True)
        return (got.reshape(groups * capacity * block_len, width), decode_table,
                decode_length[:, None])

    if len(sizes) != 4 or not on_line:
        outs = []
        keys = None
        for n, t in enumerate(sizes):
            if n == 0:
                x, keys = first_chunk()
            else:
                x = later_chunk(n, keys, (), migrate(pack()) if n == len(sizes) - 1 else None)
            mine = shift_groups(x)
            if groups % 2 == 0:
                mine += [swap_cores(y) for y in mine]
            own, others = project(place, mine, output_weight, t)
            partials = jnp.concatenate([own, others], axis=0).reshape(groups, t, columns)
            outs.append(lax.psum_scatter(partials, "tp", scatter_dimension=0, tiled=False))
        return jnp.concatenate(outs, axis=0)

    def inward(x):
        return lax.ppermute(x, "tp", INWARD)

    def across(x):
        return lax.ppermute(x, "tp", ACROSS)

    def outward(x):
        return lax.ppermute(x, "tp", OUTWARD)

    def gather(x, after):
        came = shift_groups(x)[1]
        return [x, came, swap_cores(x), swap_cores(stack([came], after))]

    t0, t1, t2, t3 = sizes
    x0, keys = first_chunk()
    decode = migrate(pack())
    x1 = later_chunk(1, keys, (decode[0],))
    own0, rest0 = project(place, gather(x0, (x1,)), output_weight, t0, (x1,))
    in0 = inward(rest0)
    x2 = later_chunk(2, keys, (own0,))
    own1, rest1 = project(place, gather(x1, (x2,)), output_weight, t1, (x2,))
    in1 = inward(rest1)
    to_across0 = add(2 * t0, [(rest0, 0), (in0, 0)], (own1,))
    on0 = across(to_across0)
    x3 = later_chunk(3, keys, (to_across0,), decode)
    own2, rest2 = project(place, gather(x2, (x3,)), output_weight, t2, (x3,))
    in2 = inward(rest2)
    to_across1 = add(2 * t1, [(rest1, 0), (in1, 0)], (own2,))
    on1 = across(to_across1)
    to_out0 = add(t0, [(rest0, 2 * t0), (on0, 0)], (own2,))
    out0 = outward(to_out0)
    own3, rest3 = project(place, gather(x3, (own2,)), output_weight, t3, (to_across1, to_out0))
    far3, mid3, near3 = (rest3[i * t3:(i + 1) * t3] for i in range(3))
    in3 = [inward(far3), inward(mid3), inward(near3)]
    to_across2 = add(2 * t2, [(rest2, 0), (in2, 0)], (own3,))
    on2 = across(to_across2)
    to_out1 = add(t1, [(rest1, 2 * t1), (on1, 0)], (to_across2,))
    out1 = outward(to_out1)
    to_far = add(t3, [(far3, 0), (in3[0], 0)], (to_out1,))
    far_on = across(to_far)
    to_out2 = add(t2, [(rest2, 2 * t2), (on2, 0)], (to_far,))
    out2 = outward(to_out2)
    to_mid = add(t3, [(mid3, 0), (in3[1], 0)], (to_out2,))
    mid_on = across(to_mid)
    out3 = outward(add(t3, [(near3, 0), (far_on, 0)], (to_mid,)))
    done = [
        add(t, [(own, 0), (came, 2 * t), (on, t), (out, 0)])
        for t, own, came, on, out in (
            (t0, own0, in0, on0, out0), (t1, own1, in1, on1, out1), (t2, own2, in2, on2, out2))
    ]
    done.append(add(t3, [(own3, 0), (in3[2], 0), (mid_on, 0), (out3, 0)]))
    return jnp.concatenate(done, axis=0)


def solution(mesh):
    return jax.shard_map(
        body,
        mesh=mesh,
        in_specs=(
            P(("replica", "dp"), "tp", None),
            P(("replica", "dp"), "tp"),
            P(("replica", "dp"), None),
            P(("replica", "dp"), None),
            P(("replica", "dp"), None, None),
            P(("replica", "dp"), None),
            P("tp", None, None),
            P("tp", None, None),
            P("tp", "dp"),
            P(("replica", "dp"), None, None),
            P(("replica", "dp"), None),
            P(("replica", "dp")),
            P(("replica", "dp"), None),
            P(("replica", "dp")),
        ),
        out_specs=P(("replica", "tp"), "dp"),
        check_vma=False,
    )
```

```python
import functools

import jax
import jax.numpy as jnp
import numpy as np
from jax import lax
from jax.experimental import pallas as pl
from jax.experimental.pallas import tpu as pltpu
from jax.sharding import PartitionSpec as P

HIDDEN = -1e30
LANES = 128
MIB = 1024 * 1024

SMEM = pl.BlockSpec(memory_space=pltpu.SMEM)
VMEM = pl.BlockSpec(memory_space=pltpu.VMEM)
HBM = pl.BlockSpec(memory_space=pltpu.HBM)
ANY = pl.BlockSpec(memory_space=pl.ANY)


def params(mib):
    return pltpu.CompilerParams(vmem_limit_bytes=mib * MIB)


def dot_nt(a, b):
    return lax.dot_general(a, b, (((1,), (1,)), ((), ())), preferred_element_type=jnp.float32)


def dot(a, b):
    return jnp.dot(a, b, preferred_element_type=jnp.float32)


def chunk_sizes(tok_group):
    if tok_group == 256:
        return (48, 64, 80, 64)
    return (tok_group,)


def rope_rows(rope_t):
    rows = jnp.transpose(rope_t.astype(jnp.float32), (1, 0))
    return jnp.concatenate(
        [rows, jnp.zeros((rows.shape[0], LANES - rows.shape[1]), jnp.float32)], axis=1
    ).astype(jnp.bfloat16)


def build_queries(q, q_nope, q_rope, first, wk, ready=None):
    heads, t, _ = q_nope.shape
    latent = wk.shape[2]
    rope_dim = q_rope.shape[1] // heads
    lane = lax.broadcasted_iota(jnp.int32, (t, LANES), 1)
    one = jnp.where(lane == rope_dim, 1.0, 0.0)
    per_tile = LANES // rope_dim
    for h in range(heads):
        pair = q_rope[first:first + t, h // per_tile * LANES:(h // per_tile + 1) * LANES].astype(jnp.float32)
        turn = h % per_tile * rope_dim
        if turn:
            pair = pltpu.roll(pair, LANES - turn, 1)
        q[h * t:(h + 1) * t, latent:] = jnp.where(lane < rope_dim, pair, one).astype(jnp.bfloat16)
    for h in range(heads):
        if ready is not None:
            ready(h)
        q[h * t:(h + 1) * t, :latent] = dot(q_nope[h], wk[h]).astype(jnp.bfloat16)


def prefill(q, keys, att, heads, t, first, prior, fresh, exp_scale):
    latent = att.shape[1]
    together = 1
    while together * 2 <= heads and together * 2 * t <= 384:
        together *= 2
    tile = together * t
    token = first + lax.broadcasted_iota(jnp.int32, (t, fresh), 0)
    key_token = lax.broadcasted_iota(jnp.int32, (t, fresh), 1)
    causal = (key_token <= token)[None]
    end = prior + fresh

    def scores_of(i):
        rows = q[i * tile:(i + 1) * tile, :]
        return dot_nt(rows, keys[:prior, :]), dot_nt(rows, keys[prior:end, :])

    steps = heads // together
    ahead = scores_of(0)
    for i in range(steps):
        s_old, s_new = ahead
        if i + 1 < steps:
            ahead = scores_of(i + 1)
        s_new = jnp.where(causal, s_new.reshape(together, t, fresh), HIDDEN).reshape(tile, fresh)
        top = jnp.maximum(jnp.max(s_old, axis=1, keepdims=True), jnp.max(s_new, axis=1, keepdims=True))
        p_old = jnp.exp2((s_old - top) * exp_scale)
        p_new = jnp.exp2((s_new - top) * exp_scale)
        total = jnp.sum(p_old, axis=1, keepdims=True) + jnp.sum(p_new, axis=1, keepdims=True)
        mixed = dot(p_old.astype(jnp.bfloat16), keys[:prior, :latent]) + dot(
            p_new.astype(jnp.bfloat16), keys[prior:end, :latent])
        att[i * tile:(i + 1) * tile, :] = (mixed / total).astype(jnp.bfloat16)


def head_outputs(out, att, wv, t):
    heads, _, dv = wv.shape
    for h in range(heads):
        out[:, h * dv:(h + 1) * dv] = dot(att[h * t:(h + 1) * t, :], wv[h]).astype(jnp.bfloat16)


def first_kernel(fresh, exp_scale, table, offset, q_nope, q_nope_hbm, q_rope_hbm, wk_hbm, wv_hbm,
                 cache_latent, cache_rope, new_latent, new_rope_t, out, keys, wk, wv, q_nope_out,
                 q_rope, q, att, sems, wsems):
    heads, t, _ = q_nope.shape
    block_len, latent = cache_latent.shape[1:]
    rope_dim = new_rope_t.shape[0]
    blocks = table.shape[1]
    prior = blocks * block_len
    tok_group = new_latent.shape[0]

    rope_copy = pltpu.make_async_copy(
        q_rope_hbm.at[pl.ds(0, t)], q_rope.at[pl.ds(0, t)], wsems.at[0])
    rope_copy.start()
    wk_copies = [pltpu.make_async_copy(wk_hbm.at[h], wk.at[h], wsems.at[1 + h]) for h in range(heads)]
    for c in wk_copies:
        c.start()
    copies = []
    for i in range(blocks):
        b = table[0, i]
        rows = pl.ds(i * block_len, block_len)
        copies.append(pltpu.make_async_copy(
            cache_latent.at[b], keys.at[rows, pl.ds(0, latent)], sems.at[2 * i]))
        copies.append(pltpu.make_async_copy(
            cache_rope.at[b], keys.at[rows, pl.ds(latent, LANES)], sems.at[2 * i + 1]))
    copies.append(pltpu.make_async_copy(
        new_latent, keys.at[pl.ds(prior, tok_group), pl.ds(0, latent)], sems.at[2 * blocks]))
    for c in copies:
        c.start()
    wv_copy = pltpu.make_async_copy(wv_hbm, wv, sems.at[2 * blocks + 1])
    wv_copy.start()
    others = [pltpu.make_async_copy(q_nope_hbm, q_nope_out, wsems.at[heads + 1])]
    if t < tok_group:
        others.append(pltpu.make_async_copy(
            q_rope_hbm.at[pl.ds(t, tok_group - t)], q_rope.at[pl.ds(t, tok_group - t)],
            wsems.at[heads + 2]))
    for c in others:
        c.start()

    keys[prior:, latent:] = rope_rows(new_rope_t[...])
    rope_copy.wait()
    build_queries(q, q_nope, q_rope, 0, wk, lambda h: wk_copies[h].wait())

    for c in copies:
        c.wait()
    lane = lax.broadcasted_iota(jnp.int32, (prior, LANES), 1)
    pos = lax.broadcasted_iota(jnp.int32, (prior, LANES), 0)
    hide = jnp.where((lane == rope_dim) & (pos >= offset[0]), HIDDEN, 0.0)
    keys[:prior, latent:] = (keys[:prior, latent:].astype(jnp.float32) + hide).astype(jnp.bfloat16)
    prefill(q, keys, att, heads, t, 0, prior, fresh, exp_scale)
    wv_copy.wait()
    head_outputs(out, att, wv, t)
    for c in others:
        c.wait()


def second_kernel(first, fresh, prior, exp_scale, n_after, me, ids, q_nope, q_rope, wk, wv, keys, w_hbm,
                  cache_latent, cache_rope, *rest):
    rest = rest[n_after:]
    groups = ids.shape[1]
    out, w, packed = rest[0], rest[1], rest[2:2 + groups]
    q, att, sems = rest[2 + groups:]
    heads, t, _ = q_nope.shape
    block_len, latent = cache_latent.shape[1:]
    capacity = ids.shape[2]
    copies = []
    for s in range(groups):
        to = lax.rem(me[0] + s, groups)
        for k in range(capacity):
            b = ids[0, to, k]
            rows = pl.ds(k * block_len, block_len)
            copies.append(pltpu.make_async_copy(
                cache_latent.at[b], packed[s].at[rows, pl.ds(0, latent)], sems.at[len(copies)]))
            copies.append(pltpu.make_async_copy(
                cache_rope.at[b], packed[s].at[rows, pl.ds(latent, LANES)], sems.at[len(copies)]))
    copies.append(pltpu.make_async_copy(w_hbm, w, sems.at[len(copies)]))
    for c in copies:
        c.start()
    build_queries(q, q_nope, q_rope, first, wk)
    prefill(q, keys, att, heads, t, first, prior, fresh, exp_scale)
    head_outputs(out, att, wv, t)
    for c in copies:
        c.wait()


def later_kernel(first, fresh, prior, exp_scale, n_after, q_nope, q_rope, wk, wv, keys, *rest):
    out, q, att = rest[n_after:]
    heads, t, _ = q_nope.shape
    build_queries(q, q_nope, q_rope, first, wk)
    prefill(q, keys, att, heads, t, first, prior, fresh, exp_scale)
    head_outputs(out, att, wv, t)


def last_kernel(first, fresh, prior, prefill_len, exp_scale, n_after, me, q_nope, q_rope, wk, wv, keys,
                cache_latent, cache_rope, decode_table, decode_length, *rest):
    received = rest[:-5 - n_after]
    out, q, att, dkeys, sems = rest[-5:]
    groups = len(received)
    heads, t, _ = q_nope.shape
    pool, block_len, latent = cache_latent.shape
    got = received[0].shape[0]
    ext = pool * block_len + groups * got
    tail = dkeys.shape[0] - ext
    start = keys.shape[0] - tail
    copies = []
    for i in range(pool):
        rows = pl.ds(i * block_len, block_len)
        copies.append(pltpu.make_async_copy(
            cache_latent.at[i], dkeys.at[rows, pl.ds(0, latent)], sems.at[2 * i]))
        copies.append(pltpu.make_async_copy(
            cache_rope.at[i], dkeys.at[rows, pl.ds(latent, LANES)], sems.at[2 * i + 1]))
    for c in copies:
        c.start()
    for s in range(groups):
        source = lax.rem(me[0] + groups - s, groups)
        at = pl.multiple_of(pool * block_len + source * got, block_len)
        dkeys[pl.ds(at, got), :] = received[s][...]
    dkeys[ext:, :] = keys[start:, :]

    build_queries(q, q_nope, q_rope, first, wk)
    prefill(q, keys, att, heads, t, first, prior, fresh, exp_scale)

    decodes = decode_table.shape[0]
    for c in copies:
        c.wait()
    span = dkeys.shape[0]
    key = lax.broadcasted_iota(jnp.int32, (decodes, span), 1)
    request = lax.broadcasted_iota(jnp.int32, (decodes, span), 0)
    block = key // block_len
    pos = key % block_len
    own_key = key - ext + (start - prior) == request + prefill_len
    count = jnp.where(own_key, 1.0, 0.0)
    for m in range(decode_table.shape[1]):
        hit = (block == decode_table[:, m:m + 1]) & (
            pos + m * block_len < decode_length[:, 0:1]) & (key < ext)
        count = count + jnp.where(hit, 1.0, 0.0)
    count = count[None]
    at = prefill_len - first
    half = heads // 2 if heads % 2 == 0 else heads
    for lo in range(0, heads, half):
        rows = jnp.concatenate(
            [q[h * t + at:h * t + at + decodes, :] for h in range(lo, lo + half)], axis=0)
        s = dot_nt(rows, dkeys[...]).reshape(half, decodes, span)
        s = jnp.where(count > 0.0, s, HIDDEN)
        top = jnp.max(s, axis=2, keepdims=True)
        p = count * jnp.exp2((s - top) * exp_scale)
        total = jnp.sum(p, axis=2, keepdims=True).reshape(half * decodes, 1)
        p = p.reshape(half * decodes, span).astype(jnp.bfloat16)
        mixed = (dot(p, dkeys[:, :latent]) / total).astype(jnp.bfloat16)
        for h in range(lo, lo + half):
            att[h * t + at:h * t + at + decodes, :] = mixed[(h - lo) * decodes:(h - lo + 1) * decodes]
    head_outputs(out, att, wv, t)


COST = pl.CostEstimate(flops=1000, bytes_accessed=1000, transcendentals=0)
LONG = pl.CostEstimate(flops=40_000_000_000, bytes_accessed=1000, transcendentals=0)


def in_hbm(x):
    return pltpu.with_memory_space_constraint(x, pltpu.HBM)


def project_kernel(n_parts, tails, place, w, *rest):
    parts, rest, x = rest[:n_parts], rest[n_parts:], rest[-1]
    own, outs = rest[-2 - len(tails)], rest[-1 - len(tails):-1]
    t = own.shape[0]
    lead = outs[-1].shape[0] - tails[-1] * t
    if lead:
        outs[-1][:lead, :] = rest[0][...]
    i = 0
    for part in parts:
        for at in range(0, part.shape[0], t):
            x[pl.ds(pl.multiple_of(place[i] * t, t), t), :] = part[at:at + t, :]
            i += 1
    columns = w.shape[1]
    step = 256 if columns % 256 == 0 else columns
    for at in range(0, columns, step):
        y = dot(x[...], w[:, at:at + step]).astype(jnp.bfloat16)
        own[:, at:at + step] = y[:t]
        row = t
        for i, n in enumerate(tails):
            skip = lead if i == len(tails) - 1 else 0
            outs[i][skip:skip + n * t, at:at + step] = y[row:row + n * t]
            row += n * t


def project(place, parts, w, tails, earlier=(), after=()):
    depth, columns = w.shape
    rows = sum(p.shape[0] for p in parts)
    t = rows // (1 + sum(tails))
    sizes = [t] + [n * t for n in tails]
    sizes[-1] += sum(e.shape[0] for e in earlier)
    return pl.pallas_call(
        functools.partial(project_kernel, len(parts), tails),
        out_shape=[jax.ShapeDtypeStruct((n, columns), jnp.bfloat16) for n in sizes],
        in_specs=[SMEM, VMEM] + [VMEM] * (len(parts) + len(earlier)) + [ANY] * len(after),
        out_specs=[VMEM] * len(sizes),
        scratch_shapes=[pltpu.VMEM((rows, depth), jnp.bfloat16)],
        name="project",
        compiler_params=params(12),
        cost_estimate=COST,
    )(place, w, *parts, *earlier, *after)


def add_kernel(spans, n_after, *refs):
    out = refs[-1]
    n = out.shape[0]
    total = None
    for ref, at in zip(refs, spans):
        x = ref[at:at + n, :].astype(jnp.float32)
        total = x if total is None else total + x
    out[...] = total.astype(jnp.bfloat16)


def add(rows, terms, after=()):
    return pl.pallas_call(
        functools.partial(add_kernel, [at for _, at in terms], len(after)),
        out_shape=jax.ShapeDtypeStruct((rows, terms[0][0].shape[1]), jnp.bfloat16),
        in_specs=[VMEM] * len(terms) + [ANY] * len(after),
        out_specs=VMEM,
        name="add",
        compiler_params=params(8),
        cost_estimate=COST,
    )(*[x for x, _ in terms], *after)


def finish_kernel(n_ready, spans, *refs):
    out = refs[-1]
    row = 0
    for ref in refs[:n_ready]:
        out[row:row + ref.shape[0], :] = ref[...]
        row += ref.shape[0]
    add_kernel(spans, 0, *refs[n_ready:-1], out.at[row:, :])


def finish(ready, terms):
    rows = sum(r.shape[0] for r in ready) + terms[0][0].shape[0]
    return pl.pallas_call(
        functools.partial(finish_kernel, len(ready), [at for _, at in terms]),
        out_shape=jax.ShapeDtypeStruct((rows, terms[0][0].shape[1]), jnp.bfloat16),
        in_specs=[VMEM] * (len(ready) + len(terms)),
        out_specs=VMEM,
        name="finish",
        compiler_params=params(8),
        cost_estimate=COST,
    )(*ready, *[x for x, _ in terms])


def gathered_ids(groups, me):
    if groups % 2:
        return [(me - s) % groups for s in range(groups)]
    return [(who - 2 * s) % groups for who in (me, me ^ 1) for s in range(groups // 2)]


def shift_groups(x):
    groups = lax.axis_size("dp")
    step = 1 if groups % 2 else 2
    return [x] + [lax.ppermute(x, "dp", [(i, (i + s) % groups) for i in range(groups)])
                  for s in range(step, groups, step)]


def stack_kernel(count, *refs):
    out, at = refs[-1], 0
    for ref in refs[:count]:
        out[at:at + ref.shape[0], :] = ref[...]
        at += ref.shape[0]


def stack(parts, after=()):
    rows = sum(p.shape[0] for p in parts)
    return pl.pallas_call(
        functools.partial(stack_kernel, len(parts)),
        out_shape=jax.ShapeDtypeStruct((rows, parts[0].shape[1]), parts[0].dtype),
        in_specs=[VMEM] * len(parts) + [ANY] * len(after),
        out_specs=VMEM,
        name="stack",
        compiler_params=params(4),
        cost_estimate=COST,
    )(*parts, *after)


def swap_cores(x):
    return lax.ppermute(x, "dp", [(i, i ^ 1) for i in range(lax.axis_size("dp"))])


LINE_ORDER = ((0, 3, 2, 1), (1, 3, 2, 0), (2, 0, 1, 3), (3, 0, 1, 2))
INWARD = [(0, 1), (3, 2)]
ACROSS = [(1, 2), (2, 1)]
OUTWARD = [(1, 0), (2, 3)]


def body(
    query_nope,
    query_rope,
    new_latent,
    new_rope,
    cache_latent,
    cache_rope,
    absorb_key,
    absorb_value,
    output_weight,
    send_blocks,
    prefill_table,
    prefill_offset,
    decode_table,
    decode_length,
):
    tok_group, heads, nope_dim = query_nope.shape
    pool, block_len, latent = cache_latent.shape
    rope_dim = new_rope.shape[1]
    capacity = send_blocks.shape[2]
    groups = lax.axis_size("dp")
    decodes = decode_length.shape[0]
    prefill_len = tok_group - decodes
    dv = absorb_value.shape[2]
    columns = output_weight.shape[1]
    exp_scale = float((nope_dim + rope_dim) ** (-0.5) * 1.4426950408889634)
    blocks = prefill_table.shape[1]
    prior = blocks * block_len
    width = latent + LANES
    on_line = lax.axis_size("tp") == 4 and groups == 4
    bf16 = jnp.bfloat16

    me = lax.axis_index("dp")
    ids = np.array([gathered_ids(groups, g) for g in range(groups)], np.int32)
    if on_line:
        places = np.argsort(np.array(LINE_ORDER), axis=1)[None, :, :]
        places = np.take_along_axis(
            np.broadcast_to(places, (4, 4, 4)), np.broadcast_to(ids[:, None, :], (4, 4, 4)), axis=2)
        place = jnp.asarray(places.astype(np.int32))[me, lax.axis_index("tp")]
    else:
        place = jnp.asarray(ids)[me]

    padded_rope = jnp.pad(
        cache_rope.reshape(pool, block_len, rope_dim), ((0, 0), (0, 0), (0, LANES - rope_dim)))
    sizes = chunk_sizes(tok_group)
    starts = [sum(sizes[:i]) for i in range(len(sizes))]

    def fresh_of(n):
        seen = min(starts[n] + sizes[n], prefill_len)
        return min(-(-seen // LANES) * LANES, tok_group)

    def scratch(t):
        return [pltpu.VMEM((heads * t, width), bf16), pltpu.VMEM((heads * t, latent), bf16)]

    def first_chunk():
        t = sizes[0]
        q_nope = query_nope[:t].transpose(1, 0, 2)
        return pl.pallas_call(
            functools.partial(first_kernel, fresh_of(0), exp_scale),
            out_shape=[jax.ShapeDtypeStruct((t, heads * dv), bf16),
                       jax.ShapeDtypeStruct((prior + tok_group, width), bf16),
                       jax.ShapeDtypeStruct(absorb_key.shape, bf16),
                       jax.ShapeDtypeStruct(absorb_value.shape, bf16),
                       jax.ShapeDtypeStruct(query_nope.shape, bf16),
                       jax.ShapeDtypeStruct(query_rope.shape, bf16)],
            in_specs=[SMEM, SMEM, VMEM, HBM, HBM, HBM, HBM, HBM, ANY, HBM, VMEM],
            out_specs=[VMEM] * 6,
            scratch_shapes=[
                *scratch(t),
                pltpu.SemaphoreType.DMA((2 * blocks + 2,)),
                pltpu.SemaphoreType.DMA((heads + 3,)),
            ],
            name="attend_first",
            compiler_params=params(20),
            cost_estimate=LONG,
        )(prefill_table, prefill_offset, q_nope, in_hbm(query_nope), in_hbm(query_rope),
          in_hbm(absorb_key), in_hbm(absorb_value), in_hbm(cache_latent), padded_rope,
          in_hbm(new_latent), new_rope.T)

    def attend(n, held, after, brought=None):
        keys, wk, wv, q_nope, q_rope = held
        t = sizes[n]
        q_nope = q_nope[starts[n]:starts[n] + t].transpose(1, 0, 2)
        args = [q_nope, q_rope, wk, wv, keys]
        specs = [VMEM] * 5
        outs = [jax.ShapeDtypeStruct((t, heads * dv), bf16)]
        scratches = scratch(t)
        limit = 20
        static = (starts[n], fresh_of(n), prior)
        if n == 1:
            kernel = functools.partial(second_kernel, *static, exp_scale, len(after))
            args = [me[None], send_blocks] + args + [
                in_hbm(output_weight), in_hbm(cache_latent), padded_rope]
            specs = [SMEM, SMEM] + specs + [HBM, HBM, ANY]
            outs.append(jax.ShapeDtypeStruct(output_weight.shape, bf16))
            outs += [jax.ShapeDtypeStruct((capacity * block_len, width), bf16)] * groups
            scratches.append(pltpu.SemaphoreType.DMA((2 * groups * capacity + 1,)))
        elif n == len(sizes) - 1:
            kernel = functools.partial(last_kernel, *static, prefill_len, exp_scale, len(after))
            args = [me[None]] + args + [
                in_hbm(cache_latent), padded_rope, decode_table, decode_length[:, None], *brought]
            specs = [SMEM] + specs + [HBM, ANY, VMEM, VMEM] + [VMEM] * len(brought)
            span = pool * block_len + groups * capacity * block_len + min(LANES, tok_group)
            scratches += [pltpu.VMEM((span, width), bf16), pltpu.SemaphoreType.DMA((2 * pool,))]
            limit = 26
        else:
            kernel = functools.partial(later_kernel, *static, exp_scale, len(after))
        return pl.pallas_call(
            kernel,
            out_shape=outs,
            in_specs=specs + [ANY] * len(after),
            out_specs=[VMEM] * len(outs),
            scratch_shapes=scratches,
            name="attend",
            compiler_params=params(limit),
            cost_estimate=LONG,
        )(*args, *after)

    def migrate(packed):
        return [packed[0]] + [
            lax.ppermute(packed[s], "dp", [(i, (i + s) % groups) for i in range(groups)])
            for s in range(1, groups)]

    x0, *held = first_chunk()
    if not on_line:
        outs = []
        w = brought = None
        for n, t in enumerate(sizes):
            if n == 0:
                x = x0
            elif n == 1:
                x, w, *packed = attend(n, held, ())
                brought = migrate(packed)
            else:
                x, = attend(n, held, (), brought)
            mine = shift_groups(x)
            if groups % 2 == 0:
                mine += [swap_cores(y) for y in mine]
            own, others = project(place, mine, output_weight, (groups - 1,))
            partials = jnp.concatenate([own, others], axis=0).reshape(groups, t, columns)
            outs.append(lax.psum_scatter(partials, "tp", scatter_dimension=0, tiled=False))
        return jnp.concatenate(outs, axis=0)

    def inward(x):
        return lax.ppermute(x, "tp", INWARD)

    def across(x):
        return lax.ppermute(x, "tp", ACROSS)

    def outward(x):
        return lax.ppermute(x, "tp", OUTWARD)

    def gather(x, after):
        came = shift_groups(x)[1]
        return [x, came, swap_cores(x), swap_cores(stack([came], after))]

    t0, t1, t2, t3 = sizes
    x1, w, *packed = attend(1, held, (x0,))
    own0, rest0 = project(place, gather(x0, (x1,)), w, (3,), (), (x1,))
    in0 = inward(rest0)
    brought = migrate(packed)
    x2, = attend(2, held, (own0,))
    own1, rest1 = project(place, gather(x1, (x2,)), w, (3,), (), (x2,))
    in1 = inward(rest1)
    to_across0 = add(2 * t0, [(rest0, 0), (in0, 0)], (own1,))
    on0 = across(to_across0)
    x3, = attend(3, held, (to_across0,), brought)
    own2, rest2, near2 = project(place, gather(x2, (x3,)), w, (2, 1), (), (x3,))
    in2 = inward(rest2)
    to_across1 = add(2 * t1, [(rest1, 0), (in1, 0)], (own2,))
    on1 = across(to_across1)
    to_out0 = add(t0, [(rest0, 2 * t0), (on0, 0)], (own2,))
    out0 = outward(to_out0)
    done0 = add(t0, [(own0, 0), (in0, 2 * t0), (on0, t0), (out0, 0)], (to_across1,))
    own3, rest3, near = project(
        place, gather(x3, (to_across1, to_out0)), w, (2, 1), (near2,), (done0,))
    in3 = inward(rest3)
    to_across2 = add(2 * t2, [(rest2, 0), (in2, 0)], (own3,))
    on2 = across(to_across2)
    near_in = inward(near)
    to_out1 = add(t1, [(rest1, 2 * t1), (on1, 0)], (to_across2,))
    out1 = outward(to_out1)
    to_far = add(t3, [(rest3, 0), (in3, 0)], (to_out1,))
    far_on = across(to_far)
    done1 = add(t1, [(own1, 0), (in1, 2 * t1), (on1, t1), (out1, 0)], (to_far,))
    to_mid = add(t3, [(rest3, t3), (in3, t3)], (done1,))
    mid_on = across(to_mid)
    to_out2 = add(t2, [(near2, 0), (on2, 0)], (to_mid,))
    out2 = outward(to_out2)
    to_out3 = add(t3, [(near, t2), (far_on, 0)], (to_out2,))
    out3 = outward(to_out3)
    done2 = add(t2, [(own2, 0), (near_in, 0), (on2, t2), (out2, 0)], (to_out3,))
    return finish([done0, done1, done2], [(own3, 0), (near_in, t2), (mid_on, 0), (out3, 0)])


def solution(mesh):
    return jax.shard_map(
        body,
        mesh=mesh,
        in_specs=(
            P(("replica", "dp"), "tp", None),
            P(("replica", "dp"), "tp"),
            P(("replica", "dp"), None),
            P(("replica", "dp"), None),
            P(("replica", "dp"), None, None),
            P(("replica", "dp"), None),
            P("tp", None, None),
            P("tp", None, None),
            P("tp", "dp"),
            P(("replica", "dp"), None, None),
            P(("replica", "dp"), None),
            P(("replica", "dp")),
            P(("replica", "dp"), None),
            P(("replica", "dp")),
        ),
        out_specs=P(("replica", "tp"), "dp"),
        check_vma=False,
    )
```

```python
import functools

import jax
import jax.numpy as jnp
import numpy as np
from jax import lax
from jax.experimental import pallas as pl
from jax.experimental.pallas import tpu as pltpu
from jax.sharding import PartitionSpec as P

HIDDEN = -1e30
LANES = 128
MIB = 1024 * 1024
WEIGHT_PIECES = 16

SMEM = pl.BlockSpec(memory_space=pltpu.SMEM)
VMEM = pl.BlockSpec(memory_space=pltpu.VMEM)
HBM = pl.BlockSpec(memory_space=pltpu.HBM)
ANY = pl.BlockSpec(memory_space=pl.ANY)


def params(mib):
    return pltpu.CompilerParams(vmem_limit_bytes=mib * MIB)


def dot_nt(a, b):
    return lax.dot_general(a, b, (((1,), (1,)), ((), ())), preferred_element_type=jnp.float32)


def dot(a, b):
    return jnp.dot(a, b, preferred_element_type=jnp.float32)


def chunk_sizes(tok_group):
    if tok_group == 256:
        return (48, 64, 80, 64)
    return (tok_group,)


def rope_rows(rope_t):
    rows = jnp.transpose(rope_t.astype(jnp.float32), (1, 0))
    return jnp.concatenate(
        [rows, jnp.zeros((rows.shape[0], LANES - rows.shape[1]), jnp.float32)], axis=1
    ).astype(jnp.bfloat16)


def build_queries(q, q_nope, q_rope, first, wk, ready=None):
    heads = q_nope.shape[0]
    t = q.shape[0] // heads
    latent = wk.shape[2]
    rope_dim = q_rope.shape[1] // heads
    lane = lax.broadcasted_iota(jnp.int32, (t, LANES), 1)
    one = jnp.where(lane == rope_dim, 1.0, 0.0)
    per_tile = LANES // rope_dim
    for h in range(heads):
        pair = q_rope[first:first + t, h // per_tile * LANES:(h // per_tile + 1) * LANES].astype(jnp.float32)
        turn = h % per_tile * rope_dim
        if turn:
            pair = pltpu.roll(pair, LANES - turn, 1)
        q[h * t:(h + 1) * t, latent:] = jnp.where(lane < rope_dim, pair, one).astype(jnp.bfloat16)
    for h in range(heads):
        if ready is not None:
            ready(h)
        q[h * t:(h + 1) * t, :latent] = dot(q_nope[h, first:first + t, :], wk[h]).astype(jnp.bfloat16)


def prefill(q, keys, att, heads, t, first, prior, fresh, exp_scale):
    latent = att.shape[1]
    together = 1
    while together * 2 <= heads and together * 2 * t <= 384:
        together *= 2
    tile = together * t
    token = first + lax.broadcasted_iota(jnp.int32, (t, fresh), 0)
    key_token = lax.broadcasted_iota(jnp.int32, (t, fresh), 1)
    causal = (key_token <= token)[None]
    end = prior + fresh

    def scores_of(i):
        rows = q[i * tile:(i + 1) * tile, :]
        return dot_nt(rows, keys[:prior, :]), dot_nt(rows, keys[prior:end, :])

    steps = heads // together
    ahead = scores_of(0)
    for i in range(steps):
        s_old, s_new = ahead
        if i + 1 < steps:
            ahead = scores_of(i + 1)
        s_new = jnp.where(causal, s_new.reshape(together, t, fresh), HIDDEN).reshape(tile, fresh)
        top = jnp.maximum(jnp.max(s_old, axis=1, keepdims=True), jnp.max(s_new, axis=1, keepdims=True))
        p_old = jnp.exp2((s_old - top) * exp_scale)
        p_new = jnp.exp2((s_new - top) * exp_scale)
        total = jnp.sum(p_old, axis=1, keepdims=True) + jnp.sum(p_new, axis=1, keepdims=True)
        mixed = dot(p_old.astype(jnp.bfloat16), keys[:prior, :latent]) + dot(
            p_new.astype(jnp.bfloat16), keys[prior:end, :latent])
        att[i * tile:(i + 1) * tile, :] = (mixed / total).astype(jnp.bfloat16)


def head_outputs(out, att, wv, t):
    heads, _, dv = wv.shape
    for h in range(heads):
        out[:, h * dv:(h + 1) * dv] = dot(att[h * t:(h + 1) * t, :], wv[h]).astype(jnp.bfloat16)


def first_kernel(fresh, exp_scale, table, offset, q_nope, q_rope_hbm, wk_hbm, wv_hbm, cache_latent,
                 cache_rope, new_latent, new_rope_t, out, keys, wk, wv, q_rope, q, att, sems, wsems):
    heads = q_nope.shape[0]
    t = out.shape[0]
    block_len, latent = cache_latent.shape[1:]
    rope_dim = new_rope_t.shape[0]
    blocks = table.shape[1]
    prior = blocks * block_len
    tok_group = new_latent.shape[0]

    rope_copy = pltpu.make_async_copy(
        q_rope_hbm.at[pl.ds(0, t)], q_rope.at[pl.ds(0, t)], wsems.at[0])
    rope_copy.start()
    wk_copies = [pltpu.make_async_copy(wk_hbm.at[h], wk.at[h], wsems.at[1 + h]) for h in range(heads)]
    for c in wk_copies:
        c.start()
    copies = []
    for i in range(blocks):
        b = table[0, i]
        rows = pl.ds(i * block_len, block_len)
        copies.append(pltpu.make_async_copy(
            cache_latent.at[b], keys.at[rows, pl.ds(0, latent)], sems.at[2 * i]))
        copies.append(pltpu.make_async_copy(
            cache_rope.at[b], keys.at[rows, pl.ds(latent, LANES)], sems.at[2 * i + 1]))
    copies.append(pltpu.make_async_copy(
        new_latent, keys.at[pl.ds(prior, tok_group), pl.ds(0, latent)], sems.at[2 * blocks]))
    for c in copies:
        c.start()
    wv_copies = [
        pltpu.make_async_copy(wv_hbm.at[h], wv.at[h], wsems.at[1 + heads + h]) for h in range(heads)]
    for c in wv_copies:
        c.start()
    if t < tok_group:
        others = pltpu.make_async_copy(
            q_rope_hbm.at[pl.ds(t, tok_group - t)], q_rope.at[pl.ds(t, tok_group - t)],
            sems.at[2 * blocks + 1])
        others.start()

    keys[prior:, latent:] = rope_rows(new_rope_t[...])
    rope_copy.wait()
    build_queries(q, q_nope, q_rope, 0, wk, lambda h: wk_copies[h].wait())

    for c in copies:
        c.wait()
    lane = lax.broadcasted_iota(jnp.int32, (prior, LANES), 1)
    pos = lax.broadcasted_iota(jnp.int32, (prior, LANES), 0)
    hide = jnp.where((lane == rope_dim) & (pos >= offset[0]), HIDDEN, 0.0)
    keys[:prior, latent:] = (keys[:prior, latent:].astype(jnp.float32) + hide).astype(jnp.bfloat16)
    prefill(q, keys, att, heads, t, 0, prior, fresh, exp_scale)
    for c in wv_copies:
        c.wait()
    head_outputs(out, att, wv, t)
    if t < tok_group:
        others.wait()


def second_kernel(first, fresh, prior, exp_scale, n_after, me, ids, q_nope, q_rope, wk, wv, keys, w_hbm,
                  cache_latent, cache_rope, *rest):
    rest = rest[n_after:]
    groups = ids.shape[2]
    out, w, packed = rest[0], rest[1], rest[2:2 + groups]
    q, att, sems = rest[2 + groups:]
    heads = q_nope.shape[0]
    t = out.shape[0]
    block_len, latent = cache_latent.shape[1:]
    capacity = ids.shape[1]
    copies = []
    for s in range(groups):
        to = lax.rem(me[0] + s, groups)
        for k in range(capacity):
            b = ids[0, k, to]
            rows = pl.ds(k * block_len, block_len)
            copies.append(pltpu.make_async_copy(
                cache_latent.at[b], packed[s].at[rows, pl.ds(0, latent)], sems.at[len(copies)]))
            copies.append(pltpu.make_async_copy(
                cache_rope.at[b], packed[s].at[rows, pl.ds(latent, LANES)], sems.at[len(copies)]))
    depth = w.shape[0] // WEIGHT_PIECES
    for i in range(WEIGHT_PIECES):
        rows = pl.ds(i * depth, depth)
        copies.append(pltpu.make_async_copy(w_hbm.at[rows], w.at[rows], sems.at[len(copies)]))
    for c in copies:
        c.start()
    build_queries(q, q_nope, q_rope, first, wk)
    prefill(q, keys, att, heads, t, first, prior, fresh, exp_scale)
    head_outputs(out, att, wv, t)
    for c in copies:
        c.wait()


def later_kernel(first, fresh, prior, exp_scale, n_after, q_nope, q_rope, wk, wv, keys, *rest):
    out, q, att = rest[n_after:]
    heads = q_nope.shape[0]
    t = out.shape[0]
    build_queries(q, q_nope, q_rope, first, wk)
    prefill(q, keys, att, heads, t, first, prior, fresh, exp_scale)
    head_outputs(out, att, wv, t)


def last_kernel(first, fresh, prior, prefill_len, exp_scale, n_after, me, q_nope, q_rope, wk, wv, keys,
                cache_latent, cache_rope, decode_table, decode_length, *rest):
    received = rest[:-5 - n_after]
    out, q, att, dkeys, sems = rest[-5:]
    groups = len(received)
    heads = q_nope.shape[0]
    t = out.shape[0]
    pool, block_len, latent = cache_latent.shape
    got = received[0].shape[0]
    ext = pool * block_len + groups * got
    tail = dkeys.shape[0] - ext
    start = keys.shape[0] - tail
    copies = []
    for i in range(pool):
        rows = pl.ds(i * block_len, block_len)
        copies.append(pltpu.make_async_copy(
            cache_latent.at[i], dkeys.at[rows, pl.ds(0, latent)], sems.at[2 * i]))
        copies.append(pltpu.make_async_copy(
            cache_rope.at[i], dkeys.at[rows, pl.ds(latent, LANES)], sems.at[2 * i + 1]))
    for c in copies:
        c.start()
    for s in range(groups):
        source = lax.rem(me[0] + groups - s, groups)
        at = pl.multiple_of(pool * block_len + source * got, block_len)
        dkeys[pl.ds(at, got), :] = received[s][...]
    dkeys[ext:, :] = keys[start:, :]

    build_queries(q, q_nope, q_rope, first, wk)
    prefill(q, keys, att, heads, t, first, prior, fresh, exp_scale)

    slots, decodes = decode_table.shape
    for c in copies:
        c.wait()
    span = dkeys.shape[0]
    key = lax.broadcasted_iota(jnp.int32, (decodes, span), 1)
    request = lax.broadcasted_iota(jnp.int32, (decodes, span), 0)
    block = key // block_len
    pos = key % block_len
    own_key = key - ext + (start - prior) == request + prefill_len
    count = jnp.where(own_key, 1.0, 0.0)
    row = lax.broadcasted_iota(jnp.int32, (decodes, LANES), 0)

    def column(read):
        value = jnp.zeros((decodes, LANES), jnp.int32)
        for r in range(decodes):
            value = jnp.where(row == r, read(r), value)
        return value[:, :1]

    length = column(lambda r: decode_length[r])
    for m in range(slots):
        hit = (block == column(lambda r: decode_table[m, r])) & (pos + m * block_len < length) & (
            key < ext)
        count = count + jnp.where(hit, 1.0, 0.0)
    count = count[None]
    at = prefill_len - first
    half = heads // 2 if heads % 2 == 0 else heads
    for lo in range(0, heads, half):
        rows = jnp.concatenate(
            [q[h * t + at:h * t + at + decodes, :] for h in range(lo, lo + half)], axis=0)
        s = dot_nt(rows, dkeys[...]).reshape(half, decodes, span)
        s = jnp.where(count > 0.0, s, HIDDEN)
        top = jnp.max(s, axis=2, keepdims=True)
        p = count * jnp.exp2((s - top) * exp_scale)
        total = jnp.sum(p, axis=2, keepdims=True).reshape(half * decodes, 1)
        p = p.reshape(half * decodes, span).astype(jnp.bfloat16)
        mixed = (dot(p, dkeys[:, :latent]) / total).astype(jnp.bfloat16)
        for h in range(lo, lo + half):
            att[h * t + at:h * t + at + decodes, :] = mixed[(h - lo) * decodes:(h - lo + 1) * decodes]
    head_outputs(out, att, wv, t)


COST = pl.CostEstimate(flops=1000, bytes_accessed=1000, transcendentals=0)
LONG = pl.CostEstimate(flops=40_000_000_000, bytes_accessed=1000, transcendentals=0)


def in_hbm(x):
    return pltpu.with_memory_space_constraint(x, pltpu.HBM)


def project_kernel(n_parts, tails, places, me, z, w, *rest):
    parts, rest, x = rest[:n_parts], rest[n_parts:], rest[-1]
    own, outs = rest[-2 - len(tails)], rest[-1 - len(tails):-1]
    t = own.shape[0]
    lead = outs[-1].shape[0] - tails[-1] * t
    if lead:
        outs[-1][:lead, :] = rest[0][...]
    for i, part in enumerate(parts):
        place = 0
        for g, row in enumerate(places):
            for p, column in enumerate(row):
                place = jnp.where((me[0] == g) & (z[0] == p), column[i], place)
        x[pl.ds(pl.multiple_of(place * t, t), t), :] = part[...]
    columns = w.shape[1]
    step = 256 if columns % 256 == 0 else columns
    for at in range(0, columns, step):
        y = dot(x[...], w[:, at:at + step]).astype(jnp.bfloat16)
        own[:, at:at + step] = y[:t]
        row = t
        for i, n in enumerate(tails):
            skip = lead if i == len(tails) - 1 else 0
            outs[i][skip:skip + n * t, at:at + step] = y[row:row + n * t]
            row += n * t


def project(where, parts, w, tails, earlier=(), after=()):
    depth, columns = w.shape
    rows = sum(p.shape[0] for p in parts)
    t = rows // (1 + sum(tails))
    sizes = [t] + [n * t for n in tails]
    sizes[-1] += sum(e.shape[0] for e in earlier)
    places, me, z = where
    return pl.pallas_call(
        functools.partial(project_kernel, len(parts), tails, places),
        out_shape=[jax.ShapeDtypeStruct((n, columns), jnp.bfloat16) for n in sizes],
        in_specs=[SMEM, SMEM, VMEM] + [VMEM] * (len(parts) + len(earlier)) + [ANY] * len(after),
        out_specs=[VMEM] * len(sizes),
        scratch_shapes=[pltpu.VMEM((rows, depth), jnp.bfloat16)],
        name="project",
        compiler_params=params(12),
        cost_estimate=COST,
    )(me[None], z[None], w, *parts, *earlier, *after)


def add_kernel(spans, n_after, *refs):
    out = refs[-1]
    n = out.shape[0]
    total = None
    for ref, at in zip(refs, spans):
        x = ref[at:at + n, :].astype(jnp.float32)
        total = x if total is None else total + x
    out[...] = total.astype(jnp.bfloat16)


def add(rows, terms, after=()):
    return pl.pallas_call(
        functools.partial(add_kernel, [at for _, at in terms], len(after)),
        out_shape=jax.ShapeDtypeStruct((rows, terms[0][0].shape[1]), jnp.bfloat16),
        in_specs=[VMEM] * len(terms) + [ANY] * len(after),
        out_specs=VMEM,
        name="add",
        compiler_params=params(8),
        cost_estimate=COST,
    )(*[x for x, _ in terms], *after)


def finish_kernel(n_ready, spans, *refs):
    out = refs[-1]
    row = 0
    for ref in refs[:n_ready]:
        out[row:row + ref.shape[0], :] = ref[...]
        row += ref.shape[0]
    add_kernel(spans, 0, *refs[n_ready:-1], out.at[row:, :])


def finish(ready, terms):
    rows = sum(r.shape[0] for r in ready) + terms[0][0].shape[0]
    return pl.pallas_call(
        functools.partial(finish_kernel, len(ready), [at for _, at in terms]),
        out_shape=jax.ShapeDtypeStruct((rows, terms[0][0].shape[1]), jnp.bfloat16),
        in_specs=[VMEM] * (len(ready) + len(terms)),
        out_specs=VMEM,
        name="finish",
        compiler_params=params(8),
        cost_estimate=COST,
    )(*ready, *[x for x, _ in terms])


def gathered_ids(groups, me):
    if groups % 2:
        return [(me - s) % groups for s in range(groups)]
    return [(who - 2 * s) % groups for who in (me, me ^ 1) for s in range(groups // 2)]


def shift_groups(x):
    groups = lax.axis_size("dp")
    step = 1 if groups % 2 else 2
    return [x] + [lax.ppermute(x, "dp", [(i, (i + s) % groups) for i in range(groups)])
                  for s in range(step, groups, step)]


def stack_kernel(count, *refs):
    out, at = refs[-1], 0
    for ref in refs[:count]:
        out[at:at + ref.shape[0], :] = ref[...]
        at += ref.shape[0]


def stack(parts, after=()):
    rows = sum(p.shape[0] for p in parts)
    return pl.pallas_call(
        functools.partial(stack_kernel, len(parts)),
        out_shape=jax.ShapeDtypeStruct((rows, parts[0].shape[1]), parts[0].dtype),
        in_specs=[VMEM] * len(parts) + [ANY] * len(after),
        out_specs=VMEM,
        name="stack",
        compiler_params=params(4),
        cost_estimate=COST,
    )(*parts, *after)


def swap_cores(x):
    return lax.ppermute(x, "dp", [(i, i ^ 1) for i in range(lax.axis_size("dp"))])


LINE_ORDER = ((0, 3, 2, 1), (1, 3, 2, 0), (2, 0, 1, 3), (3, 0, 1, 2))
INWARD = [(0, 1), (3, 2)]
ACROSS = [(1, 2), (2, 1)]
OUTWARD = [(1, 0), (2, 3)]


def body(
    query_nope,
    query_rope,
    new_latent,
    new_rope,
    cache_latent,
    cache_rope,
    absorb_key,
    absorb_value,
    output_weight,
    send_blocks,
    prefill_table,
    prefill_offset,
    decode_table,
    decode_length,
):
    tok_group, heads, nope_dim = query_nope.shape
    pool, block_len, latent = cache_latent.shape
    rope_dim = new_rope.shape[1]
    capacity = send_blocks.shape[2]
    groups = lax.axis_size("dp")
    decodes = decode_length.shape[0]
    prefill_len = tok_group - decodes
    dv = absorb_value.shape[2]
    columns = output_weight.shape[1]
    exp_scale = float((nope_dim + rope_dim) ** (-0.5) * 1.4426950408889634)
    blocks = prefill_table.shape[1]
    prior = blocks * block_len
    width = latent + LANES
    on_line = lax.axis_size("tp") == 4 and groups == 4
    bf16 = jnp.bfloat16

    me = lax.axis_index("dp")
    z = lax.axis_index("tp")
    places = []
    for g in range(groups):
        came = gathered_ids(groups, g)
        if on_line:
            places.append([[order.index(k) for k in came] for order in LINE_ORDER])
        else:
            places.append([came])
    where = (places, me, z if on_line else z * 0)

    padded_rope = jnp.pad(
        cache_rope.reshape(pool, block_len, rope_dim), ((0, 0), (0, 0), (0, LANES - rope_dim)))
    q_nope = query_nope.transpose(1, 0, 2)
    sizes = chunk_sizes(tok_group)
    starts = [sum(sizes[:i]) for i in range(len(sizes))]

    def fresh_of(n):
        seen = min(starts[n] + sizes[n], prefill_len)
        return min(-(-seen // LANES) * LANES, tok_group)

    def scratch(t):
        return [pltpu.VMEM((heads * t, width), bf16), pltpu.VMEM((heads * t, latent), bf16)]

    def first_chunk():
        t = sizes[0]
        return pl.pallas_call(
            functools.partial(first_kernel, fresh_of(0), exp_scale),
            out_shape=[jax.ShapeDtypeStruct((t, heads * dv), bf16),
                       jax.ShapeDtypeStruct((prior + tok_group, width), bf16),
                       jax.ShapeDtypeStruct(absorb_key.shape, bf16),
                       jax.ShapeDtypeStruct(absorb_value.shape, bf16),
                       jax.ShapeDtypeStruct(query_rope.shape, bf16)],
            in_specs=[SMEM, SMEM, VMEM, HBM, HBM, HBM, HBM, ANY, HBM, VMEM],
            out_specs=[VMEM] * 5,
            scratch_shapes=[
                *scratch(t),
                pltpu.SemaphoreType.DMA((2 * blocks + 2,)),
                pltpu.SemaphoreType.DMA((2 * heads + 1,)),
            ],
            name="attend_first",
            compiler_params=params(20),
            cost_estimate=LONG,
        )(prefill_table, prefill_offset, q_nope, in_hbm(query_rope), in_hbm(absorb_key),
          in_hbm(absorb_value), in_hbm(cache_latent), padded_rope,
          in_hbm(new_latent), new_rope.T)

    def attend(n, held, after, brought=None):
        keys, wk, wv, q_rope = held
        t = sizes[n]
        args = [q_nope, q_rope, wk, wv, keys]
        specs = [VMEM] * 5
        outs = [jax.ShapeDtypeStruct((t, heads * dv), bf16)]
        scratches = scratch(t)
        limit = 20
        static = (starts[n], fresh_of(n), prior)
        if n == 1:
            kernel = functools.partial(second_kernel, *static, exp_scale, len(after))
            args = [me[None], send_blocks.transpose(0, 2, 1)] + args + [
                in_hbm(output_weight), in_hbm(cache_latent), padded_rope]
            specs = [SMEM, SMEM] + specs + [HBM, HBM, ANY]
            outs.append(jax.ShapeDtypeStruct(output_weight.shape, bf16))
            outs += [jax.ShapeDtypeStruct((capacity * block_len, width), bf16)] * groups
            scratches.append(pltpu.SemaphoreType.DMA((2 * groups * capacity + WEIGHT_PIECES,)))
        elif n == len(sizes) - 1:
            kernel = functools.partial(last_kernel, *static, prefill_len, exp_scale, len(after))
            args = [me[None]] + args + [
                in_hbm(cache_latent), padded_rope, decode_table.T, decode_length, *brought]
            specs = [SMEM] + specs + [HBM, ANY, SMEM, SMEM] + [VMEM] * len(brought)
            span = pool * block_len + groups * capacity * block_len + min(LANES, tok_group)
            scratches += [pltpu.VMEM((span, width), bf16), pltpu.SemaphoreType.DMA((2 * pool,))]
            limit = 26
        else:
            kernel = functools.partial(later_kernel, *static, exp_scale, len(after))
        return pl.pallas_call(
            kernel,
            out_shape=outs,
            in_specs=specs + [ANY] * len(after),
            out_specs=[VMEM] * len(outs),
            scratch_shapes=scratches,
            name="attend",
            compiler_params=params(limit),
            cost_estimate=LONG,
        )(*args, *after)

    def migrate(packed):
        return [packed[0]] + [
            lax.ppermute(packed[s], "dp", [(i, (i + s) % groups) for i in range(groups)])
            for s in range(1, groups)]

    x0, *held = first_chunk()
    if not on_line:
        outs = []
        w = brought = None
        for n, t in enumerate(sizes):
            if n == 0:
                x = x0
            elif n == 1:
                x, w, *packed = attend(n, held, ())
                brought = migrate(packed)
            else:
                x, = attend(n, held, (), brought)
            mine = shift_groups(x)
            if groups % 2 == 0:
                mine += [swap_cores(y) for y in mine]
            own, others = project(where, mine, output_weight, (groups - 1,))
            partials = jnp.concatenate([own, others], axis=0).reshape(groups, t, columns)
            outs.append(lax.psum_scatter(partials, "tp", scatter_dimension=0, tiled=False))
        return jnp.concatenate(outs, axis=0)

    def inward(x):
        return lax.ppermute(x, "tp", INWARD)

    def across(x):
        return lax.ppermute(x, "tp", ACROSS)

    def outward(x):
        return lax.ppermute(x, "tp", OUTWARD)

    def gather(x, after):
        came = shift_groups(x)[1]
        return [x, came, swap_cores(x), swap_cores(stack([came], after))]

    t0, t1, t2, t3 = sizes
    x1, w, *packed = attend(1, held, (x0,))
    own0, rest0 = project(where, gather(x0, (x1,)), w, (3,), (), (x1,))
    in0 = inward(rest0)
    brought = migrate(packed)
    x2, = attend(2, held, (own0,))
    own1, rest1 = project(where, gather(x1, (x2,)), w, (3,), (), (x2,))
    in1 = inward(rest1)
    to_across0 = add(2 * t0, [(rest0, 0), (in0, 0)], (own1,))
    on0 = across(to_across0)
    x3, = attend(3, held, (to_across0,), brought)
    own2, rest2, near2 = project(where, gather(x2, (x3,)), w, (2, 1), (), (x3,))
    in2 = inward(rest2)
    to_across1 = add(2 * t1, [(rest1, 0), (in1, 0)], (own2,))
    on1 = across(to_across1)
    to_out0 = add(t0, [(rest0, 2 * t0), (on0, 0)], (own2,))
    out0 = outward(to_out0)
    done0 = add(t0, [(own0, 0), (in0, 2 * t0), (on0, t0), (out0, 0)], (to_across1,))
    own3, rest3, near = project(
        where, gather(x3, (to_across1, to_out0)), w, (2, 1), (near2,), (done0,))
    in3 = inward(rest3)
    to_across2 = add(2 * t2, [(rest2, 0), (in2, 0)], (own3,))
    on2 = across(to_across2)
    near_in = inward(near)
    to_out1 = add(t1, [(rest1, 2 * t1), (on1, 0)], (to_across2,))
    out1 = outward(to_out1)
    to_far = add(t3, [(rest3, 0), (in3, 0)], (to_out1,))
    far_on = across(to_far)
    done1 = add(t1, [(own1, 0), (in1, 2 * t1), (on1, t1), (out1, 0)], (to_far,))
    to_mid = add(t3, [(rest3, t3), (in3, t3)], (done1,))
    mid_on = across(to_mid)
    to_out2 = add(t2, [(near2, 0), (on2, 0)], (to_mid,))
    out2 = outward(to_out2)
    to_out3 = add(t3, [(near, t2), (far_on, 0)], (to_out2,))
    out3 = outward(to_out3)
    done2 = add(t2, [(own2, 0), (near_in, 0), (on2, t2), (out2, 0)], (to_out3,))
    return finish([done0, done1, done2], [(own3, 0), (near_in, t2), (mid_on, 0), (out3, 0)])


def solution(mesh):
    return jax.shard_map(
        body,
        mesh=mesh,
        in_specs=(
            P(("replica", "dp"), "tp", None),
            P(("replica", "dp"), "tp"),
            P(("replica", "dp"), None),
            P(("replica", "dp"), None),
            P(("replica", "dp"), None, None),
            P(("replica", "dp"), None),
            P("tp", None, None),
            P("tp", None, None),
            P("tp", "dp"),
            P(("replica", "dp"), None, None),
            P(("replica", "dp"), None),
            P(("replica", "dp")),
            P(("replica", "dp"), None),
            P(("replica", "dp")),
        ),
        out_specs=P(("replica", "tp"), "dp"),
        check_vma=False,
    )
```

```python
import functools

import jax
import jax.numpy as jnp
import numpy as np
from jax import lax
from jax.experimental import pallas as pl
from jax.experimental.pallas import tpu as pltpu
from jax.sharding import PartitionSpec as P

HIDDEN = -1e30
LANES = 128
MIB = 1024 * 1024
PIECES = 4

SMEM = pl.BlockSpec(memory_space=pltpu.SMEM)
VMEM = pl.BlockSpec(memory_space=pltpu.VMEM)
HBM = pl.BlockSpec(memory_space=pltpu.HBM)
ANY = pl.BlockSpec(memory_space=pl.ANY)


def params(mib):
    return pltpu.CompilerParams(vmem_limit_bytes=mib * MIB)


def dot_nt(a, b):
    return lax.dot_general(a, b, (((1,), (1,)), ((), ())), preferred_element_type=jnp.float32)


def dot(a, b):
    return jnp.dot(a, b, preferred_element_type=jnp.float32)


def chunk_sizes(tok_group):
    if tok_group == 256:
        return (48, 80, 64, 64)
    return (tok_group,)


def rope_rows(rope_t):
    rows = jnp.transpose(rope_t.astype(jnp.float32), (1, 0))
    return jnp.concatenate(
        [rows, jnp.zeros((rows.shape[0], LANES - rows.shape[1]), jnp.float32)], axis=1
    ).astype(jnp.bfloat16)


def build_queries(q, q_nope, q_rope, first, wk, ready=None):
    heads = q_nope.shape[0]
    t = q.shape[0] // heads
    latent = wk.shape[2]
    rope_dim = q_rope.shape[1] // heads
    lane = lax.broadcasted_iota(jnp.int32, (t, LANES), 1)
    one = jnp.where(lane == rope_dim, 1.0, 0.0)
    per_tile = LANES // rope_dim
    for h in range(heads):
        pair = q_rope[first:first + t, h // per_tile * LANES:(h // per_tile + 1) * LANES].astype(jnp.float32)
        turn = h % per_tile * rope_dim
        if turn:
            pair = pltpu.roll(pair, LANES - turn, 1)
        q[h * t:(h + 1) * t, latent:] = jnp.where(lane < rope_dim, pair, one).astype(jnp.bfloat16)
    for h in range(heads):
        if ready is not None:
            ready(h)
        q[h * t:(h + 1) * t, :latent] = dot(q_nope[h, first:first + t, :], wk[h]).astype(jnp.bfloat16)


def prefill(q, keys, att, heads, t, first, prior, fresh, exp_scale):
    latent = att.shape[1]
    together = 1
    while together * 2 <= heads and together * 2 * t <= 384:
        together *= 2
    tile = together * t
    token = first + lax.broadcasted_iota(jnp.int32, (t, fresh), 0)
    key_token = lax.broadcasted_iota(jnp.int32, (t, fresh), 1)
    causal = (key_token <= token)[None]
    end = prior + fresh

    def scores_of(i):
        rows = q[i * tile:(i + 1) * tile, :]
        return dot_nt(rows, keys[:prior, :]), dot_nt(rows, keys[prior:end, :])

    steps = heads // together
    ahead = scores_of(0)
    for i in range(steps):
        s_old, s_new = ahead
        if i + 1 < steps:
            ahead = scores_of(i + 1)
        s_new = jnp.where(causal, s_new.reshape(together, t, fresh), HIDDEN).reshape(tile, fresh)
        top = jnp.maximum(jnp.max(s_old, axis=1, keepdims=True), jnp.max(s_new, axis=1, keepdims=True))
        p_old = jnp.exp2((s_old - top) * exp_scale)
        p_new = jnp.exp2((s_new - top) * exp_scale)
        total = jnp.sum(p_old, axis=1, keepdims=True) + jnp.sum(p_new, axis=1, keepdims=True)
        mixed = dot(p_old.astype(jnp.bfloat16), keys[:prior, :latent]) + dot(
            p_new.astype(jnp.bfloat16), keys[prior:end, :latent])
        att[i * tile:(i + 1) * tile, :] = (mixed / total).astype(jnp.bfloat16)


def head_outputs(out, att, wv, t):
    heads, _, dv = wv.shape
    for h in range(heads):
        out[:, h * dv:(h + 1) * dv] = dot(att[h * t:(h + 1) * t, :], wv[h]).astype(jnp.bfloat16)


def pieces(source, target, sems, first):
    size = source.shape[0] // PIECES
    return [pltpu.make_async_copy(source.at[pl.ds(i * size, size)], target.at[pl.ds(i * size, size)],
                                  sems.at[first + i]) for i in range(PIECES)]


def first_kernel(fresh, exp_scale, me, z, table, offset, q_nope, q_rope_hbm, wk_hbm, wv_hbm, cache_latent,
                 cache_rope, new_latent, new_rope_t, out, keys, wk, wv, q_rope, q, att, sems, wsems):
    heads = q_nope.shape[0]
    t = out.shape[0]
    block_len, latent = cache_latent.shape[1:]
    rope_dim = new_rope_t.shape[0]
    blocks = table.shape[1]
    prior = blocks * block_len
    tok_group = new_latent.shape[0]

    rope_copy = pltpu.make_async_copy(q_rope_hbm, q_rope, wsems.at[0])
    wk_copies = pieces(wk_hbm, wk, wsems, 1)
    wv_copies = pieces(wv_hbm, wv, wsems, 1 + PIECES)
    for c in wk_copies:
        c.start()
    rope_copy.start()
    copies = []
    for i in range(blocks):
        copies.append(pltpu.make_async_copy(
            cache_latent.at[table[0, i]],
            keys.at[pl.ds(i * block_len, block_len), pl.ds(0, latent)], sems.at[i]))
    copies.append(pltpu.make_async_copy(
        new_latent, keys.at[pl.ds(prior, tok_group), pl.ds(0, latent)], sems.at[blocks]))
    for c in copies + wv_copies:
        c.start()

    keys[prior:, latent:] = rope_rows(new_rope_t[...])
    lane = lax.broadcasted_iota(jnp.int32, (block_len, LANES), 1)
    pos = lax.broadcasted_iota(jnp.int32, (block_len, LANES), 0)
    for i in range(blocks):
        hide = jnp.where((lane == rope_dim) & (pos >= offset[0] - i * block_len), HIDDEN, 0.0)
        rope = cache_rope[table[0, i]].astype(jnp.float32) + hide
        keys[i * block_len:(i + 1) * block_len, latent:] = rope.astype(jnp.bfloat16)

    rope_copy.wait()

    def ready(h):
        if h * PIECES % heads == 0:
            wk_copies[h * PIECES // heads].wait()

    build_queries(q, q_nope, q_rope, 0, wk, ready)
    for c in copies:
        c.wait()
    prefill(q, keys, att, heads, t, 0, prior, fresh, exp_scale)
    for c in wv_copies:
        c.wait()
    head_outputs(out, att, wv, t)


def pack_kernel(me, ids, cache_latent, cache_rope, *rest):
    outs, sems = rest[:-1], rest[-1]
    groups = len(outs)
    block_len, latent = cache_latent.shape[1:]
    copies = []
    for s, out in enumerate(outs):
        to = lax.rem(me[0] + s, groups)
        for k in range(ids.shape[1]):
            rows = pl.ds(k * block_len, block_len)
            copies.append(pltpu.make_async_copy(
                cache_latent.at[ids[0, k, to]], out.at[rows, pl.ds(0, latent)], sems.at[len(copies)]))
    for c in copies:
        c.start()
    for s, out in enumerate(outs):
        to = lax.rem(me[0] + s, groups)
        for k in range(ids.shape[1]):
            out[k * block_len:(k + 1) * block_len, latent:] = cache_rope[ids[0, k, to]]
    for c in copies:
        c.wait()


def second_kernel(first, fresh, prior, exp_scale, n_after, q_nope, q_rope, wk, wv, keys, w_hbm, *rest):
    out, w, q, att, sems = rest[n_after:]
    heads = q_nope.shape[0]
    t = out.shape[0]
    copies = pieces(w_hbm, w, sems, 0)
    for c in copies:
        c.start()
    build_queries(q, q_nope, q_rope, first, wk)
    prefill(q, keys, att, heads, t, first, prior, fresh, exp_scale)
    head_outputs(out, att, wv, t)
    for c in copies:
        c.wait()


def later_kernel(first, fresh, prior, exp_scale, n_after, q_nope, q_rope, wk, wv, keys, *rest):
    out, q, att = rest[n_after:]
    heads = q_nope.shape[0]
    t = out.shape[0]
    build_queries(q, q_nope, q_rope, first, wk)
    prefill(q, keys, att, heads, t, first, prior, fresh, exp_scale)
    head_outputs(out, att, wv, t)


def last_kernel(first, fresh, prior, prefill_len, exp_scale, n_after, me, q_nope, q_rope, wk, wv, keys,
                flat_latent, cache_rope, decode_table, decode_length, *rest):
    received = rest[:-5 - n_after]
    out, q, att, dkeys, sems = rest[-5:]
    groups = len(received)
    heads = q_nope.shape[0]
    t = out.shape[0]
    pool, block_len, _ = cache_rope.shape
    latent = flat_latent.shape[1]
    got = received[0].shape[0]
    ext = pool * block_len + groups * got
    tail = dkeys.shape[0] - ext
    start = keys.shape[0] - tail
    copies = []
    for i in range(PIECES):
        rows = pl.ds(i * pool * block_len // PIECES, pool * block_len // PIECES)
        copies.append(pltpu.make_async_copy(
            flat_latent.at[rows], dkeys.at[rows, pl.ds(0, latent)], sems.at[i]))
    for c in copies:
        c.start()
    for i in range(pool):
        dkeys[i * block_len:(i + 1) * block_len, latent:] = cache_rope[i]
    for s in range(groups):
        source = lax.rem(me[0] + groups - s, groups)
        at = pl.multiple_of(pool * block_len + source * got, block_len)
        dkeys[pl.ds(at, got), :] = received[s][...]
    dkeys[ext:, :] = keys[start:, :]

    build_queries(q, q_nope, q_rope, first, wk)
    prefill(q, keys, att, heads, t, first, prior, fresh, exp_scale)

    slots, decodes = decode_table.shape
    for c in copies:
        c.wait()
    span = dkeys.shape[0]
    key = lax.broadcasted_iota(jnp.int32, (decodes, span), 1)
    request = lax.broadcasted_iota(jnp.int32, (decodes, span), 0)
    block = key // block_len
    pos = key % block_len
    own_key = key - ext + (start - prior) == request + prefill_len
    count = jnp.where(own_key, 1.0, 0.0)
    row = lax.broadcasted_iota(jnp.int32, (decodes, LANES), 0)

    def column(read):
        value = jnp.zeros((decodes, LANES), jnp.int32)
        for r in range(decodes):
            value = jnp.where(row == r, read(r), value)
        return value[:, :1]

    length = column(lambda r: decode_length[r])
    for m in range(slots):
        hit = (block == column(lambda r: decode_table[m, r])) & (pos + m * block_len < length) & (
            key < ext)
        count = count + jnp.where(hit, 1.0, 0.0)
    count = count[None]
    at = prefill_len - first
    half = heads // 2 if heads % 2 == 0 else heads
    for lo in range(0, heads, half):
        rows = jnp.concatenate(
            [q[h * t + at:h * t + at + decodes, :] for h in range(lo, lo + half)], axis=0)
        s = dot_nt(rows, dkeys[...]).reshape(half, decodes, span)
        s = jnp.where(count > 0.0, s, HIDDEN)
        top = jnp.max(s, axis=2, keepdims=True)
        p = count * jnp.exp2((s - top) * exp_scale)
        total = jnp.sum(p, axis=2, keepdims=True).reshape(half * decodes, 1)
        p = p.reshape(half * decodes, span).astype(jnp.bfloat16)
        mixed = (dot(p, dkeys[:, :latent]) / total).astype(jnp.bfloat16)
        for h in range(lo, lo + half):
            att[h * t + at:h * t + at + decodes, :] = mixed[(h - lo) * decodes:(h - lo + 1) * decodes]
    head_outputs(out, att, wv, t)


COST = pl.CostEstimate(flops=1000, bytes_accessed=1000, transcendentals=0)
LONG = pl.CostEstimate(flops=40_000_000_000, bytes_accessed=1000, transcendentals=0)
SHORT = pl.CostEstimate(flops=6_000_000_000, bytes_accessed=1000, transcendentals=0)


def in_hbm(x):
    return pltpu.with_memory_space_constraint(x, pltpu.HBM)


def project_kernel(n_parts, tails, places, me, z, w, *rest):
    parts, rest, x = rest[:n_parts], rest[n_parts:], rest[-1]
    own, outs = rest[-2 - len(tails)], rest[-1 - len(tails):-1]
    t = own.shape[0]
    lead = outs[-1].shape[0] - tails[-1] * t
    if lead:
        outs[-1][:lead, :] = rest[0][...]
    for i, part in enumerate(parts):
        place = 0
        for g, row in enumerate(places):
            for p, column in enumerate(row):
                place = jnp.where((me[0] == g) & (z[0] == p), column[i], place)
        x[pl.ds(pl.multiple_of(place * t, t), t), :] = part[...]
    columns = w.shape[1]
    step = 256 if columns % 256 == 0 else columns
    for at in range(0, columns, step):
        y = dot(x[...], w[:, at:at + step]).astype(jnp.bfloat16)
        own[:, at:at + step] = y[:t]
        row = t
        for i, n in enumerate(tails):
            skip = lead if i == len(tails) - 1 else 0
            outs[i][skip:skip + n * t, at:at + step] = y[row:row + n * t]
            row += n * t


def project(where, parts, w, tails, earlier=(), after=()):
    depth, columns = w.shape
    rows = sum(p.shape[0] for p in parts)
    t = rows // (1 + sum(tails))
    sizes = [t] + [n * t for n in tails]
    sizes[-1] += sum(e.shape[0] for e in earlier)
    places, me, z = where
    return pl.pallas_call(
        functools.partial(project_kernel, len(parts), tails, places),
        out_shape=[jax.ShapeDtypeStruct((n, columns), jnp.bfloat16) for n in sizes],
        in_specs=[SMEM, SMEM, VMEM] + [VMEM] * (len(parts) + len(earlier)) + [ANY] * len(after),
        out_specs=[VMEM] * len(sizes),
        scratch_shapes=[pltpu.VMEM((rows, depth), jnp.bfloat16)],
        name="project",
        compiler_params=params(12),
        cost_estimate=COST,
    )(me[None], z[None], w, *parts, *earlier, *after)


def add_kernel(spans, n_after, *refs):
    out = refs[-1]
    n = out.shape[0]
    total = None
    for ref, at in zip(refs, spans):
        x = ref[at:at + n, :].astype(jnp.float32)
        total = x if total is None else total + x
    out[...] = total.astype(jnp.bfloat16)


def add(rows, terms, after=()):
    return pl.pallas_call(
        functools.partial(add_kernel, [at for _, at in terms], len(after)),
        out_shape=jax.ShapeDtypeStruct((rows, terms[0][0].shape[1]), jnp.bfloat16),
        in_specs=[VMEM] * len(terms) + [ANY] * len(after),
        out_specs=VMEM,
        name="add",
        compiler_params=params(8),
        cost_estimate=COST,
    )(*[x for x, _ in terms], *after)


def finish_kernel(n_ready, spans, *refs):
    out = refs[-1]
    row = 0
    for ref in refs[:n_ready]:
        out[row:row + ref.shape[0], :] = ref[...]
        row += ref.shape[0]
    add_kernel(spans, 0, *refs[n_ready:-1], out.at[row:, :])


def finish(ready, terms):
    rows = sum(r.shape[0] for r in ready) + terms[0][0].shape[0]
    return pl.pallas_call(
        functools.partial(finish_kernel, len(ready), [at for _, at in terms]),
        out_shape=jax.ShapeDtypeStruct((rows, terms[0][0].shape[1]), jnp.bfloat16),
        in_specs=[VMEM] * (len(ready) + len(terms)),
        out_specs=VMEM,
        name="finish",
        compiler_params=params(8),
        cost_estimate=COST,
    )(*ready, *[x for x, _ in terms])


def gathered_ids(groups, me):
    if groups % 2:
        return [(me - s) % groups for s in range(groups)]
    return [(who - 2 * s) % groups for who in (me, me ^ 1) for s in range(groups // 2)]


def shift_groups(x):
    groups = lax.axis_size("dp")
    step = 1 if groups % 2 else 2
    return [x] + [lax.ppermute(x, "dp", [(i, (i + s) % groups) for i in range(groups)])
                  for s in range(step, groups, step)]


def stack_kernel(count, *refs):
    out, at = refs[-1], 0
    for ref in refs[:count]:
        out[at:at + ref.shape[0], :] = ref[...]
        at += ref.shape[0]


def stack(parts, after=()):
    rows = sum(p.shape[0] for p in parts)
    return pl.pallas_call(
        functools.partial(stack_kernel, len(parts)),
        out_shape=jax.ShapeDtypeStruct((rows, parts[0].shape[1]), parts[0].dtype),
        in_specs=[VMEM] * len(parts) + [ANY] * len(after),
        out_specs=VMEM,
        name="stack",
        compiler_params=params(4),
        cost_estimate=COST,
    )(*parts, *after)


def swap_cores(x):
    return lax.ppermute(x, "dp", [(i, i ^ 1) for i in range(lax.axis_size("dp"))])


LINE_ORDER = ((0, 3, 2, 1), (1, 3, 2, 0), (2, 0, 1, 3), (3, 0, 1, 2))
INWARD = [(0, 1), (3, 2)]
ACROSS = [(1, 2), (2, 1)]
OUTWARD = [(1, 0), (2, 3)]


def body(
    query_nope,
    query_rope,
    new_latent,
    new_rope,
    cache_latent,
    cache_rope,
    absorb_key,
    absorb_value,
    output_weight,
    send_blocks,
    prefill_table,
    prefill_offset,
    decode_table,
    decode_length,
):
    tok_group, heads, nope_dim = query_nope.shape
    pool, block_len, latent = cache_latent.shape
    rope_dim = new_rope.shape[1]
    capacity = send_blocks.shape[2]
    groups = lax.axis_size("dp")
    decodes = decode_length.shape[0]
    prefill_len = tok_group - decodes
    dv = absorb_value.shape[2]
    columns = output_weight.shape[1]
    exp_scale = float((nope_dim + rope_dim) ** (-0.5) * 1.4426950408889634)
    blocks = prefill_table.shape[1]
    prior = blocks * block_len
    width = latent + LANES
    on_line = lax.axis_size("tp") == 4 and groups == 4
    bf16 = jnp.bfloat16

    me = lax.axis_index("dp")
    z = lax.axis_index("tp")
    places = []
    for g in range(groups):
        came = gathered_ids(groups, g)
        if on_line:
            places.append([[order.index(k) for k in came] for order in LINE_ORDER])
        else:
            places.append([came])
    where = (places, me, z if on_line else z * 0)

    padded_rope = jnp.pad(
        cache_rope.reshape(pool, block_len, rope_dim), ((0, 0), (0, 0), (0, LANES - rope_dim)))
    q_nope = query_nope.transpose(1, 0, 2)
    sizes = chunk_sizes(tok_group)
    starts = [sum(sizes[:i]) for i in range(len(sizes))]

    def fresh_of(n):
        seen = min(starts[n] + sizes[n], prefill_len)
        return min(-(-seen // LANES) * LANES, tok_group)

    def scratch(t):
        return [pltpu.VMEM((heads * t, width), bf16), pltpu.VMEM((heads * t, latent), bf16)]

    def first_chunk():
        t = sizes[0]
        return pl.pallas_call(
            functools.partial(first_kernel, fresh_of(0), exp_scale),
            out_shape=[jax.ShapeDtypeStruct((t, heads * dv), bf16),
                       jax.ShapeDtypeStruct((prior + tok_group, width), bf16),
                       jax.ShapeDtypeStruct(absorb_key.shape, bf16),
                       jax.ShapeDtypeStruct(absorb_value.shape, bf16),
                       jax.ShapeDtypeStruct(query_rope.shape, bf16)],
            in_specs=[SMEM] * 4 + [VMEM, HBM, HBM, HBM, HBM, VMEM, HBM, VMEM],
            out_specs=[VMEM] * 5,
            scratch_shapes=[
                *scratch(t),
                pltpu.SemaphoreType.DMA((blocks + 1,)),
                pltpu.SemaphoreType.DMA((2 * PIECES + 1,)),
            ],
            name="attend_first",
            compiler_params=params(20),
            cost_estimate=LONG,
        )(me[None], z[None], prefill_table, prefill_offset, q_nope, in_hbm(query_rope), in_hbm(absorb_key),
          in_hbm(absorb_value), in_hbm(cache_latent), padded_rope,
          in_hbm(new_latent), new_rope.T)

    def attend(n, held, after, brought=None):
        keys, wk, wv, q_rope = held
        t = sizes[n]
        args = [q_nope, q_rope, wk, wv, keys]
        specs = [VMEM] * 5
        outs = [jax.ShapeDtypeStruct((t, heads * dv), bf16)]
        scratches = scratch(t)
        limit = 20
        static = (starts[n], fresh_of(n), prior)
        if n == 1:
            kernel = functools.partial(second_kernel, *static, exp_scale, len(after))
            args.append(in_hbm(output_weight))
            specs = specs + [HBM]
            outs.append(jax.ShapeDtypeStruct(output_weight.shape, bf16))
            scratches.append(pltpu.SemaphoreType.DMA((PIECES,)))
        elif n == len(sizes) - 1:
            kernel = functools.partial(last_kernel, *static, prefill_len, exp_scale, len(after))
            args = [me[None]] + args + [
                in_hbm(cache_latent.reshape(pool * block_len, latent)), padded_rope, decode_table.T, decode_length, *brought]
            specs = [SMEM] + specs + [HBM, VMEM, SMEM, SMEM] + [VMEM] * len(brought)
            span = pool * block_len + groups * capacity * block_len + min(LANES, tok_group)
            scratches += [pltpu.VMEM((span, width), bf16), pltpu.SemaphoreType.DMA((PIECES,))]
            limit = 26
        else:
            kernel = functools.partial(later_kernel, *static, exp_scale, len(after))
        return pl.pallas_call(
            kernel,
            out_shape=outs,
            in_specs=specs + [ANY] * len(after),
            out_specs=[VMEM] * len(outs),
            scratch_shapes=scratches,
            name="attend",
            compiler_params=params(limit),
            cost_estimate=SHORT if n == len(sizes) - 1 else LONG,
        )(*args, *after)

    def migrate():
        packed = pl.pallas_call(
            pack_kernel,
            out_shape=[jax.ShapeDtypeStruct((capacity * block_len, width), bf16)] * groups,
            in_specs=[SMEM, SMEM, HBM, VMEM],
            out_specs=[VMEM] * groups,
            scratch_shapes=[pltpu.SemaphoreType.DMA((groups * capacity,))],
            name="pack",
            compiler_params=params(8),
            cost_estimate=COST,
        )(me[None], send_blocks.transpose(0, 2, 1), in_hbm(cache_latent), padded_rope)
        return [packed[0]] + [
            lax.ppermute(packed[s], "dp", [(i, (i + s) % groups) for i in range(groups)])
            for s in range(1, groups)]

    brought = migrate()
    x0, *held = first_chunk()
    if not on_line:
        outs = []
        w = None
        for n, t in enumerate(sizes):
            if n == 0:
                x = x0
            elif n == 1:
                x, w = attend(n, held, ())
            else:
                x, = attend(n, held, (), brought)
            mine = shift_groups(x)
            if groups % 2 == 0:
                mine += [swap_cores(y) for y in mine]
            own, others = project(where, mine, output_weight, (groups - 1,))
            partials = jnp.concatenate([own, others], axis=0).reshape(groups, t, columns)
            outs.append(lax.psum_scatter(partials, "tp", scatter_dimension=0, tiled=False))
        return jnp.concatenate(outs, axis=0)

    def inward(x):
        return lax.ppermute(x, "tp", INWARD)

    def across(x):
        return lax.ppermute(x, "tp", ACROSS)

    def outward(x):
        return lax.ppermute(x, "tp", OUTWARD)

    def gather(x, after):
        came = shift_groups(x)[1]
        return [x, came, swap_cores(x), swap_cores(stack([came], after))]

    t0, t1, t2, t3 = sizes
    x1, w = attend(1, held, (x0, *brought))
    own0, rest0 = project(where, gather(x0, (x1,)), w, (3,), (), (x1,))
    in0 = inward(rest0)
    x2, = attend(2, held, (own0,))
    own1, rest1 = project(where, gather(x1, (x2,)), w, (3,), (), (x2,))
    in1 = inward(rest1)
    to_across0 = add(2 * t0, [(rest0, 0), (in0, 0)], (own1,))
    on0 = across(to_across0)
    x3, = attend(3, held, (to_across0,), brought)
    own2, rest2, near2 = project(where, gather(x2, (x3,)), w, (2, 1), (), (x3,))
    in2 = inward(rest2)
    to_across1 = add(2 * t1, [(rest1, 0), (in1, 0)], (own2,))
    on1 = across(to_across1)
    to_out0 = add(t0, [(rest0, 2 * t0), (on0, 0)], (own2,))
    out0 = outward(to_out0)
    own3, rest3, near = project(
        where, gather(x3, (to_across1, to_out0)), w, (2, 1), (near2,),
        (to_across1, to_out0))
    done0 = add(t0, [(own0, 0), (in0, 2 * t0), (on0, t0), (out0, 0)], (own3,))
    in3 = inward(rest3)
    to_across2 = add(2 * t2, [(rest2, 0), (in2, 0)], (done0,))
    on2 = across(to_across2)
    near_in = inward(near)
    to_out1 = add(t1, [(rest1, 2 * t1), (on1, 0)], (to_across2,))
    out1 = outward(to_out1)
    to_far = add(t3, [(rest3, 0), (in3, 0)], (to_out1,))
    far_on = across(to_far)
    done1 = add(t1, [(own1, 0), (in1, 2 * t1), (on1, t1), (out1, 0)], (to_far,))
    to_mid = add(t3, [(rest3, t3), (in3, t3)], (done1,))
    mid_on = across(to_mid)
    to_out2 = add(t2, [(near2, 0), (on2, 0)], (to_mid,))
    out2 = outward(to_out2)
    to_out3 = add(t3, [(near, t2), (far_on, 0)], (to_out2,))
    out3 = outward(to_out3)
    done2 = add(t2, [(own2, 0), (near_in, 0), (on2, t2), (out2, 0)], (to_out3,))
    return finish([done0, done1, done2], [(own3, 0), (near_in, t2), (mid_on, 0), (out3, 0)])


def solution(mesh):
    return jax.shard_map(
        body,
        mesh=mesh,
        in_specs=(
            P(("replica", "dp"), "tp", None),
            P(("replica", "dp"), "tp"),
            P(("replica", "dp"), None),
            P(("replica", "dp"), None),
            P(("replica", "dp"), None, None),
            P(("replica", "dp"), None),
            P("tp", None, None),
            P("tp", None, None),
            P("tp", "dp"),
            P(("replica", "dp"), None, None),
            P(("replica", "dp"), None),
            P(("replica", "dp")),
            P(("replica", "dp"), None),
            P(("replica", "dp")),
        ),
        out_specs=P(("replica", "tp"), "dp"),
        check_vma=False,
    )
```

```python
import functools

import jax
import jax.numpy as jnp
import numpy as np
from jax import lax
from jax.experimental import pallas as pl
from jax.experimental.pallas import tpu as pltpu
from jax.sharding import PartitionSpec as P

HIDDEN = -1e30
LANES = 128
MIB = 1024 * 1024
PIECES = 4

SMEM = pl.BlockSpec(memory_space=pltpu.SMEM)
VMEM = pl.BlockSpec(memory_space=pltpu.VMEM)
HBM = pl.BlockSpec(memory_space=pltpu.HBM)
ANY = pl.BlockSpec(memory_space=pl.ANY)


def params(mib):
    return pltpu.CompilerParams(vmem_limit_bytes=mib * MIB)


def dot_nt(a, b):
    return lax.dot_general(a, b, (((1,), (1,)), ((), ())), preferred_element_type=jnp.float32)


def dot(a, b):
    return jnp.dot(a, b, preferred_element_type=jnp.float32)


def chunk_sizes(tok_group):
    if tok_group == 256:
        return (48, 64, 80, 64)
    return (tok_group,)


def rope_rows(rope_t):
    rows = jnp.transpose(rope_t.astype(jnp.float32), (1, 0))
    return jnp.concatenate(
        [rows, jnp.zeros((rows.shape[0], LANES - rows.shape[1]), jnp.float32)], axis=1
    ).astype(jnp.bfloat16)


def build_queries(q, q_nope, q_rope, first, wk, ready=None):
    heads = q_nope.shape[0]
    t = q.shape[0] // heads
    latent = wk.shape[2]
    rope_dim = q_rope.shape[1] // heads
    lane = lax.broadcasted_iota(jnp.int32, (t, LANES), 1)
    one = jnp.where(lane == rope_dim, 1.0, 0.0)
    per_tile = LANES // rope_dim
    for h in range(heads):
        pair = q_rope[first:first + t, h // per_tile * LANES:(h // per_tile + 1) * LANES].astype(jnp.float32)
        turn = h % per_tile * rope_dim
        if turn:
            pair = pltpu.roll(pair, LANES - turn, 1)
        q[h * t:(h + 1) * t, latent:] = jnp.where(lane < rope_dim, pair, one).astype(jnp.bfloat16)
    for h in range(heads):
        if ready is not None:
            ready(h)
        q[h * t:(h + 1) * t, :latent] = dot(q_nope[h, first:first + t, :], wk[h]).astype(jnp.bfloat16)


def prefill(q, keys, att, heads, t, first, prior, fresh, exp_scale):
    latent = att.shape[1]
    together = 1
    while together * 2 <= heads and together * 2 * t <= 384:
        together *= 2
    tile = together * t
    token = first + lax.broadcasted_iota(jnp.int32, (t, fresh), 0)
    key_token = lax.broadcasted_iota(jnp.int32, (t, fresh), 1)
    causal = (key_token <= token)[None]
    end = prior + fresh

    def scores_of(i):
        rows = q[i * tile:(i + 1) * tile, :]
        return dot_nt(rows, keys[:prior, :]), dot_nt(rows, keys[prior:end, :])

    steps = heads // together
    ahead = scores_of(0)
    for i in range(steps):
        s_old, s_new = ahead
        if i + 1 < steps:
            ahead = scores_of(i + 1)
        s_new = jnp.where(causal, s_new.reshape(together, t, fresh), HIDDEN).reshape(tile, fresh)
        top = jnp.maximum(jnp.max(s_old, axis=1, keepdims=True), jnp.max(s_new, axis=1, keepdims=True))
        p_old = jnp.exp2((s_old - top) * exp_scale)
        p_new = jnp.exp2((s_new - top) * exp_scale)
        total = jnp.sum(p_old, axis=1, keepdims=True) + jnp.sum(p_new, axis=1, keepdims=True)
        mixed = dot(p_old.astype(jnp.bfloat16), keys[:prior, :latent]) + dot(
            p_new.astype(jnp.bfloat16), keys[prior:end, :latent])
        att[i * tile:(i + 1) * tile, :] = (mixed / total).astype(jnp.bfloat16)


def head_outputs(out, att, wv, t):
    heads, _, dv = wv.shape
    for h in range(heads):
        out[:, h * dv:(h + 1) * dv] = dot(att[h * t:(h + 1) * t, :], wv[h]).astype(jnp.bfloat16)


def pieces(source, target, sems, first):
    size = source.shape[0] // PIECES
    return [pltpu.make_async_copy(source.at[pl.ds(i * size, size)], target.at[pl.ds(i * size, size)],
                                  sems.at[first + i]) for i in range(PIECES)]


def first_kernel(fresh, exp_scale, me, z, table, offset, q_nope, q_rope_hbm, wk_hbm, wv_hbm, cache_latent,
                 cache_rope, new_latent, new_rope_t, out, keys, wk, wv, q_rope, q, att, sems, wsems):
    heads = q_nope.shape[0]
    t = out.shape[0]
    block_len, latent = cache_latent.shape[1:]
    rope_dim = new_rope_t.shape[0]
    blocks = table.shape[1]
    prior = blocks * block_len
    tok_group = new_latent.shape[0]

    rope_copies = [pltpu.make_async_copy(
        q_rope_hbm.at[pl.ds(at, size)], q_rope.at[pl.ds(at, size)], wsems.at[n])
        for n, (at, size) in enumerate(((0, t), (t, tok_group - t))) if size]
    wk_copies = pieces(wk_hbm, wk, wsems, 2)
    later = pieces(wv_hbm, wv, wsems, 2 + PIECES) + rope_copies[1:]
    for c in wk_copies + rope_copies[:1]:
        c.start()
    copies = []
    for i in range(blocks):
        copies.append(pltpu.make_async_copy(
            cache_latent.at[table[0, i]],
            keys.at[pl.ds(i * block_len, block_len), pl.ds(0, latent)], sems.at[i]))
    copies.append(pltpu.make_async_copy(
        new_latent, keys.at[pl.ds(prior, tok_group), pl.ds(0, latent)], sems.at[blocks]))
    for c in copies:
        c.start()

    keys[prior:, latent:] = rope_rows(new_rope_t[...])
    lane = lax.broadcasted_iota(jnp.int32, (block_len, LANES), 1)
    pos = lax.broadcasted_iota(jnp.int32, (block_len, LANES), 0)
    for i in range(blocks):
        hide = jnp.where((lane == rope_dim) & (pos >= offset[0] - i * block_len), HIDDEN, 0.0)
        rope = cache_rope[table[0, i]].astype(jnp.float32) + hide
        keys[i * block_len:(i + 1) * block_len, latent:] = rope.astype(jnp.bfloat16)

    rope_copies[0].wait()

    def ready(h):
        if h * PIECES % heads == 0:
            wk_copies[h * PIECES // heads].wait()

    build_queries(q, q_nope, q_rope, 0, wk, ready)
    for c in copies:
        c.wait()
    for c in later:
        c.start()
    prefill(q, keys, att, heads, t, 0, prior, fresh, exp_scale)
    for c in later:
        c.wait()
    head_outputs(out, att, wv, t)


def pack_kernel(n_after, plan, me, ids, cache_latent, cache_rope, *rest):
    outs, sems = rest[n_after:-1], rest[-1]
    block_len, latent = cache_latent.shape[1:]
    copies = []
    places = []
    for out, targets in zip(outs, plan):
        row = 0
        for target in targets:
            to = target(me[0])
            for k in range(ids.shape[1]):
                places.append((out, row, ids[0, k, to]))
                row += block_len
    for n, (out, row, b) in enumerate(places):
        copies.append(pltpu.make_async_copy(
            cache_latent.at[b], out.at[pl.ds(row, block_len), pl.ds(0, latent)], sems.at[n]))
        copies[-1].start()
    for out, row, b in places:
        out[row:row + block_len, latent:] = cache_rope[b]
    for c in copies:
        c.wait()


def later_kernel(first, fresh, prior, exp_scale, n_after, q_nope, q_rope, wk, wv, keys, *rest):
    out, q, att = rest[n_after:]
    heads = q_nope.shape[0]
    t = out.shape[0]
    build_queries(q, q_nope, q_rope, first, wk)
    prefill(q, keys, att, heads, t, first, prior, fresh, exp_scale)
    head_outputs(out, att, wv, t)


def last_kernel(first, fresh, prior, prefill_len, exp_scale, n_after, spots, got, me, q_nope, q_rope, wk, wv, keys,
                flat_latent, cache_rope, decode_table, decode_length, *rest):
    received = rest[:-5 - n_after]
    out, q, att, dkeys, sems = rest[-5:]
    groups = len(spots)
    heads = q_nope.shape[0]
    t = out.shape[0]
    pool, block_len, _ = cache_rope.shape
    latent = flat_latent.shape[1]
    ext = pool * block_len + groups * got
    tail = dkeys.shape[0] - ext
    start = keys.shape[0] - tail
    copies = []
    for i in range(PIECES):
        rows = pl.ds(i * pool * block_len // PIECES, pool * block_len // PIECES)
        copies.append(pltpu.make_async_copy(
            flat_latent.at[rows], dkeys.at[rows, pl.ds(0, latent)], sems.at[i]))
    for c in copies:
        c.start()
    for i in range(pool):
        dkeys[i * block_len:(i + 1) * block_len, latent:] = cache_rope[i]
    for n, row, source in spots:
        at = pl.multiple_of(pool * block_len + source(me[0]) * got, block_len)
        dkeys[pl.ds(at, got), :] = received[n][row:row + got, :]
    dkeys[ext:, :] = keys[start:, :]

    build_queries(q, q_nope, q_rope, first, wk)
    prefill(q, keys, att, heads, t, first, prior, fresh, exp_scale)

    slots, decodes = decode_table.shape
    for c in copies:
        c.wait()
    span = dkeys.shape[0]
    key = lax.broadcasted_iota(jnp.int32, (decodes, span), 1)
    request = lax.broadcasted_iota(jnp.int32, (decodes, span), 0)
    block = key // block_len
    pos = key % block_len
    own_key = key - ext + (start - prior) == request + prefill_len
    count = jnp.where(own_key, 1.0, 0.0)
    row = lax.broadcasted_iota(jnp.int32, (decodes, LANES), 0)

    def column(read):
        value = jnp.zeros((decodes, LANES), jnp.int32)
        for r in range(decodes):
            value = jnp.where(row == r, read(r), value)
        return value[:, :1]

    length = column(lambda r: decode_length[r])
    for m in range(slots):
        hit = (block == column(lambda r: decode_table[m, r])) & (pos + m * block_len < length) & (
            key < ext)
        count = count + jnp.where(hit, 1.0, 0.0)
    count = count[None]
    at = prefill_len - first
    half = heads // 2 if heads % 2 == 0 else heads
    for lo in range(0, heads, half):
        rows = jnp.concatenate(
            [q[h * t + at:h * t + at + decodes, :] for h in range(lo, lo + half)], axis=0)
        s = dot_nt(rows, dkeys[...]).reshape(half, decodes, span)
        s = jnp.where(count > 0.0, s, HIDDEN)
        top = jnp.max(s, axis=2, keepdims=True)
        p = count * jnp.exp2((s - top) * exp_scale)
        total = jnp.sum(p, axis=2, keepdims=True).reshape(half * decodes, 1)
        p = p.reshape(half * decodes, span).astype(jnp.bfloat16)
        mixed = (dot(p, dkeys[:, :latent]) / total).astype(jnp.bfloat16)
        for h in range(lo, lo + half):
            att[h * t + at:h * t + at + decodes, :] = mixed[(h - lo) * decodes:(h - lo + 1) * decodes]
    head_outputs(out, att, wv, t)


COST = pl.CostEstimate(flops=1000, bytes_accessed=1000, transcendentals=0)
LONG = pl.CostEstimate(flops=40_000_000_000, bytes_accessed=1000, transcendentals=0)
SHORT = pl.CostEstimate(flops=6_000_000_000, bytes_accessed=1000, transcendentals=0)


def in_hbm(x):
    return pltpu.with_memory_space_constraint(x, pltpu.HBM)


def project_kernel(n_parts, tails, places, me, z, w, *rest):
    parts, rest, x = rest[:n_parts], rest[n_parts:], rest[-1]
    own, outs = rest[-2 - len(tails)], rest[-1 - len(tails):-1]
    t = own.shape[0]
    lead = outs[-1].shape[0] - tails[-1] * t
    if lead:
        outs[-1][:lead, :] = rest[0][...]
    for i, part in enumerate(parts):
        place = 0
        for g, row in enumerate(places):
            for p, column in enumerate(row):
                place = jnp.where((me[0] == g) & (z[0] == p), column[i], place)
        x[pl.ds(pl.multiple_of(place * t, t), t), :] = part[...]
    columns = w.shape[1]
    step = 256 if columns % 256 == 0 else columns
    for at in range(0, columns, step):
        y = dot(x[...], w[:, at:at + step]).astype(jnp.bfloat16)
        own[:, at:at + step] = y[:t]
        row = t
        for i, n in enumerate(tails):
            skip = lead if i == len(tails) - 1 else 0
            outs[i][skip:skip + n * t, at:at + step] = y[row:row + n * t]
            row += n * t


def project(where, parts, w, tails, earlier=(), after=()):
    depth, columns = w.shape
    rows = sum(p.shape[0] for p in parts)
    t = rows // (1 + sum(tails))
    sizes = [t] + [n * t for n in tails]
    sizes[-1] += sum(e.shape[0] for e in earlier)
    places, me, z = where
    return pl.pallas_call(
        functools.partial(project_kernel, len(parts), tails, places),
        out_shape=[jax.ShapeDtypeStruct((n, columns), jnp.bfloat16) for n in sizes],
        in_specs=[SMEM, SMEM, VMEM] + [VMEM] * (len(parts) + len(earlier)) + [ANY] * len(after),
        out_specs=[VMEM] * len(sizes),
        scratch_shapes=[pltpu.VMEM((rows, depth), jnp.bfloat16)],
        name="project",
        compiler_params=params(12),
        cost_estimate=COST,
    )(me[None], z[None], w, *parts, *earlier, *after)


def add_kernel(sums, *refs):
    out = refs[-1]
    row = i = 0
    for rows, spans in sums:
        total = None
        for at in spans:
            x = refs[i][at:at + rows, :].astype(jnp.float32)
            total = x if total is None else total + x
            i += 1
        out[row:row + rows, :] = total.astype(jnp.bfloat16)
        row += rows


def add_all(sums, after=()):
    terms = [x for _, parts in sums for x, _ in parts]
    return pl.pallas_call(
        functools.partial(add_kernel, [(rows, [at for _, at in parts]) for rows, parts in sums]),
        out_shape=jax.ShapeDtypeStruct((sum(rows for rows, _ in sums), terms[0].shape[1]), jnp.bfloat16),
        in_specs=[VMEM] * len(terms) + [ANY] * len(after),
        out_specs=VMEM,
        name="add",
        compiler_params=params(8),
        cost_estimate=COST,
    )(*terms, *after)


def add(rows, terms, after=()):
    return add_all([(rows, terms)], after)


def finish_kernel(n_ready, spans, *refs):
    out = refs[-1]
    row = 0
    for ref in refs[:n_ready]:
        out[row:row + ref.shape[0], :] = ref[...]
        row += ref.shape[0]
    add_kernel([(out.shape[0] - row, spans)], *refs[n_ready:-1], out.at[row:, :])


def finish(ready, terms):
    rows = sum(r.shape[0] for r in ready) + terms[0][0].shape[0]
    return pl.pallas_call(
        functools.partial(finish_kernel, len(ready), [at for _, at in terms]),
        out_shape=jax.ShapeDtypeStruct((rows, terms[0][0].shape[1]), jnp.bfloat16),
        in_specs=[VMEM] * (len(ready) + len(terms)),
        out_specs=VMEM,
        name="finish",
        compiler_params=params(8),
        cost_estimate=COST,
    )(*ready, *[x for x, _ in terms])


def gathered_ids(groups, me):
    if groups % 2:
        return [(me - s) % groups for s in range(groups)]
    return [(who - 2 * s) % groups for who in (me, me ^ 1) for s in range(groups // 2)]


def shift_groups(x):
    groups = lax.axis_size("dp")
    step = 1 if groups % 2 else 2
    return [x] + [lax.ppermute(x, "dp", [(i, (i + s) % groups) for i in range(groups)])
                  for s in range(step, groups, step)]


def stack_kernel(firsts, *refs):
    out, at = refs[-1], 0
    for ref, first in zip(refs, firsts):
        n = ref.shape[0] - first
        out[at:at + n, :] = ref[first:, :]
        at += n


def stack(parts, after=()):
    parts = [p if isinstance(p, tuple) else (p, 0) for p in parts]
    rows = sum(p.shape[0] - first for p, first in parts)
    return pl.pallas_call(
        functools.partial(stack_kernel, [first for _, first in parts]),
        out_shape=jax.ShapeDtypeStruct((rows, parts[0][0].shape[1]), jnp.bfloat16),
        in_specs=[VMEM] * len(parts) + [ANY] * len(after),
        out_specs=VMEM,
        name="stack",
        compiler_params=params(4),
        cost_estimate=COST,
    )(*[p for p, _ in parts], *after)


def swap_cores(x):
    return lax.ppermute(x, "dp", [(i, i ^ 1) for i in range(lax.axis_size("dp"))])


LINE_ORDER = ((0, 3, 2, 1), (1, 3, 2, 0), (2, 0, 1, 3), (3, 0, 1, 2))
INWARD = [(0, 1), (3, 2)]
ACROSS = [(1, 2), (2, 1)]
OUTWARD = [(1, 0), (2, 3)]


def body(
    query_nope,
    query_rope,
    new_latent,
    new_rope,
    cache_latent,
    cache_rope,
    absorb_key,
    absorb_value,
    output_weight,
    send_blocks,
    prefill_table,
    prefill_offset,
    decode_table,
    decode_length,
):
    tok_group, heads, nope_dim = query_nope.shape
    pool, block_len, latent = cache_latent.shape
    rope_dim = new_rope.shape[1]
    capacity = send_blocks.shape[2]
    groups = lax.axis_size("dp")
    decodes = decode_length.shape[0]
    prefill_len = tok_group - decodes
    dv = absorb_value.shape[2]
    columns = output_weight.shape[1]
    exp_scale = float((nope_dim + rope_dim) ** (-0.5) * 1.4426950408889634)
    blocks = prefill_table.shape[1]
    prior = blocks * block_len
    width = latent + LANES
    on_line = lax.axis_size("tp") == 4 and groups == 4
    bf16 = jnp.bfloat16

    me = lax.axis_index("dp")
    z = lax.axis_index("tp")
    places = []
    for g in range(groups):
        came = gathered_ids(groups, g)
        if on_line:
            places.append([[order.index(k) for k in came] for order in LINE_ORDER])
        else:
            places.append([came])
    where = (places, me, z if on_line else z * 0)

    padded_rope = jnp.pad(
        cache_rope.reshape(pool, block_len, rope_dim), ((0, 0), (0, 0), (0, LANES - rope_dim)))
    q_nope = query_nope.transpose(1, 0, 2)
    sizes = chunk_sizes(tok_group)
    starts = [sum(sizes[:i]) for i in range(len(sizes))]

    def fresh_of(n):
        seen = min(starts[n] + sizes[n], prefill_len)
        return min(-(-seen // LANES) * LANES, tok_group)

    def scratch(t):
        return [pltpu.VMEM((heads * t, width), bf16), pltpu.VMEM((heads * t, latent), bf16)]

    def first_chunk():
        t = sizes[0]
        return pl.pallas_call(
            functools.partial(first_kernel, fresh_of(0), exp_scale),
            out_shape=[jax.ShapeDtypeStruct((t, heads * dv), bf16),
                       jax.ShapeDtypeStruct((prior + tok_group, width), bf16),
                       jax.ShapeDtypeStruct(absorb_key.shape, bf16),
                       jax.ShapeDtypeStruct(absorb_value.shape, bf16),
                       jax.ShapeDtypeStruct(query_rope.shape, bf16)],
            in_specs=[SMEM] * 4 + [VMEM, HBM, HBM, HBM, HBM, VMEM, HBM, VMEM],
            out_specs=[VMEM] * 5,
            scratch_shapes=[
                *scratch(t),
                pltpu.SemaphoreType.DMA((blocks + 1,)),
                pltpu.SemaphoreType.DMA((2 * PIECES + 2,)),
            ],
            name="attend_first",
            compiler_params=params(20),
            cost_estimate=LONG,
        )(me[None], z[None], prefill_table, prefill_offset, q_nope, in_hbm(query_rope), in_hbm(absorb_key),
          in_hbm(absorb_value), in_hbm(cache_latent), padded_rope,
          in_hbm(new_latent), new_rope.T)

    def attend(n, held, after, brought=None):
        keys, wk, wv, q_rope = held
        t = sizes[n]
        args = [q_nope, q_rope, wk, wv, keys]
        specs = [VMEM] * 5
        scratches = scratch(t)
        limit = 20
        static = (starts[n], fresh_of(n), prior)
        if n == len(sizes) - 1:
            brought, spots = brought
            kernel = functools.partial(
                last_kernel, *static, prefill_len, exp_scale, len(after), spots, capacity * block_len)
            args = [me[None]] + args + [
                in_hbm(cache_latent.reshape(pool * block_len, latent)), padded_rope, decode_table.T, decode_length, *brought]
            specs = [SMEM] + specs + [HBM, VMEM, SMEM, SMEM] + [VMEM] * len(brought)
            span = pool * block_len + groups * capacity * block_len + min(LANES, tok_group)
            scratches += [pltpu.VMEM((span, width), bf16), pltpu.SemaphoreType.DMA((PIECES,))]
            limit = 26
        else:
            kernel = functools.partial(later_kernel, *static, exp_scale, len(after))
        return pl.pallas_call(
            kernel,
            out_shape=jax.ShapeDtypeStruct((t, heads * dv), bf16),
            in_specs=specs + [ANY] * len(after),
            out_specs=VMEM,
            scratch_shapes=scratches,
            name="attend",
            compiler_params=params(limit),
            cost_estimate=SHORT if n == len(sizes) - 1 else LONG,
        )(*args, *after)

    def pack(plan, after):
        return pl.pallas_call(
            functools.partial(pack_kernel, len(after), plan),
            out_shape=[jax.ShapeDtypeStruct((len(p) * capacity * block_len, width), bf16) for p in plan],
            in_specs=[SMEM, SMEM, HBM, VMEM] + [ANY] * len(after),
            out_specs=[VMEM] * len(plan),
            scratch_shapes=[pltpu.SemaphoreType.DMA((groups * capacity,))],
            name="pack",
            compiler_params=params(8),
            cost_estimate=COST,
        )(me[None], send_blocks.transpose(0, 2, 1), in_hbm(cache_latent), padded_rope, *after)

    def migrate():
        packed = pack([(lambda g, s=s: lax.rem(g + s, groups),) for s in range(groups)], ())
        return [packed[0]] + [
            lax.ppermute(packed[s], "dp", [(i, (i + s) % groups) for i in range(groups)])
            for s in range(1, groups)
        ], [(s, 0, lambda g, s=s: lax.rem(g + groups - s, groups)) for s in range(groups)]

    w = output_weight
    x0, *held = first_chunk()
    if not on_line:
        outs = []
        brought = migrate()
        for n, t in enumerate(sizes):
            x = attend(n, held, (), brought) if n else x0
            mine = shift_groups(x)
            if groups % 2 == 0:
                mine += [swap_cores(y) for y in mine]
            own, others = project(where, mine, w, (groups - 1,))
            partials = jnp.concatenate([own, others], axis=0).reshape(groups, t, columns)
            outs.append(lax.psum_scatter(partials, "tp", scatter_dimension=0, tiled=False))
        return jnp.concatenate(outs, axis=0)

    def inward(x):
        return lax.ppermute(x, "tp", INWARD)

    def across(x):
        return lax.ppermute(x, "tp", ACROSS)

    def outward(x):
        return lax.ppermute(x, "tp", OUTWARD)

    def gather(x, after):
        came = shift_groups(x)[1]
        return [x, came, swap_cores(x), swap_cores(stack([came], after))]

    t0, t1, t2, t3 = sizes
    apart = [lambda g, k=k: g ^ k for k in range(4)]
    own_blocks, core_blocks, far_blocks = pack([(apart[0],), (apart[1],), (apart[2], apart[3])], ())
    x_blocks = lax.ppermute(far_blocks, "dp", [(i, i ^ 2) for i in range(groups)])
    x1 = attend(1, held, (x0,))
    half = capacity * block_len
    on_blocks = swap_cores(stack([core_blocks, (x_blocks, half)], (x0,)))
    brought = ((own_blocks, x_blocks, on_blocks), [(0, 0, apart[0]), (1, 0, apart[2]), (2, 0, apart[1]), (2, half, apart[3])])
    own0, rest0 = project(where, gather(x0, (x1,)), w, (3,), (), (x1,))
    in0 = inward(rest0)
    x2 = attend(2, held, (own0, on_blocks))
    own1, rest1 = project(where, gather(x1, (x2,)), w, (3,), (), (x2,))
    in1 = inward(rest1)
    to_across0 = add(2 * t0, [(rest0, 0), (in0, 0)], (own1,))
    on0 = across(to_across0)
    x3 = attend(3, held, (to_across0,), brought)
    own2, rest2, near2 = project(where, gather(x2, (x3,)), w, (2, 1), (), (x3,))
    in2 = inward(rest2)
    to_across1 = add(2 * t1, [(rest1, 0), (in1, 0)], (own2, on0))
    on1 = across(to_across1)
    own3, rest3, near = project(
        where, gather(x3, (own2,)), w, (2, 1), (near2,), (to_across1,))
    in3 = inward(rest3)
    to_across2 = add(2 * t2, [(rest2, 0), (in2, 0)], (own3,))
    on2 = across(to_across2)
    near_in = inward(near)
    to_out01 = add_all([(t0, [(rest0, 2 * t0), (on0, 0)]), (t1, [(rest1, 2 * t1), (on1, 0)])],
                       (to_across2,))
    out01 = outward(to_out01)
    to_far = add(t3, [(rest3, 0), (in3, 0)], (to_out01,))
    far_on = across(to_far)
    to_mid = add(t3, [(rest3, t3), (in3, t3)], (to_far,))
    mid_on = across(to_mid)
    done01 = add_all([(t0, [(own0, 0), (in0, 2 * t0), (on0, t0), (out01, 0)]),
                      (t1, [(own1, 0), (in1, 2 * t1), (on1, t1), (out01, t0)])], (to_mid,))
    to_out2 = add(t2, [(near2, 0), (on2, 0)], (done01,))
    out2 = outward(to_out2)
    to_out3 = add(t3, [(near, t2), (far_on, 0)], (to_out2,))
    out3 = outward(to_out3)
    done2 = add(t2, [(own2, 0), (near_in, 0), (on2, t2), (out2, 0)], (to_out3,))
    return finish([done01, done2], [(own3, 0), (near_in, t2), (mid_on, 0), (out3, 0)])


def solution(mesh):
    return jax.shard_map(
        body,
        mesh=mesh,
        in_specs=(
            P(("replica", "dp"), "tp", None),
            P(("replica", "dp"), "tp"),
            P(("replica", "dp"), None),
            P(("replica", "dp"), None),
            P(("replica", "dp"), None, None),
            P(("replica", "dp"), None),
            P("tp", None, None),
            P("tp", None, None),
            P("tp", "dp"),
            P(("replica", "dp"), None, None),
            P(("replica", "dp"), None),
            P(("replica", "dp")),
            P(("replica", "dp"), None),
            P(("replica", "dp")),
        ),
        out_specs=P(("replica", "tp"), "dp"),
        check_vma=False,
    )
```

```python
import functools

import jax
import jax.numpy as jnp
import numpy as np
from jax import lax
from jax.experimental import pallas as pl
from jax.experimental.pallas import tpu as pltpu
from jax.sharding import PartitionSpec as P

HIDDEN = -1e30
LANES = 128
MIB = 1024 * 1024
PIECES = 4

SMEM = pl.BlockSpec(memory_space=pltpu.SMEM)
VMEM = pl.BlockSpec(memory_space=pltpu.VMEM)
HBM = pl.BlockSpec(memory_space=pltpu.HBM)
ANY = pl.BlockSpec(memory_space=pl.ANY)


def params(mib):
    return pltpu.CompilerParams(vmem_limit_bytes=mib * MIB)


def dot_nt(a, b):
    return lax.dot_general(a, b, (((1,), (1,)), ((), ())), preferred_element_type=jnp.float32)


def dot(a, b):
    return jnp.dot(a, b, preferred_element_type=jnp.float32)


def chunk_sizes(tok_group):
    if tok_group == 256:
        return (48, 80, 80, 48)
    return (tok_group,)


def rope_rows(rope_t):
    rows = jnp.transpose(rope_t.astype(jnp.float32), (1, 0))
    return jnp.concatenate(
        [rows, jnp.zeros((rows.shape[0], LANES - rows.shape[1]), jnp.float32)], axis=1
    ).astype(jnp.bfloat16)


def build_queries(q, q_nope, q_rope, first, wk, ready=None):
    heads = q_nope.shape[0]
    t = q.shape[0] // heads
    latent = wk.shape[2]
    rope_dim = q_rope.shape[1] // heads
    lane = lax.broadcasted_iota(jnp.int32, (t, LANES), 1)
    one = jnp.where(lane == rope_dim, 1.0, 0.0)
    per_tile = LANES // rope_dim
    for h in range(heads):
        pair = q_rope[first:first + t, h // per_tile * LANES:(h // per_tile + 1) * LANES].astype(jnp.float32)
        turn = h % per_tile * rope_dim
        if turn:
            pair = pltpu.roll(pair, LANES - turn, 1)
        q[h * t:(h + 1) * t, latent:] = jnp.where(lane < rope_dim, pair, one).astype(jnp.bfloat16)
    for h in range(heads):
        if ready is not None:
            ready(h)
        q[h * t:(h + 1) * t, :latent] = dot(q_nope[h, first:first + t, :], wk[h]).astype(jnp.bfloat16)


def prefill(q, keys, att, heads, t, first, prior, fresh, exp_scale):
    latent = att.shape[1]
    together = 1
    while together * 2 <= heads and together * 2 * t <= 384:
        together *= 2
    tile = together * t
    token = first + lax.broadcasted_iota(jnp.int32, (t, fresh), 0)
    key_token = lax.broadcasted_iota(jnp.int32, (t, fresh), 1)
    causal = (key_token <= token)[None]
    end = prior + fresh

    def scores_of(i):
        rows = q[i * tile:(i + 1) * tile, :]
        return dot_nt(rows, keys[:prior, :]), dot_nt(rows, keys[prior:end, :])

    steps = heads // together
    ahead = scores_of(0)
    for i in range(steps):
        s_old, s_new = ahead
        if i + 1 < steps:
            ahead = scores_of(i + 1)
        s_new = jnp.where(causal, s_new.reshape(together, t, fresh), HIDDEN).reshape(tile, fresh)
        top = jnp.maximum(jnp.max(s_old, axis=1, keepdims=True), jnp.max(s_new, axis=1, keepdims=True))
        p_old = jnp.exp2((s_old - top) * exp_scale)
        p_new = jnp.exp2((s_new - top) * exp_scale)
        total = jnp.sum(p_old, axis=1, keepdims=True) + jnp.sum(p_new, axis=1, keepdims=True)
        mixed = dot(p_old.astype(jnp.bfloat16), keys[:prior, :latent]) + dot(
            p_new.astype(jnp.bfloat16), keys[prior:end, :latent])
        att[i * tile:(i + 1) * tile, :] = (mixed / total).astype(jnp.bfloat16)


def head_outputs(out, att, wv, t):
    heads, _, dv = wv.shape
    for h in range(heads):
        out[:, h * dv:(h + 1) * dv] = dot(att[h * t:(h + 1) * t, :], wv[h]).astype(jnp.bfloat16)


def pieces(source, target, sems, first):
    size = source.shape[0] // PIECES
    return [pltpu.make_async_copy(source.at[pl.ds(i * size, size)], target.at[pl.ds(i * size, size)],
                                  sems.at[first + i]) for i in range(PIECES)]


def first_kernel(fresh, exp_scale, me, z, table, offset, q_nope, q_rope_hbm, wk_hbm, wv_hbm, cache_latent,
                 cache_rope, new_latent, new_rope_t, out, keys, wk, wv, q_rope, q, att, sems, wsems):
    heads = q_nope.shape[0]
    t = out.shape[0]
    block_len, latent = cache_latent.shape[1:]
    rope_dim = new_rope_t.shape[0]
    blocks = table.shape[1]
    prior = blocks * block_len
    tok_group = new_latent.shape[0]

    rope_copies = [pltpu.make_async_copy(
        q_rope_hbm.at[pl.ds(at, size)], q_rope.at[pl.ds(at, size)], wsems.at[n])
        for n, (at, size) in enumerate(((0, t), (t, tok_group - t))) if size]
    wk_copies = pieces(wk_hbm, wk, wsems, 2)
    later = pieces(wv_hbm, wv, wsems, 2 + PIECES) + rope_copies[1:]
    for c in wk_copies + rope_copies[:1]:
        c.start()
    copies = []
    for i in range(blocks):
        copies.append(pltpu.make_async_copy(
            cache_latent.at[table[0, i]],
            keys.at[pl.ds(i * block_len, block_len), pl.ds(0, latent)], sems.at[i]))
    copies.append(pltpu.make_async_copy(
        new_latent, keys.at[pl.ds(prior, tok_group), pl.ds(0, latent)], sems.at[blocks]))
    for c in copies:
        c.start()

    keys[prior:, latent:] = rope_rows(new_rope_t[...])
    lane = lax.broadcasted_iota(jnp.int32, (block_len, LANES), 1)
    pos = lax.broadcasted_iota(jnp.int32, (block_len, LANES), 0)
    for i in range(blocks):
        hide = jnp.where((lane == rope_dim) & (pos >= offset[0] - i * block_len), HIDDEN, 0.0)
        rope = cache_rope[table[0, i]].astype(jnp.float32) + hide
        keys[i * block_len:(i + 1) * block_len, latent:] = rope.astype(jnp.bfloat16)

    rope_copies[0].wait()

    def ready(h):
        if h * PIECES % heads == 0:
            wk_copies[h * PIECES // heads].wait()

    build_queries(q, q_nope, q_rope, 0, wk, ready)
    for c in copies:
        c.wait()
    for c in later:
        c.start()
    prefill(q, keys, att, heads, t, 0, prior, fresh, exp_scale)
    for c in later:
        c.wait()
    head_outputs(out, att, wv, t)


def pack_kernel(n_after, plan, me, ids, cache_latent, cache_rope, *rest):
    outs, sems = rest[n_after:-1], rest[-1]
    block_len, latent = cache_latent.shape[1:]
    copies = []
    places = []
    for out, targets in zip(outs, plan):
        row = 0
        for target in targets:
            to = target(me[0])
            for k in range(ids.shape[1]):
                places.append((out, row, ids[0, k, to]))
                row += block_len
    for n, (out, row, b) in enumerate(places):
        copies.append(pltpu.make_async_copy(
            cache_latent.at[b], out.at[pl.ds(row, block_len), pl.ds(0, latent)], sems.at[n]))
        copies[-1].start()
    for out, row, b in places:
        out[row:row + block_len, latent:] = cache_rope[b]
    for c in copies:
        c.wait()


def later_kernel(first, fresh, prior, exp_scale, n_after, q_nope, q_rope, wk, wv, keys, *rest):
    out, q, att = rest[n_after:]
    heads = q_nope.shape[0]
    t = out.shape[0]
    build_queries(q, q_nope, q_rope, first, wk)
    prefill(q, keys, att, heads, t, first, prior, fresh, exp_scale)
    head_outputs(out, att, wv, t)


def last_kernel(first, fresh, prior, prefill_len, exp_scale, n_after, spots, got, me, q_nope, q_rope, wk, wv, keys,
                flat_latent, cache_rope, decode_table, decode_length, *rest):
    received = rest[:-5 - n_after]
    out, q, att, dkeys, sems = rest[-5:]
    groups = len(spots)
    heads = q_nope.shape[0]
    t = out.shape[0]
    pool, block_len, _ = cache_rope.shape
    latent = flat_latent.shape[1]
    ext = pool * block_len + groups * got
    tail = dkeys.shape[0] - ext
    start = keys.shape[0] - tail
    copies = []
    for i in range(PIECES):
        rows = pl.ds(i * pool * block_len // PIECES, pool * block_len // PIECES)
        copies.append(pltpu.make_async_copy(
            flat_latent.at[rows], dkeys.at[rows, pl.ds(0, latent)], sems.at[i]))
    for c in copies:
        c.start()
    for i in range(pool):
        dkeys[i * block_len:(i + 1) * block_len, latent:] = cache_rope[i]
    for n, row, source in spots:
        at = pl.multiple_of(pool * block_len + source(me[0]) * got, block_len)
        dkeys[pl.ds(at, got), :] = received[n][row:row + got, :]
    dkeys[ext:, :] = keys[start:, :]

    build_queries(q, q_nope, q_rope, first, wk)
    prefill(q, keys, att, heads, t, first, prior, fresh, exp_scale)

    slots, decodes = decode_table.shape
    for c in copies:
        c.wait()
    span = dkeys.shape[0]
    key = lax.broadcasted_iota(jnp.int32, (decodes, span), 1)
    request = lax.broadcasted_iota(jnp.int32, (decodes, span), 0)
    block = key // block_len
    pos = key % block_len
    own_key = key - ext + (start - prior) == request + prefill_len
    count = jnp.where(own_key, 1.0, 0.0)
    row = lax.broadcasted_iota(jnp.int32, (decodes, LANES), 0)

    def column(read):
        value = jnp.zeros((decodes, LANES), jnp.int32)
        for r in range(decodes):
            value = jnp.where(row == r, read(r), value)
        return value[:, :1]

    length = column(lambda r: decode_length[r])
    for m in range(slots):
        hit = (block == column(lambda r: decode_table[m, r])) & (pos + m * block_len < length) & (
            key < ext)
        count = count + jnp.where(hit, 1.0, 0.0)
    count = count[None]
    at = prefill_len - first
    half = heads // 2 if heads % 2 == 0 else heads
    for lo in range(0, heads, half):
        rows = jnp.concatenate(
            [q[h * t + at:h * t + at + decodes, :] for h in range(lo, lo + half)], axis=0)
        s = dot_nt(rows, dkeys[...]).reshape(half, decodes, span)
        s = jnp.where(count > 0.0, s, HIDDEN)
        top = jnp.max(s, axis=2, keepdims=True)
        p = count * jnp.exp2((s - top) * exp_scale)
        total = jnp.sum(p, axis=2, keepdims=True).reshape(half * decodes, 1)
        p = p.reshape(half * decodes, span).astype(jnp.bfloat16)
        mixed = (dot(p, dkeys[:, :latent]) / total).astype(jnp.bfloat16)
        for h in range(lo, lo + half):
            att[h * t + at:h * t + at + decodes, :] = mixed[(h - lo) * decodes:(h - lo + 1) * decodes]
    head_outputs(out, att, wv, t)


COST = pl.CostEstimate(flops=1000, bytes_accessed=1000, transcendentals=0)
LONG = pl.CostEstimate(flops=40_000_000_000, bytes_accessed=1000, transcendentals=0)
SHORT = pl.CostEstimate(flops=6_000_000_000, bytes_accessed=1000, transcendentals=0)


def in_hbm(x):
    return pltpu.with_memory_space_constraint(x, pltpu.HBM)


def project_kernel(n_parts, tails, places, me, z, w, *rest):
    parts, rest, x = rest[:n_parts], rest[n_parts:], rest[-1]
    own, outs = rest[-2 - len(tails)], rest[-1 - len(tails):-1]
    t = own.shape[0]
    if outs[0].shape[0] > tails[0] * t:
        outs[0][tails[0] * t:, :] = rest[0][...]
    for i, part in enumerate(parts):
        place = 0
        for g, row in enumerate(places):
            for p, column in enumerate(row):
                place = jnp.where((me[0] == g) & (z[0] == p), column[i], place)
        x[pl.ds(pl.multiple_of(place * t, t), t), :] = part[...]
    columns = w.shape[1]
    step = 256 if columns % 256 == 0 else columns
    for at in range(0, columns, step):
        y = dot(x[...], w[:, at:at + step]).astype(jnp.bfloat16)
        own[:, at:at + step] = y[:t]
        row = t
        for i, n in enumerate(tails):
            outs[i][:n * t, at:at + step] = y[row:row + n * t]
            row += n * t


def project(where, parts, w, tails, earlier=(), after=()):
    depth, columns = w.shape
    rows = sum(p.shape[0] for p in parts)
    t = rows // (1 + sum(tails))
    sizes = [t] + [n * t for n in tails]
    sizes[1] += sum(e.shape[0] for e in earlier)
    places, me, z = where
    return pl.pallas_call(
        functools.partial(project_kernel, len(parts), tails, places),
        out_shape=[jax.ShapeDtypeStruct((n, columns), jnp.bfloat16) for n in sizes],
        in_specs=[SMEM, SMEM, VMEM] + [VMEM] * (len(parts) + len(earlier)) + [ANY] * len(after),
        out_specs=[VMEM] * len(sizes),
        scratch_shapes=[pltpu.VMEM((rows, depth), jnp.bfloat16)],
        name="project",
        compiler_params=params(12),
        cost_estimate=COST,
    )(me[None], z[None], w, *parts, *earlier, *after)


def add_kernel(sums, *refs):
    out = refs[-1]
    row = i = 0
    for rows, spans in sums:
        total = None
        for at in spans:
            x = refs[i][at:at + rows, :].astype(jnp.float32)
            total = x if total is None else total + x
            i += 1
        out[row:row + rows, :] = total.astype(jnp.bfloat16)
        row += rows


def add_all(sums, after=()):
    terms = [x for _, parts in sums for x, _ in parts]
    return pl.pallas_call(
        functools.partial(add_kernel, [(rows, [at for _, at in parts]) for rows, parts in sums]),
        out_shape=jax.ShapeDtypeStruct((sum(rows for rows, _ in sums), terms[0].shape[1]), jnp.bfloat16),
        in_specs=[VMEM] * len(terms) + [ANY] * len(after),
        out_specs=VMEM,
        name="add",
        compiler_params=params(8),
        cost_estimate=COST,
    )(*terms, *after)


def add(rows, terms, after=()):
    return add_all([(rows, terms)], after)


def finish_kernel(n_ready, spans, *refs):
    out = refs[-1]
    row = 0
    for ref in refs[:n_ready]:
        out[row:row + ref.shape[0], :] = ref[...]
        row += ref.shape[0]
    add_kernel([(out.shape[0] - row, spans)], *refs[n_ready:-1], out.at[row:, :])


def finish(ready, terms):
    rows = sum(r.shape[0] for r in ready) + terms[0][0].shape[0]
    return pl.pallas_call(
        functools.partial(finish_kernel, len(ready), [at for _, at in terms]),
        out_shape=jax.ShapeDtypeStruct((rows, terms[0][0].shape[1]), jnp.bfloat16),
        in_specs=[VMEM] * (len(ready) + len(terms)),
        out_specs=VMEM,
        name="finish",
        compiler_params=params(8),
        cost_estimate=COST,
    )(*ready, *[x for x, _ in terms])


def gathered_ids(groups, me):
    if groups % 2:
        return [(me - s) % groups for s in range(groups)]
    return [(who - 2 * s) % groups for who in (me, me ^ 1) for s in range(groups // 2)]


def shift_groups(x):
    groups = lax.axis_size("dp")
    step = 1 if groups % 2 else 2
    return [x] + [lax.ppermute(x, "dp", [(i, (i + s) % groups) for i in range(groups)])
                  for s in range(step, groups, step)]


def stack_kernel(firsts, *refs):
    out, at = refs[-1], 0
    for ref, first in zip(refs, firsts):
        n = ref.shape[0] - first
        out[at:at + n, :] = ref[first:, :]
        at += n


def stack(parts, after=()):
    parts = [p if isinstance(p, tuple) else (p, 0) for p in parts]
    rows = sum(p.shape[0] - first for p, first in parts)
    return pl.pallas_call(
        functools.partial(stack_kernel, [first for _, first in parts]),
        out_shape=jax.ShapeDtypeStruct((rows, parts[0][0].shape[1]), jnp.bfloat16),
        in_specs=[VMEM] * len(parts) + [ANY] * len(after),
        out_specs=VMEM,
        name="stack",
        compiler_params=params(4),
        cost_estimate=COST,
    )(*[p for p, _ in parts], *after)


def swap_cores(x):
    return lax.ppermute(x, "dp", [(i, i ^ 1) for i in range(lax.axis_size("dp"))])


LINE_ORDER = ((0, 3, 2, 1), (1, 3, 2, 0), (2, 0, 1, 3), (3, 0, 1, 2))
INWARD = [(0, 1), (3, 2)]
ACROSS = [(1, 2), (2, 1)]
OUTWARD = [(1, 0), (2, 3)]


def body(
    query_nope,
    query_rope,
    new_latent,
    new_rope,
    cache_latent,
    cache_rope,
    absorb_key,
    absorb_value,
    output_weight,
    send_blocks,
    prefill_table,
    prefill_offset,
    decode_table,
    decode_length,
):
    tok_group, heads, nope_dim = query_nope.shape
    pool, block_len, latent = cache_latent.shape
    rope_dim = new_rope.shape[1]
    capacity = send_blocks.shape[2]
    groups = lax.axis_size("dp")
    decodes = decode_length.shape[0]
    prefill_len = tok_group - decodes
    dv = absorb_value.shape[2]
    columns = output_weight.shape[1]
    exp_scale = float((nope_dim + rope_dim) ** (-0.5) * 1.4426950408889634)
    blocks = prefill_table.shape[1]
    prior = blocks * block_len
    width = latent + LANES
    on_line = lax.axis_size("tp") == 4 and groups == 4
    bf16 = jnp.bfloat16

    me = lax.axis_index("dp")
    z = lax.axis_index("tp")
    places = []
    for g in range(groups):
        came = gathered_ids(groups, g)
        if on_line:
            places.append([[order.index(k) for k in came] for order in LINE_ORDER])
        else:
            places.append([came])
    where = (places, me, z if on_line else z * 0)

    padded_rope = jnp.pad(
        cache_rope.reshape(pool, block_len, rope_dim), ((0, 0), (0, 0), (0, LANES - rope_dim)))
    q_nope = query_nope.transpose(1, 0, 2)
    sizes = chunk_sizes(tok_group)
    starts = [sum(sizes[:i]) for i in range(len(sizes))]

    def fresh_of(n):
        seen = min(starts[n] + sizes[n], prefill_len)
        return min(-(-seen // LANES) * LANES, tok_group)

    def scratch(t):
        return [pltpu.VMEM((heads * t, width), bf16), pltpu.VMEM((heads * t, latent), bf16)]

    def first_chunk():
        t = sizes[0]
        return pl.pallas_call(
            functools.partial(first_kernel, fresh_of(0), exp_scale),
            out_shape=[jax.ShapeDtypeStruct((t, heads * dv), bf16),
                       jax.ShapeDtypeStruct((prior + tok_group, width), bf16),
                       jax.ShapeDtypeStruct(absorb_key.shape, bf16),
                       jax.ShapeDtypeStruct(absorb_value.shape, bf16),
                       jax.ShapeDtypeStruct(query_rope.shape, bf16)],
            in_specs=[SMEM] * 4 + [VMEM, HBM, HBM, HBM, HBM, VMEM, HBM, VMEM],
            out_specs=[VMEM] * 5,
            scratch_shapes=[
                *scratch(t),
                pltpu.SemaphoreType.DMA((blocks + 1,)),
                pltpu.SemaphoreType.DMA((2 * PIECES + 2,)),
            ],
            name="attend_first",
            compiler_params=params(20),
            cost_estimate=LONG,
        )(me[None], z[None], prefill_table, prefill_offset, q_nope, in_hbm(query_rope), in_hbm(absorb_key),
          in_hbm(absorb_value), in_hbm(cache_latent), padded_rope,
          in_hbm(new_latent), new_rope.T)

    def attend(n, held, after, brought=None):
        keys, wk, wv, q_rope = held
        t = sizes[n]
        args = [q_nope, q_rope, wk, wv, keys]
        specs = [VMEM] * 5
        scratches = scratch(t)
        limit = 20
        static = (starts[n], fresh_of(n), prior)
        if n == len(sizes) - 1:
            brought, spots = brought
            kernel = functools.partial(
                last_kernel, *static, prefill_len, exp_scale, len(after), spots, capacity * block_len)
            args = [me[None]] + args + [
                in_hbm(cache_latent.reshape(pool * block_len, latent)), padded_rope, decode_table.T, decode_length, *brought]
            specs = [SMEM] + specs + [HBM, VMEM, SMEM, SMEM] + [VMEM] * len(brought)
            span = pool * block_len + groups * capacity * block_len + min(LANES, tok_group)
            scratches += [pltpu.VMEM((span, width), bf16), pltpu.SemaphoreType.DMA((PIECES,))]
            limit = 26
        else:
            kernel = functools.partial(later_kernel, *static, exp_scale, len(after))
        return pl.pallas_call(
            kernel,
            out_shape=jax.ShapeDtypeStruct((t, heads * dv), bf16),
            in_specs=specs + [ANY] * len(after),
            out_specs=VMEM,
            scratch_shapes=scratches,
            name="attend",
            compiler_params=params(limit),
            cost_estimate=SHORT if n == len(sizes) - 1 else LONG,
        )(*args, *after)

    def pack(plan, after):
        return pl.pallas_call(
            functools.partial(pack_kernel, len(after), plan),
            out_shape=[jax.ShapeDtypeStruct((len(p) * capacity * block_len, width), bf16) for p in plan],
            in_specs=[SMEM, SMEM, HBM, VMEM] + [ANY] * len(after),
            out_specs=[VMEM] * len(plan),
            scratch_shapes=[pltpu.SemaphoreType.DMA((groups * capacity,))],
            name="pack",
            compiler_params=params(8),
            cost_estimate=COST,
        )(me[None], send_blocks.transpose(0, 2, 1), in_hbm(cache_latent), padded_rope, *after)

    def migrate():
        packed = pack([(lambda g, s=s: lax.rem(g + s, groups),) for s in range(groups)], ())
        return [packed[0]] + [
            lax.ppermute(packed[s], "dp", [(i, (i + s) % groups) for i in range(groups)])
            for s in range(1, groups)
        ], [(s, 0, lambda g, s=s: lax.rem(g + groups - s, groups)) for s in range(groups)]

    w = output_weight
    x0, *held = first_chunk()
    if not on_line:
        outs = []
        brought = migrate()
        for n, t in enumerate(sizes):
            x = attend(n, held, (), brought) if n else x0
            mine = shift_groups(x)
            if groups % 2 == 0:
                mine += [swap_cores(y) for y in mine]
            own, others = project(where, mine, w, (groups - 1,))
            partials = jnp.concatenate([own, others], axis=0).reshape(groups, t, columns)
            outs.append(lax.psum_scatter(partials, "tp", scatter_dimension=0, tiled=False))
        return jnp.concatenate(outs, axis=0)

    def inward(x):
        return lax.ppermute(x, "tp", INWARD)

    def across(x):
        return lax.ppermute(x, "tp", ACROSS)

    def outward(x):
        return lax.ppermute(x, "tp", OUTWARD)

    def gather(x, after):
        came = shift_groups(x)[1]
        return [x, came, swap_cores(x), swap_cores(stack([came], after))]

    t0, t1, t2, t3 = sizes
    apart = [lambda g, k=k: g ^ k for k in range(4)]
    own_blocks, core_blocks, far_blocks = pack(
        [(apart[0],), (apart[1],), (apart[2], apart[3])], (x0,))
    x1 = attend(1, held, (own_blocks,))
    half = capacity * block_len
    x_blocks = lax.ppermute(stack([far_blocks], (x1,)), "dp", [(i, i ^ 2) for i in range(groups)])
    own0, rest0 = project(where, gather(x0, (x1,)), w, (3,), (), (x1,))
    in0 = inward(rest0)
    x2 = attend(2, held, (own0,))
    on_blocks = swap_cores(stack([core_blocks, (x_blocks, half)], (x2,)))
    brought = ((own_blocks, x_blocks, on_blocks), [
        (0, 0, apart[0]), (1, 0, apart[2]), (2, 0, apart[1]), (2, half, apart[3])])
    own1, rest1 = project(where, gather(x1, (x2,)), w, (3,), (), (x2,))
    in1 = inward(rest1)
    to_across0 = add(2 * t0, [(rest0, 0), (in0, 0)], (own1,))
    on0 = across(to_across0)
    x3 = attend(3, held, (to_across0,), brought)
    own2, rest2, near2 = project(where, gather(x2, (x3,)), w, (2, 1), (), (x3,))
    in2 = inward(rest2)
    to_across1 = add(2 * t1, [(rest1, 0), (in1, 0)], (own2, on0))
    on1 = across(to_across1)
    own3, rest3, near3 = project(
        where, gather(x3, (own2,)), w, (2, 1), (near2,), (to_across1,))
    in3 = inward(rest3)
    to_across2 = add(2 * t2, [(rest2, 0), (in2, 0)], (own3,))
    on2 = across(to_across2)
    to_out01 = add_all([(t0, [(rest0, 2 * t0), (on0, 0)]), (t1, [(rest1, 2 * t1), (on1, 0)])],
                       (to_across2,))
    out01 = outward(to_out01)
    to_far = add(t3, [(rest3, 0), (in3, 0)], (to_out01,))
    far_on = across(to_far)
    near_in = inward(stack([near3], (to_far,)))
    to_mid = add(t3, [(rest3, t3), (in3, t3)], (to_far,))
    mid_on = across(to_mid)
    done01 = add_all([(t0, [(own0, 0), (in0, 2 * t0), (on0, t0), (out01, 0)]),
                      (t1, [(own1, 0), (in1, 2 * t1), (on1, t1), (out01, t0)])], (to_mid,))
    to_out2 = add(t2, [(near2, 0), (on2, 0)], (done01,))
    out2 = outward(to_out2)
    to_out3 = add(t3, [(near3, 0), (far_on, 0)], (to_out2, near_in))
    out3 = outward(to_out3)
    done2 = add(t2, [(own2, 0), (in3, 2 * t3), (on2, t2), (out2, 0)], (to_out3,))
    return finish([done01, done2], [(own3, 0), (near_in, 0), (mid_on, 0), (out3, 0)])


def solution(mesh):
    return jax.shard_map(
        body,
        mesh=mesh,
        in_specs=(
            P(("replica", "dp"), "tp", None),
            P(("replica", "dp"), "tp"),
            P(("replica", "dp"), None),
            P(("replica", "dp"), None),
            P(("replica", "dp"), None, None),
            P(("replica", "dp"), None),
            P("tp", None, None),
            P("tp", None, None),
            P("tp", "dp"),
            P(("replica", "dp"), None, None),
            P(("replica", "dp"), None),
            P(("replica", "dp")),
            P(("replica", "dp"), None),
            P(("replica", "dp")),
        ),
        out_specs=P(("replica", "tp"), "dp"),
        check_vma=False,
    )
```

```python
import functools

import jax
import jax.numpy as jnp
import numpy as np
from jax import lax
from jax.experimental import pallas as pl
from jax.experimental.pallas import tpu as pltpu
from jax.sharding import PartitionSpec as P

HIDDEN = -1e30
LANES = 128
MIB = 1024 * 1024
PIECES = 4

SMEM = pl.BlockSpec(memory_space=pltpu.SMEM)
VMEM = pl.BlockSpec(memory_space=pltpu.VMEM)
HBM = pl.BlockSpec(memory_space=pltpu.HBM)
ANY = pl.BlockSpec(memory_space=pl.ANY)


def params(mib):
    return pltpu.CompilerParams(vmem_limit_bytes=mib * MIB)


def dot_nt(a, b):
    return lax.dot_general(a, b, (((1,), (1,)), ((), ())), preferred_element_type=jnp.float32)


def dot(a, b):
    return jnp.dot(a, b, preferred_element_type=jnp.float32)


def chunk_sizes(tok_group):
    if tok_group == 256:
        return (48, 64, 80, 64)
    return (tok_group,)


def rope_rows(rope_t):
    rows = jnp.transpose(rope_t.astype(jnp.float32), (1, 0))
    return jnp.concatenate(
        [rows, jnp.zeros((rows.shape[0], LANES - rows.shape[1]), jnp.float32)], axis=1
    ).astype(jnp.bfloat16)


def build_queries(q, q_nope, q_rope, first, wk, ready=None):
    heads = q_nope.shape[0]
    t = q.shape[0] // heads
    latent = wk.shape[2]
    rope_dim = q_rope.shape[1] // heads
    lane = lax.broadcasted_iota(jnp.int32, (t, LANES), 1)
    one = jnp.where(lane == rope_dim, 1.0, 0.0)
    per_tile = LANES // rope_dim
    for h in range(heads):
        pair = q_rope[first:first + t, h // per_tile * LANES:(h // per_tile + 1) * LANES].astype(jnp.float32)
        turn = h % per_tile * rope_dim
        if turn:
            pair = pltpu.roll(pair, LANES - turn, 1)
        q[h * t:(h + 1) * t, latent:] = jnp.where(lane < rope_dim, pair, one).astype(jnp.bfloat16)
    for h in range(heads):
        if ready is not None:
            ready(h)
        q[h * t:(h + 1) * t, :latent] = dot(q_nope[h, first:first + t, :], wk[h]).astype(jnp.bfloat16)


def prefill(q, keys, att, heads, t, first, prior, fresh, exp_scale):
    latent = att.shape[1]
    together = 1
    while together * 2 <= heads and together * 2 * t <= 384:
        together *= 2
    tile = together * t
    token = first + lax.broadcasted_iota(jnp.int32, (t, fresh), 0)
    key_token = lax.broadcasted_iota(jnp.int32, (t, fresh), 1)
    causal = (key_token <= token)[None]
    end = prior + fresh

    def scores_of(i):
        rows = q[i * tile:(i + 1) * tile, :]
        return dot_nt(rows, keys[:prior, :]), dot_nt(rows, keys[prior:end, :])

    steps = heads // together
    ahead = scores_of(0)
    for i in range(steps):
        s_old, s_new = ahead
        if i + 1 < steps:
            ahead = scores_of(i + 1)
        s_new = jnp.where(causal, s_new.reshape(together, t, fresh), HIDDEN).reshape(tile, fresh)
        top = jnp.maximum(jnp.max(s_old, axis=1, keepdims=True), jnp.max(s_new, axis=1, keepdims=True))
        p_old = jnp.exp2((s_old - top) * exp_scale)
        p_new = jnp.exp2((s_new - top) * exp_scale)
        total = jnp.sum(p_old, axis=1, keepdims=True) + jnp.sum(p_new, axis=1, keepdims=True)
        mixed = dot(p_old.astype(jnp.bfloat16), keys[:prior, :latent]) + dot(
            p_new.astype(jnp.bfloat16), keys[prior:end, :latent])
        att[i * tile:(i + 1) * tile, :] = (mixed / total).astype(jnp.bfloat16)


def head_outputs(out, att, wv, t):
    heads, _, dv = wv.shape
    for h in range(heads):
        out[:, h * dv:(h + 1) * dv] = dot(att[h * t:(h + 1) * t, :], wv[h]).astype(jnp.bfloat16)


def pieces(source, target, sems, first):
    size = source.shape[0] // PIECES
    return [pltpu.make_async_copy(source.at[pl.ds(i * size, size)], target.at[pl.ds(i * size, size)],
                                  sems.at[first + i]) for i in range(PIECES)]


def first_kernel(fresh, exp_scale, me, z, table, offset, q_nope, q_rope_hbm, wk_hbm, wv_hbm, cache_latent,
                 cache_rope, new_latent, new_rope_t, out, keys, wk, wv, q_rope, q, att, sems, wsems):
    heads = q_nope.shape[0]
    t = out.shape[0]
    block_len, latent = cache_latent.shape[1:]
    rope_dim = new_rope_t.shape[0]
    blocks = table.shape[1]
    prior = blocks * block_len
    tok_group = new_latent.shape[0]

    rope_copies = [pltpu.make_async_copy(
        q_rope_hbm.at[pl.ds(at, size)], q_rope.at[pl.ds(at, size)], wsems.at[n])
        for n, (at, size) in enumerate(((0, t), (t, tok_group - t))) if size]
    wk_copies = pieces(wk_hbm, wk, wsems, 2)
    later = pieces(wv_hbm, wv, wsems, 2 + PIECES) + rope_copies[1:]
    for c in wk_copies + rope_copies[:1]:
        c.start()
    copies = []
    for i in range(blocks):
        copies.append(pltpu.make_async_copy(
            cache_latent.at[table[0, i]],
            keys.at[pl.ds(i * block_len, block_len), pl.ds(0, latent)], sems.at[i]))
    copies.append(pltpu.make_async_copy(
        new_latent, keys.at[pl.ds(prior, tok_group), pl.ds(0, latent)], sems.at[blocks]))
    for c in copies:
        c.start(priority=1)

    keys[prior:, latent:] = rope_rows(new_rope_t[...])
    lane = lax.broadcasted_iota(jnp.int32, (block_len, LANES), 1)
    pos = lax.broadcasted_iota(jnp.int32, (block_len, LANES), 0)
    for i in range(blocks):
        hide = jnp.where((lane == rope_dim) & (pos >= offset[0] - i * block_len), HIDDEN, 0.0)
        rope = cache_rope[table[0, i]].astype(jnp.float32) + hide
        keys[i * block_len:(i + 1) * block_len, latent:] = rope.astype(jnp.bfloat16)

    rope_copies[0].wait()

    def ready(h):
        if h * PIECES % heads == 0:
            wk_copies[h * PIECES // heads].wait()

    build_queries(q, q_nope, q_rope, 0, wk, ready)
    for c in copies:
        c.wait()
    for c in later:
        c.start()
    prefill(q, keys, att, heads, t, 0, prior, fresh, exp_scale)
    for c in later:
        c.wait()
    head_outputs(out, att, wv, t)


def pack_kernel(n_after, plan, me, ids, cache_latent, cache_rope, *rest):
    outs, sems = rest[n_after:-1], rest[-1]
    block_len, latent = cache_latent.shape[1:]
    copies = []
    places = []
    for out, targets in zip(outs, plan):
        row = 0
        for target in targets:
            to = target(me[0])
            for k in range(ids.shape[1]):
                places.append((out, row, ids[0, k, to]))
                row += block_len
    for n, (out, row, b) in enumerate(places):
        copies.append(pltpu.make_async_copy(
            cache_latent.at[b], out.at[pl.ds(row, block_len), pl.ds(0, latent)], sems.at[n]))
        copies[-1].start()
    for out, row, b in places:
        out[row:row + block_len, latent:] = cache_rope[b]
    for c in copies:
        c.wait()


def later_kernel(first, fresh, prior, exp_scale, n_after, q_nope, q_rope, wk, wv, keys, *rest):
    out, q, att = rest[n_after:]
    heads = q_nope.shape[0]
    t = out.shape[0]
    build_queries(q, q_nope, q_rope, first, wk)
    prefill(q, keys, att, heads, t, first, prior, fresh, exp_scale)
    head_outputs(out, att, wv, t)


def last_kernel(first, fresh, prior, prefill_len, exp_scale, n_after, spots, got, me, q_nope, q_rope, wk, wv, keys,
                flat_latent, cache_rope, decode_table, decode_length, *rest):
    received = rest[:-5 - n_after]
    out, q, att, dkeys, sems = rest[-5:]
    groups = len(spots)
    heads = q_nope.shape[0]
    t = out.shape[0]
    pool, block_len, _ = cache_rope.shape
    latent = flat_latent.shape[1]
    ext = pool * block_len + groups * got
    tail = dkeys.shape[0] - ext
    start = keys.shape[0] - tail
    copies = []
    for i in range(PIECES):
        rows = pl.ds(i * pool * block_len // PIECES, pool * block_len // PIECES)
        copies.append(pltpu.make_async_copy(
            flat_latent.at[rows], dkeys.at[rows, pl.ds(0, latent)], sems.at[i]))
    for c in copies:
        c.start()
    for i in range(pool):
        dkeys[i * block_len:(i + 1) * block_len, latent:] = cache_rope[i]
    for n, row, source in spots:
        at = pl.multiple_of(pool * block_len + source(me[0]) * got, block_len)
        dkeys[pl.ds(at, got), :] = received[n][row:row + got, :]
    dkeys[ext:, :] = keys[start:, :]

    build_queries(q, q_nope, q_rope, first, wk)
    prefill(q, keys, att, heads, t, first, prior, fresh, exp_scale)

    slots, decodes = decode_table.shape
    for c in copies:
        c.wait()
    span = dkeys.shape[0]
    key = lax.broadcasted_iota(jnp.int32, (decodes, span), 1)
    request = lax.broadcasted_iota(jnp.int32, (decodes, span), 0)
    block = key // block_len
    pos = key % block_len
    own_key = key - ext + (start - prior) == request + prefill_len
    count = jnp.where(own_key, 1.0, 0.0)
    row = lax.broadcasted_iota(jnp.int32, (decodes, LANES), 0)

    def column(read):
        value = jnp.zeros((decodes, LANES), jnp.int32)
        for r in range(decodes):
            value = jnp.where(row == r, read(r), value)
        return value[:, :1]

    length = column(lambda r: decode_length[r])
    for m in range(slots):
        hit = (block == column(lambda r: decode_table[m, r])) & (pos + m * block_len < length) & (
            key < ext)
        count = count + jnp.where(hit, 1.0, 0.0)
    count = count[None]
    at = prefill_len - first
    half = heads // 2 if heads % 2 == 0 else heads
    for lo in range(0, heads, half):
        rows = jnp.concatenate(
            [q[h * t + at:h * t + at + decodes, :] for h in range(lo, lo + half)], axis=0)
        s = dot_nt(rows, dkeys[...]).reshape(half, decodes, span)
        s = jnp.where(count > 0.0, s, HIDDEN)
        top = jnp.max(s, axis=2, keepdims=True)
        p = count * jnp.exp2((s - top) * exp_scale)
        total = jnp.sum(p, axis=2, keepdims=True).reshape(half * decodes, 1)
        p = p.reshape(half * decodes, span).astype(jnp.bfloat16)
        mixed = (dot(p, dkeys[:, :latent]) / total).astype(jnp.bfloat16)
        for h in range(lo, lo + half):
            att[h * t + at:h * t + at + decodes, :] = mixed[(h - lo) * decodes:(h - lo + 1) * decodes]
    head_outputs(out, att, wv, t)


COST = pl.CostEstimate(flops=1000, bytes_accessed=1000, transcendentals=0)
LONG = pl.CostEstimate(flops=40_000_000_000, bytes_accessed=1000, transcendentals=0)
SHORT = pl.CostEstimate(flops=6_000_000_000, bytes_accessed=1000, transcendentals=0)


def in_hbm(x):
    return pltpu.with_memory_space_constraint(x, pltpu.HBM)


def project_kernel(n_parts, tails, places, me, z, w, *rest):
    parts, rest, x = rest[:n_parts], rest[n_parts:], rest[-1]
    own, outs = rest[-2 - len(tails)], rest[-1 - len(tails):-1]
    t = own.shape[0]
    lead = outs[-1].shape[0] - tails[-1] * t
    if lead:
        outs[-1][:lead, :] = rest[0][...]
    for i, part in enumerate(parts):
        place = 0
        for g, row in enumerate(places):
            for p, column in enumerate(row):
                place = jnp.where((me[0] == g) & (z[0] == p), column[i], place)
        x[pl.ds(pl.multiple_of(place * t, t), t), :] = part[...]
    columns = w.shape[1]
    step = 256 if columns % 256 == 0 else columns
    for at in range(0, columns, step):
        y = dot(x[...], w[:, at:at + step]).astype(jnp.bfloat16)
        own[:, at:at + step] = y[:t]
        row = t
        for i, n in enumerate(tails):
            skip = lead if i == len(tails) - 1 else 0
            outs[i][skip:skip + n * t, at:at + step] = y[row:row + n * t]
            row += n * t


def project(where, parts, w, tails, earlier=(), after=()):
    depth, columns = w.shape
    rows = sum(p.shape[0] for p in parts)
    t = rows // (1 + sum(tails))
    sizes = [t] + [n * t for n in tails]
    sizes[-1] += sum(e.shape[0] for e in earlier)
    places, me, z = where
    return pl.pallas_call(
        functools.partial(project_kernel, len(parts), tails, places),
        out_shape=[jax.ShapeDtypeStruct((n, columns), jnp.bfloat16) for n in sizes],
        in_specs=[SMEM, SMEM, VMEM] + [VMEM] * (len(parts) + len(earlier)) + [ANY] * len(after),
        out_specs=[VMEM] * len(sizes),
        scratch_shapes=[pltpu.VMEM((rows, depth), jnp.bfloat16)],
        name="project",
        compiler_params=params(12),
        cost_estimate=COST,
    )(me[None], z[None], w, *parts, *earlier, *after)


def add_kernel(sums, *refs):
    out = refs[-1]
    row = i = 0
    for rows, spans in sums:
        total = None
        for at in spans:
            x = refs[i][at:at + rows, :].astype(jnp.float32)
            total = x if total is None else total + x
            i += 1
        out[row:row + rows, :] = total.astype(jnp.bfloat16)
        row += rows


def add_all(sums, after=()):
    terms = [x for _, parts in sums for x, _ in parts]
    return pl.pallas_call(
        functools.partial(add_kernel, [(rows, [at for _, at in parts]) for rows, parts in sums]),
        out_shape=jax.ShapeDtypeStruct((sum(rows for rows, _ in sums), terms[0].shape[1]), jnp.bfloat16),
        in_specs=[VMEM] * len(terms) + [ANY] * len(after),
        out_specs=VMEM,
        name="add",
        compiler_params=params(8),
        cost_estimate=COST,
    )(*terms, *after)


def add(rows, terms, after=()):
    return add_all([(rows, terms)], after)


def finish_kernel(n_ready, spans, *refs):
    out = refs[-1]
    row = 0
    for ref in refs[:n_ready]:
        out[row:row + ref.shape[0], :] = ref[...]
        row += ref.shape[0]
    add_kernel([(out.shape[0] - row, spans)], *refs[n_ready:-1], out.at[row:, :])


def finish(ready, terms):
    rows = sum(r.shape[0] for r in ready) + terms[0][0].shape[0]
    return pl.pallas_call(
        functools.partial(finish_kernel, len(ready), [at for _, at in terms]),
        out_shape=jax.ShapeDtypeStruct((rows, terms[0][0].shape[1]), jnp.bfloat16),
        in_specs=[VMEM] * (len(ready) + len(terms)),
        out_specs=VMEM,
        name="finish",
        compiler_params=params(8),
        cost_estimate=COST,
    )(*ready, *[x for x, _ in terms])


def gathered_ids(groups, me):
    if groups % 2:
        return [(me - s) % groups for s in range(groups)]
    return [(who - 2 * s) % groups for who in (me, me ^ 1) for s in range(groups // 2)]


def shift_groups(x):
    groups = lax.axis_size("dp")
    step = 1 if groups % 2 else 2
    return [x] + [lax.ppermute(x, "dp", [(i, (i + s) % groups) for i in range(groups)])
                  for s in range(step, groups, step)]


def stack_kernel(firsts, *refs):
    out, at = refs[-1], 0
    for ref, first in zip(refs, firsts):
        n = ref.shape[0] - first
        out[at:at + n, :] = ref[first:, :]
        at += n


def stack(parts, after=()):
    parts = [p if isinstance(p, tuple) else (p, 0) for p in parts]
    rows = sum(p.shape[0] - first for p, first in parts)
    return pl.pallas_call(
        functools.partial(stack_kernel, [first for _, first in parts]),
        out_shape=jax.ShapeDtypeStruct((rows, parts[0][0].shape[1]), jnp.bfloat16),
        in_specs=[VMEM] * len(parts) + [ANY] * len(after),
        out_specs=VMEM,
        name="stack",
        compiler_params=params(4),
        cost_estimate=COST,
    )(*[p for p, _ in parts], *after)


def swap_cores(x):
    return lax.ppermute(x, "dp", [(i, i ^ 1) for i in range(lax.axis_size("dp"))])


LINE_ORDER = ((0, 3, 2, 1), (1, 3, 2, 0), (2, 0, 1, 3), (3, 0, 1, 2))
INWARD = [(0, 1), (3, 2)]
ACROSS = [(1, 2), (2, 1)]
OUTWARD = [(1, 0), (2, 3)]


def body(
    query_nope,
    query_rope,
    new_latent,
    new_rope,
    cache_latent,
    cache_rope,
    absorb_key,
    absorb_value,
    output_weight,
    send_blocks,
    prefill_table,
    prefill_offset,
    decode_table,
    decode_length,
):
    tok_group, heads, nope_dim = query_nope.shape
    pool, block_len, latent = cache_latent.shape
    rope_dim = new_rope.shape[1]
    capacity = send_blocks.shape[2]
    groups = lax.axis_size("dp")
    decodes = decode_length.shape[0]
    prefill_len = tok_group - decodes
    dv = absorb_value.shape[2]
    columns = output_weight.shape[1]
    exp_scale = float((nope_dim + rope_dim) ** (-0.5) * 1.4426950408889634)
    blocks = prefill_table.shape[1]
    prior = blocks * block_len
    width = latent + LANES
    on_line = lax.axis_size("tp") == 4 and groups == 4
    bf16 = jnp.bfloat16

    me = lax.axis_index("dp")
    z = lax.axis_index("tp")
    places = []
    for g in range(groups):
        came = gathered_ids(groups, g)
        if on_line:
            places.append([[order.index(k) for k in came] for order in LINE_ORDER])
        else:
            places.append([came])
    where = (places, me, z if on_line else z * 0)

    padded_rope = jnp.pad(
        cache_rope.reshape(pool, block_len, rope_dim), ((0, 0), (0, 0), (0, LANES - rope_dim)))
    q_nope = query_nope.transpose(1, 0, 2)
    sizes = chunk_sizes(tok_group)
    starts = [sum(sizes[:i]) for i in range(len(sizes))]

    def fresh_of(n):
        seen = min(starts[n] + sizes[n], prefill_len)
        return min(-(-seen // LANES) * LANES, tok_group)

    def scratch(t):
        return [pltpu.VMEM((heads * t, width), bf16), pltpu.VMEM((heads * t, latent), bf16)]

    def first_chunk():
        t = sizes[0]
        return pl.pallas_call(
            functools.partial(first_kernel, fresh_of(0), exp_scale),
            out_shape=[jax.ShapeDtypeStruct((t, heads * dv), bf16),
                       jax.ShapeDtypeStruct((prior + tok_group, width), bf16),
                       jax.ShapeDtypeStruct(absorb_key.shape, bf16),
                       jax.ShapeDtypeStruct(absorb_value.shape, bf16),
                       jax.ShapeDtypeStruct(query_rope.shape, bf16)],
            in_specs=[SMEM] * 4 + [VMEM, HBM, HBM, HBM, HBM, VMEM, HBM, VMEM],
            out_specs=[VMEM] * 5,
            scratch_shapes=[
                *scratch(t),
                pltpu.SemaphoreType.DMA((blocks + 1,)),
                pltpu.SemaphoreType.DMA((2 * PIECES + 2,)),
            ],
            name="attend_first",
            compiler_params=params(20),
            cost_estimate=LONG,
        )(me[None], z[None], prefill_table, prefill_offset, q_nope, in_hbm(query_rope), in_hbm(absorb_key),
          in_hbm(absorb_value), in_hbm(cache_latent), padded_rope,
          in_hbm(new_latent), new_rope.T)

    def attend(n, held, after, brought=None):
        keys, wk, wv, q_rope = held
        t = sizes[n]
        args = [q_nope, q_rope, wk, wv, keys]
        specs = [VMEM] * 5
        scratches = scratch(t)
        limit = 20
        static = (starts[n], fresh_of(n), prior)
        if n == len(sizes) - 1:
            brought, spots = brought
            kernel = functools.partial(
                last_kernel, *static, prefill_len, exp_scale, len(after), spots, capacity * block_len)
            args = [me[None]] + args + [
                in_hbm(cache_latent.reshape(pool * block_len, latent)), padded_rope, decode_table.T, decode_length, *brought]
            specs = [SMEM] + specs + [HBM, VMEM, SMEM, SMEM] + [VMEM] * len(brought)
            span = pool * block_len + groups * capacity * block_len + min(LANES, tok_group)
            scratches += [pltpu.VMEM((span, width), bf16), pltpu.SemaphoreType.DMA((PIECES,))]
            limit = 26
        else:
            kernel = functools.partial(later_kernel, *static, exp_scale, len(after))
        return pl.pallas_call(
            kernel,
            out_shape=jax.ShapeDtypeStruct((t, heads * dv), bf16),
            in_specs=specs + [ANY] * len(after),
            out_specs=VMEM,
            scratch_shapes=scratches,
            name="attend",
            compiler_params=params(limit),
            cost_estimate=SHORT if n == len(sizes) - 1 else LONG,
        )(*args, *after)

    def pack(plan, after):
        return pl.pallas_call(
            functools.partial(pack_kernel, len(after), plan),
            out_shape=[jax.ShapeDtypeStruct((len(p) * capacity * block_len, width), bf16) for p in plan],
            in_specs=[SMEM, SMEM, HBM, VMEM] + [ANY] * len(after),
            out_specs=[VMEM] * len(plan),
            scratch_shapes=[pltpu.SemaphoreType.DMA((groups * capacity,))],
            name="pack",
            compiler_params=params(8),
            cost_estimate=COST,
        )(me[None], send_blocks.transpose(0, 2, 1), in_hbm(cache_latent), padded_rope, *after)

    def migrate():
        packed = pack([(lambda g, s=s: lax.rem(g + s, groups),) for s in range(groups)], ())
        return [packed[0]] + [
            lax.ppermute(packed[s], "dp", [(i, (i + s) % groups) for i in range(groups)])
            for s in range(1, groups)
        ], [(s, 0, lambda g, s=s: lax.rem(g + groups - s, groups)) for s in range(groups)]

    w = output_weight
    x0, *held = first_chunk()
    if not on_line:
        outs = []
        brought = migrate()
        for n, t in enumerate(sizes):
            x = attend(n, held, (), brought) if n else x0
            mine = shift_groups(x)
            if groups % 2 == 0:
                mine += [swap_cores(y) for y in mine]
            own, others = project(where, mine, w, (groups - 1,))
            partials = jnp.concatenate([own, others], axis=0).reshape(groups, t, columns)
            outs.append(lax.psum_scatter(partials, "tp", scatter_dimension=0, tiled=False))
        return jnp.concatenate(outs, axis=0)

    def inward(x):
        return lax.ppermute(x, "tp", INWARD)

    def across(x):
        return lax.ppermute(x, "tp", ACROSS)

    def outward(x):
        return lax.ppermute(x, "tp", OUTWARD)

    def gather(x, after):
        came = shift_groups(x)[1]
        return [x, came, swap_cores(x), swap_cores(stack([came], after))]

    t0, t1, t2, t3 = sizes
    apart = [lambda g, k=k: g ^ k for k in range(4)]
    own_blocks, core_blocks, far_blocks = pack([(apart[0],), (apart[1],), (apart[2], apart[3])], ())
    x_blocks = lax.ppermute(far_blocks, "dp", [(i, i ^ 2) for i in range(groups)])
    x1 = attend(1, held, (x0,))
    half = capacity * block_len
    on_blocks = swap_cores(stack([core_blocks, (x_blocks, half)], (x0,)))
    brought = ((own_blocks, x_blocks, on_blocks), [(0, 0, apart[0]), (1, 0, apart[2]), (2, 0, apart[1]), (2, half, apart[3])])
    own0, rest0 = project(where, gather(x0, (x1,)), w, (3,), (), (x1,))
    in0 = inward(rest0)
    x2 = attend(2, held, (own0, on_blocks))
    own1, rest1 = project(where, gather(x1, (x2,)), w, (3,), (), (x2,))
    in1 = inward(rest1)
    to_across0 = add(2 * t0, [(rest0, 0), (in0, 0)], (own1,))
    x3 = attend(3, held, (to_across0,), brought)
    own2, rest2, near2 = project(where, gather(x2, (x3,)), w, (2, 1), (), (x3,))
    in2 = inward(rest2)
    on0 = across(stack([to_across0], (own2,)))
    to_across1 = add(2 * t1, [(rest1, 0), (in1, 0)], (own2,))
    on1 = across(to_across1)
    own3, rest3, near = project(
        where, gather(x3, (own2,)), w, (2, 1), (near2,), (to_across1,))
    in3 = inward(rest3)
    to_across2 = add(2 * t2, [(rest2, 0), (in2, 0)], (own3, on0))
    on2 = across(to_across2)
    near_in = inward(near)
    to_out01 = add_all([(t0, [(rest0, 2 * t0), (on0, 0)]), (t1, [(rest1, 2 * t1), (on1, 0)])],
                       (to_across2,))
    out01 = outward(to_out01)
    to_far = add(t3, [(rest3, 0), (in3, 0)], (to_out01,))
    far_on = across(to_far)
    to_mid = add(t3, [(rest3, t3), (in3, t3)], (to_far,))
    mid_on = across(to_mid)
    done01 = add_all([(t0, [(own0, 0), (in0, 2 * t0), (on0, t0), (out01, 0)]),
                      (t1, [(own1, 0), (in1, 2 * t1), (on1, t1), (out01, t0)])], (to_mid,))
    to_out2 = add(t2, [(near2, 0), (on2, 0)], (done01,))
    out2 = outward(to_out2)
    to_out3 = add(t3, [(near, t2), (far_on, 0)], (to_out2,))
    out3 = outward(to_out3)
    done2 = add(t2, [(own2, 0), (near_in, 0), (on2, t2), (out2, 0)], (to_out3,))
    return finish([done01, done2], [(own3, 0), (near_in, t2), (mid_on, 0), (out3, 0)])


def solution(mesh):
    return jax.shard_map(
        body,
        mesh=mesh,
        in_specs=(
            P(("replica", "dp"), "tp", None),
            P(("replica", "dp"), "tp"),
            P(("replica", "dp"), None),
            P(("replica", "dp"), None),
            P(("replica", "dp"), None, None),
            P(("replica", "dp"), None),
            P("tp", None, None),
            P("tp", None, None),
            P("tp", "dp"),
            P(("replica", "dp"), None, None),
            P(("replica", "dp"), None),
            P(("replica", "dp")),
            P(("replica", "dp"), None),
            P(("replica", "dp")),
        ),
        out_specs=P(("replica", "tp"), "dp"),
        check_vma=False,
    )
```

```python
import functools

import jax
import jax.numpy as jnp
import numpy as np
from jax import lax
from jax.experimental import pallas as pl
from jax.experimental.pallas import tpu as pltpu
from jax.sharding import PartitionSpec as P

HIDDEN = -1e30
LANES = 128
MIB = 1024 * 1024
PIECES = 4

SMEM = pl.BlockSpec(memory_space=pltpu.SMEM)
VMEM = pl.BlockSpec(memory_space=pltpu.VMEM)
HBM = pl.BlockSpec(memory_space=pltpu.HBM)
ANY = pl.BlockSpec(memory_space=pl.ANY)


def params(mib):
    return pltpu.CompilerParams(vmem_limit_bytes=mib * MIB)


def dot_nt(a, b):
    return lax.dot_general(a, b, (((1,), (1,)), ((), ())), preferred_element_type=jnp.float32)


def dot(a, b):
    return jnp.dot(a, b, preferred_element_type=jnp.float32)


def chunk_sizes(tok_group):
    if tok_group == 256:
        return (64, 80, 64, 48)
    return (tok_group,)


def rope_rows(rope_t):
    rows = jnp.transpose(rope_t.astype(jnp.float32), (1, 0))
    return jnp.concatenate(
        [rows, jnp.zeros((rows.shape[0], LANES - rows.shape[1]), jnp.float32)], axis=1
    ).astype(jnp.bfloat16)


def build_queries(q, q_nope, q_rope, first, wk, ready=None):
    heads = q_nope.shape[0]
    t = q.shape[0] // heads
    latent = wk.shape[2]
    rope_dim = q_rope.shape[1] // heads
    lane = lax.broadcasted_iota(jnp.int32, (t, LANES), 1)
    one = jnp.where(lane == rope_dim, 1.0, 0.0)
    per_tile = LANES // rope_dim
    for h in range(heads):
        pair = q_rope[first:first + t, h // per_tile * LANES:(h // per_tile + 1) * LANES].astype(jnp.float32)
        turn = h % per_tile * rope_dim
        if turn:
            pair = pltpu.roll(pair, LANES - turn, 1)
        q[h * t:(h + 1) * t, latent:] = jnp.where(lane < rope_dim, pair, one).astype(jnp.bfloat16)
    for h in range(heads):
        if ready is not None:
            ready(h)
        q[h * t:(h + 1) * t, :latent] = dot(q_nope[h, first:first + t, :], wk[h]).astype(jnp.bfloat16)


def prefill(q, keys, att, heads, t, first, prior, fresh, exp_scale):
    latent = att.shape[1]
    together = 1
    while together * 2 <= heads and together * 2 * t <= 384:
        together *= 2
    tile = together * t
    token = first + lax.broadcasted_iota(jnp.int32, (t, fresh), 0)
    key_token = lax.broadcasted_iota(jnp.int32, (t, fresh), 1)
    causal = (key_token <= token)[None]
    end = prior + fresh

    def scores_of(i):
        rows = q[i * tile:(i + 1) * tile, :]
        return dot_nt(rows, keys[:prior, :]), dot_nt(rows, keys[prior:end, :])

    steps = heads // together
    ahead = scores_of(0)
    for i in range(steps):
        s_old, s_new = ahead
        if i + 1 < steps:
            ahead = scores_of(i + 1)
        s_new = jnp.where(causal, s_new.reshape(together, t, fresh), HIDDEN).reshape(tile, fresh)
        top = jnp.maximum(jnp.max(s_old, axis=1, keepdims=True), jnp.max(s_new, axis=1, keepdims=True))
        p_old = jnp.exp2((s_old - top) * exp_scale)
        p_new = jnp.exp2((s_new - top) * exp_scale)
        total = jnp.sum(p_old, axis=1, keepdims=True) + jnp.sum(p_new, axis=1, keepdims=True)
        mixed = dot(p_old.astype(jnp.bfloat16), keys[:prior, :latent]) + dot(
            p_new.astype(jnp.bfloat16), keys[prior:end, :latent])
        att[i * tile:(i + 1) * tile, :] = (mixed / total).astype(jnp.bfloat16)


def head_outputs(out, att, wv, t):
    heads, _, dv = wv.shape
    for h in range(heads):
        out[:, h * dv:(h + 1) * dv] = dot(att[h * t:(h + 1) * t, :], wv[h]).astype(jnp.bfloat16)


def pieces(source, target, sems, first):
    size = source.shape[0] // PIECES
    return [pltpu.make_async_copy(source.at[pl.ds(i * size, size)], target.at[pl.ds(i * size, size)],
                                  sems.at[first + i]) for i in range(PIECES)]


def first_kernel(fresh, exp_scale, me, z, table, offset, q_nope, q_rope_hbm, wk_hbm, wv_hbm, cache_latent,
                 cache_rope, new_latent, new_rope_t, out, keys, wk, wv, q_rope, q, att, sems, wsems):
    heads = q_nope.shape[0]
    t = out.shape[0]
    block_len, latent = cache_latent.shape[1:]
    rope_dim = new_rope_t.shape[0]
    blocks = table.shape[1]
    prior = blocks * block_len
    tok_group = new_latent.shape[0]

    rope_copies = [pltpu.make_async_copy(
        q_rope_hbm.at[pl.ds(at, size)], q_rope.at[pl.ds(at, size)], wsems.at[n])
        for n, (at, size) in enumerate(((0, t), (t, tok_group - t))) if size]
    wk_copies = pieces(wk_hbm, wk, wsems, 2)
    later = pieces(wv_hbm, wv, wsems, 2 + PIECES) + rope_copies[1:]
    for c in wk_copies + rope_copies[:1]:
        c.start()
    copies = []
    for i in range(blocks):
        copies.append(pltpu.make_async_copy(
            cache_latent.at[table[0, i]],
            keys.at[pl.ds(i * block_len, block_len), pl.ds(0, latent)], sems.at[i]))
    copies.append(pltpu.make_async_copy(
        new_latent, keys.at[pl.ds(prior, tok_group), pl.ds(0, latent)], sems.at[blocks]))
    for c in copies:
        c.start(priority=1)

    keys[prior:, latent:] = rope_rows(new_rope_t[...])
    lane = lax.broadcasted_iota(jnp.int32, (block_len, LANES), 1)
    pos = lax.broadcasted_iota(jnp.int32, (block_len, LANES), 0)
    for i in range(blocks):
        hide = jnp.where((lane == rope_dim) & (pos >= offset[0] - i * block_len), HIDDEN, 0.0)
        rope = cache_rope[table[0, i]].astype(jnp.float32) + hide
        keys[i * block_len:(i + 1) * block_len, latent:] = rope.astype(jnp.bfloat16)

    rope_copies[0].wait()

    def ready(h):
        if h * PIECES % heads == 0:
            wk_copies[h * PIECES // heads].wait()

    build_queries(q, q_nope, q_rope, 0, wk, ready)
    for c in copies:
        c.wait()
    for c in later:
        c.start()
    prefill(q, keys, att, heads, t, 0, prior, fresh, exp_scale)
    for c in later:
        c.wait()
    head_outputs(out, att, wv, t)


def pack_kernel(n_after, plan, me, ids, cache_latent, cache_rope, *rest):
    outs, sems = rest[n_after:-1], rest[-1]
    block_len, latent = cache_latent.shape[1:]
    copies = []
    places = []
    for out, targets in zip(outs, plan):
        row = 0
        for target in targets:
            to = target(me[0])
            for k in range(ids.shape[1]):
                places.append((out, row, ids[0, k, to]))
                row += block_len
    for n, (out, row, b) in enumerate(places):
        copies.append(pltpu.make_async_copy(
            cache_latent.at[b], out.at[pl.ds(row, block_len), pl.ds(0, latent)], sems.at[n]))
        copies[-1].start()
    for out, row, b in places:
        out[row:row + block_len, latent:] = cache_rope[b]
    for c in copies:
        c.wait()


def later_kernel(first, fresh, prior, exp_scale, n_after, q_nope, q_rope, wk, wv, keys, *rest):
    out, q, att = rest[n_after:]
    heads = q_nope.shape[0]
    t = out.shape[0]
    build_queries(q, q_nope, q_rope, first, wk)
    prefill(q, keys, att, heads, t, first, prior, fresh, exp_scale)
    head_outputs(out, att, wv, t)


def last_kernel(first, fresh, prior, prefill_len, exp_scale, n_after, spots, got, me, q_nope, q_rope, wk, wv, keys,
                flat_latent, cache_rope, decode_table, decode_length, *rest):
    received = rest[:-5 - n_after]
    out, q, att, dkeys, sems = rest[-5:]
    groups = len(spots)
    heads = q_nope.shape[0]
    t = out.shape[0]
    pool, block_len, _ = cache_rope.shape
    latent = flat_latent.shape[1]
    ext = pool * block_len + groups * got
    tail = dkeys.shape[0] - ext
    start = keys.shape[0] - tail
    copies = []
    for i in range(PIECES):
        rows = pl.ds(i * pool * block_len // PIECES, pool * block_len // PIECES)
        copies.append(pltpu.make_async_copy(
            flat_latent.at[rows], dkeys.at[rows, pl.ds(0, latent)], sems.at[i]))
    for c in copies:
        c.start()
    for i in range(pool):
        dkeys[i * block_len:(i + 1) * block_len, latent:] = cache_rope[i]
    for n, row, source in spots:
        at = pl.multiple_of(pool * block_len + source(me[0]) * got, block_len)
        dkeys[pl.ds(at, got), :] = received[n][row:row + got, :]
    dkeys[ext:, :] = keys[start:, :]

    build_queries(q, q_nope, q_rope, first, wk)
    prefill(q, keys, att, heads, t, first, prior, fresh, exp_scale)

    slots, decodes = decode_table.shape
    for c in copies:
        c.wait()
    span = dkeys.shape[0]
    key = lax.broadcasted_iota(jnp.int32, (decodes, span), 1)
    request = lax.broadcasted_iota(jnp.int32, (decodes, span), 0)
    block = key // block_len
    pos = key % block_len
    own_key = key - ext + (start - prior) == request + prefill_len
    count = jnp.where(own_key, 1.0, 0.0)
    row = lax.broadcasted_iota(jnp.int32, (decodes, LANES), 0)

    def column(read):
        value = jnp.zeros((decodes, LANES), jnp.int32)
        for r in range(decodes):
            value = jnp.where(row == r, read(r), value)
        return value[:, :1]

    length = column(lambda r: decode_length[r])
    for m in range(slots):
        hit = (block == column(lambda r: decode_table[m, r])) & (pos + m * block_len < length) & (
            key < ext)
        count = count + jnp.where(hit, 1.0, 0.0)
    count = count[None]
    at = prefill_len - first
    half = heads // 2 if heads % 2 == 0 else heads
    for lo in range(0, heads, half):
        rows = jnp.concatenate(
            [q[h * t + at:h * t + at + decodes, :] for h in range(lo, lo + half)], axis=0)
        s = dot_nt(rows, dkeys[...]).reshape(half, decodes, span)
        s = jnp.where(count > 0.0, s, HIDDEN)
        top = jnp.max(s, axis=2, keepdims=True)
        p = count * jnp.exp2((s - top) * exp_scale)
        total = jnp.sum(p, axis=2, keepdims=True).reshape(half * decodes, 1)
        p = p.reshape(half * decodes, span).astype(jnp.bfloat16)
        mixed = (dot(p, dkeys[:, :latent]) / total).astype(jnp.bfloat16)
        for h in range(lo, lo + half):
            att[h * t + at:h * t + at + decodes, :] = mixed[(h - lo) * decodes:(h - lo + 1) * decodes]
    head_outputs(out, att, wv, t)


COST = pl.CostEstimate(flops=1000, bytes_accessed=1000, transcendentals=0)
LONG = pl.CostEstimate(flops=40_000_000_000, bytes_accessed=1000, transcendentals=0)
SHORT = pl.CostEstimate(flops=6_000_000_000, bytes_accessed=1000, transcendentals=0)


def in_hbm(x):
    return pltpu.with_memory_space_constraint(x, pltpu.HBM)


def project_kernel(n_parts, tails, places, me, z, w, *rest):
    parts, rest, x = rest[:n_parts], rest[n_parts:], rest[-1]
    own, outs = rest[-2 - len(tails)], rest[-1 - len(tails):-1]
    t = own.shape[0]
    lead = outs[-1].shape[0] - tails[-1] * t
    if lead:
        outs[-1][:lead, :] = rest[0][...]
    for i, part in enumerate(parts):
        place = 0
        for g, row in enumerate(places):
            for p, column in enumerate(row):
                place = jnp.where((me[0] == g) & (z[0] == p), column[i], place)
        x[pl.ds(pl.multiple_of(place * t, t), t), :] = part[...]
    columns = w.shape[1]
    step = 256 if columns % 256 == 0 else columns
    for at in range(0, columns, step):
        y = dot(x[...], w[:, at:at + step]).astype(jnp.bfloat16)
        own[:, at:at + step] = y[:t]
        row = t
        for i, n in enumerate(tails):
            skip = lead if i == len(tails) - 1 else 0
            outs[i][skip:skip + n * t, at:at + step] = y[row:row + n * t]
            row += n * t


def project(where, parts, w, tails, earlier=(), after=()):
    depth, columns = w.shape
    rows = sum(p.shape[0] for p in parts)
    t = rows // (1 + sum(tails))
    sizes = [t] + [n * t for n in tails]
    sizes[-1] += sum(e.shape[0] for e in earlier)
    places, me, z = where
    return pl.pallas_call(
        functools.partial(project_kernel, len(parts), tails, places),
        out_shape=[jax.ShapeDtypeStruct((n, columns), jnp.bfloat16) for n in sizes],
        in_specs=[SMEM, SMEM, VMEM] + [VMEM] * (len(parts) + len(earlier)) + [ANY] * len(after),
        out_specs=[VMEM] * len(sizes),
        scratch_shapes=[pltpu.VMEM((rows, depth), jnp.bfloat16)],
        name="project",
        compiler_params=params(12),
        cost_estimate=COST,
    )(me[None], z[None], w, *parts, *earlier, *after)


def add_kernel(sums, *refs):
    out = refs[-1]
    row = i = 0
    for rows, spans in sums:
        total = None
        for at in spans:
            x = refs[i][at:at + rows, :].astype(jnp.float32)
            total = x if total is None else total + x
            i += 1
        out[row:row + rows, :] = total.astype(jnp.bfloat16)
        row += rows


def add_all(sums, after=()):
    terms = [x for _, parts in sums for x, _ in parts]
    return pl.pallas_call(
        functools.partial(add_kernel, [(rows, [at for _, at in parts]) for rows, parts in sums]),
        out_shape=jax.ShapeDtypeStruct((sum(rows for rows, _ in sums), terms[0].shape[1]), jnp.bfloat16),
        in_specs=[VMEM] * len(terms) + [ANY] * len(after),
        out_specs=VMEM,
        name="add",
        compiler_params=params(8),
        cost_estimate=COST,
    )(*terms, *after)


def add(rows, terms, after=()):
    return add_all([(rows, terms)], after)


def finish_kernel(n_ready, spans, *refs):
    out = refs[-1]
    row = 0
    for ref in refs[:n_ready]:
        out[row:row + ref.shape[0], :] = ref[...]
        row += ref.shape[0]
    add_kernel([(out.shape[0] - row, spans)], *refs[n_ready:-1], out.at[row:, :])


def finish(ready, terms):
    rows = sum(r.shape[0] for r in ready) + terms[0][0].shape[0]
    return pl.pallas_call(
        functools.partial(finish_kernel, len(ready), [at for _, at in terms]),
        out_shape=jax.ShapeDtypeStruct((rows, terms[0][0].shape[1]), jnp.bfloat16),
        in_specs=[VMEM] * (len(ready) + len(terms)),
        out_specs=VMEM,
        name="finish",
        compiler_params=params(8),
        cost_estimate=COST,
    )(*ready, *[x for x, _ in terms])


def gathered_ids(groups, me):
    if groups % 2:
        return [(me - s) % groups for s in range(groups)]
    return [(who - 2 * s) % groups for who in (me, me ^ 1) for s in range(groups // 2)]


def shift_groups(x):
    groups = lax.axis_size("dp")
    step = 1 if groups % 2 else 2
    return [x] + [lax.ppermute(x, "dp", [(i, (i + s) % groups) for i in range(groups)])
                  for s in range(step, groups, step)]


def stack_kernel(firsts, *refs):
    out, at = refs[-1], 0
    for ref, first in zip(refs, firsts):
        n = ref.shape[0] - first
        out[at:at + n, :] = ref[first:, :]
        at += n


def stack(parts, after=()):
    parts = [p if isinstance(p, tuple) else (p, 0) for p in parts]
    rows = sum(p.shape[0] - first for p, first in parts)
    return pl.pallas_call(
        functools.partial(stack_kernel, [first for _, first in parts]),
        out_shape=jax.ShapeDtypeStruct((rows, parts[0][0].shape[1]), jnp.bfloat16),
        in_specs=[VMEM] * len(parts) + [ANY] * len(after),
        out_specs=VMEM,
        name="stack",
        compiler_params=params(4),
        cost_estimate=COST,
    )(*[p for p, _ in parts], *after)


def swap_cores(x):
    return lax.ppermute(x, "dp", [(i, i ^ 1) for i in range(lax.axis_size("dp"))])


LINE_ORDER = ((0, 3, 2, 1), (1, 3, 2, 0), (2, 0, 1, 3), (3, 0, 1, 2))
INWARD = [(0, 1), (3, 2)]
ACROSS = [(1, 2), (2, 1)]
OUTWARD = [(1, 0), (2, 3)]


def body(
    query_nope,
    query_rope,
    new_latent,
    new_rope,
    cache_latent,
    cache_rope,
    absorb_key,
    absorb_value,
    output_weight,
    send_blocks,
    prefill_table,
    prefill_offset,
    decode_table,
    decode_length,
):
    tok_group, heads, nope_dim = query_nope.shape
    pool, block_len, latent = cache_latent.shape
    rope_dim = new_rope.shape[1]
    capacity = send_blocks.shape[2]
    groups = lax.axis_size("dp")
    decodes = decode_length.shape[0]
    prefill_len = tok_group - decodes
    dv = absorb_value.shape[2]
    columns = output_weight.shape[1]
    exp_scale = float((nope_dim + rope_dim) ** (-0.5) * 1.4426950408889634)
    blocks = prefill_table.shape[1]
    prior = blocks * block_len
    width = latent + LANES
    on_line = lax.axis_size("tp") == 4 and groups == 4
    bf16 = jnp.bfloat16

    me = lax.axis_index("dp")
    z = lax.axis_index("tp")
    places = []
    for g in range(groups):
        came = gathered_ids(groups, g)
        if on_line:
            places.append([[order.index(k) for k in came] for order in LINE_ORDER])
        else:
            places.append([came])
    where = (places, me, z if on_line else z * 0)

    padded_rope = jnp.pad(
        cache_rope.reshape(pool, block_len, rope_dim), ((0, 0), (0, 0), (0, LANES - rope_dim)))
    q_nope = query_nope.transpose(1, 0, 2)
    sizes = chunk_sizes(tok_group)
    starts = [sum(sizes[:i]) for i in range(len(sizes))]

    def fresh_of(n):
        seen = min(starts[n] + sizes[n], prefill_len)
        return min(-(-seen // LANES) * LANES, tok_group)

    def scratch(t):
        return [pltpu.VMEM((heads * t, width), bf16), pltpu.VMEM((heads * t, latent), bf16)]

    def first_chunk():
        t = sizes[0]
        return pl.pallas_call(
            functools.partial(first_kernel, fresh_of(0), exp_scale),
            out_shape=[jax.ShapeDtypeStruct((t, heads * dv), bf16),
                       jax.ShapeDtypeStruct((prior + tok_group, width), bf16),
                       jax.ShapeDtypeStruct(absorb_key.shape, bf16),
                       jax.ShapeDtypeStruct(absorb_value.shape, bf16),
                       jax.ShapeDtypeStruct(query_rope.shape, bf16)],
            in_specs=[SMEM] * 4 + [VMEM, HBM, HBM, HBM, HBM, VMEM, HBM, VMEM],
            out_specs=[VMEM] * 5,
            scratch_shapes=[
                *scratch(t),
                pltpu.SemaphoreType.DMA((blocks + 1,)),
                pltpu.SemaphoreType.DMA((2 * PIECES + 2,)),
            ],
            name="attend_first",
            compiler_params=params(20),
            cost_estimate=LONG,
        )(me[None], z[None], prefill_table, prefill_offset, q_nope, in_hbm(query_rope), in_hbm(absorb_key),
          in_hbm(absorb_value), in_hbm(cache_latent), padded_rope,
          in_hbm(new_latent), new_rope.T)

    def attend(n, held, after, brought=None):
        keys, wk, wv, q_rope = held
        t = sizes[n]
        args = [q_nope, q_rope, wk, wv, keys]
        specs = [VMEM] * 5
        scratches = scratch(t)
        limit = 20
        static = (starts[n], fresh_of(n), prior)
        if n == len(sizes) - 1:
            brought, spots = brought
            kernel = functools.partial(
                last_kernel, *static, prefill_len, exp_scale, len(after), spots, capacity * block_len)
            args = [me[None]] + args + [
                in_hbm(cache_latent.reshape(pool * block_len, latent)), padded_rope, decode_table.T, decode_length, *brought]
            specs = [SMEM] + specs + [HBM, VMEM, SMEM, SMEM] + [VMEM] * len(brought)
            span = pool * block_len + groups * capacity * block_len + min(LANES, tok_group)
            scratches += [pltpu.VMEM((span, width), bf16), pltpu.SemaphoreType.DMA((PIECES,))]
            limit = 26
        else:
            kernel = functools.partial(later_kernel, *static, exp_scale, len(after))
        return pl.pallas_call(
            kernel,
            out_shape=jax.ShapeDtypeStruct((t, heads * dv), bf16),
            in_specs=specs + [ANY] * len(after),
            out_specs=VMEM,
            scratch_shapes=scratches,
            name="attend",
            compiler_params=params(limit),
            cost_estimate=SHORT if n == len(sizes) - 1 else LONG,
        )(*args, *after)

    def pack(plan, after):
        return pl.pallas_call(
            functools.partial(pack_kernel, len(after), plan),
            out_shape=[jax.ShapeDtypeStruct((len(p) * capacity * block_len, width), bf16) for p in plan],
            in_specs=[SMEM, SMEM, HBM, VMEM] + [ANY] * len(after),
            out_specs=[VMEM] * len(plan),
            scratch_shapes=[pltpu.SemaphoreType.DMA((groups * capacity,))],
            name="pack",
            compiler_params=params(8),
            cost_estimate=COST,
        )(me[None], send_blocks.transpose(0, 2, 1), in_hbm(cache_latent), padded_rope, *after)

    def migrate():
        packed = pack([(lambda g, s=s: lax.rem(g + s, groups),) for s in range(groups)], ())
        return [packed[0]] + [
            lax.ppermute(packed[s], "dp", [(i, (i + s) % groups) for i in range(groups)])
            for s in range(1, groups)
        ], [(s, 0, lambda g, s=s: lax.rem(g + groups - s, groups)) for s in range(groups)]

    w = output_weight
    x0, *held = first_chunk()
    if not on_line:
        outs = []
        brought = migrate()
        for n, t in enumerate(sizes):
            x = attend(n, held, (), brought) if n else x0
            mine = shift_groups(x)
            if groups % 2 == 0:
                mine += [swap_cores(y) for y in mine]
            own, others = project(where, mine, w, (groups - 1,))
            partials = jnp.concatenate([own, others], axis=0).reshape(groups, t, columns)
            outs.append(lax.psum_scatter(partials, "tp", scatter_dimension=0, tiled=False))
        return jnp.concatenate(outs, axis=0)

    def inward(x):
        return lax.ppermute(x, "tp", INWARD)

    def across(x):
        return lax.ppermute(x, "tp", ACROSS)

    def outward(x):
        return lax.ppermute(x, "tp", OUTWARD)

    def gather(x, after):
        came = shift_groups(x)[1]
        return [x, came, swap_cores(x), swap_cores(stack([came], after))]

    t0, t1, t2, t3 = sizes
    apart = [lambda g, k=k: g ^ k for k in range(4)]
    own_blocks, core_blocks, far_blocks = pack([(apart[0],), (apart[1],), (apart[2], apart[3])], ())
    x_blocks = lax.ppermute(far_blocks, "dp", [(i, i ^ 2) for i in range(groups)])
    x1 = attend(1, held, (x0,))
    half = capacity * block_len
    on_blocks = swap_cores(stack([core_blocks, (x_blocks, half)], (x0,)))
    brought = ((own_blocks, x_blocks, on_blocks), [(0, 0, apart[0]), (1, 0, apart[2]), (2, 0, apart[1]), (2, half, apart[3])])
    own0, rest0 = project(where, gather(x0, (x1,)), w, (3,), (), (x1,))
    in0 = inward(rest0)
    x2 = attend(2, held, (own0, on_blocks))
    own1, rest1 = project(where, gather(x1, (x2,)), w, (3,), (), (x2,))
    in1 = inward(rest1)
    to_across0 = add(2 * t0, [(rest0, 0), (in0, 0)], (own1,))
    on0 = across(to_across0)
    x3 = attend(3, held, (to_across0,), brought)
    own2, rest2 = project(where, gather(x2, (x3,)), w, (3,), (), (x3,))
    in2 = inward(rest2)
    to_across1 = add(2 * t1, [(rest1, 0), (in1, 0)], (own2, on0))
    on1 = across(to_across1)
    own3, rest3 = project(
        where, gather(x3, (own2,)), w, (3,), (), (to_across1,))
    in3 = inward(rest3)
    to_across2 = add(2 * t2, [(rest2, 0), (in2, 0)], (own3,))
    on2 = across(to_across2)
    to_out01 = add_all([(t0, [(rest0, 2 * t0), (on0, 0)]), (t1, [(rest1, 2 * t1), (on1, 0)])],
                       (to_across2,))
    out01 = outward(to_out01)
    to_far = add(t3, [(rest3, 0), (in3, 0)], (to_out01,))
    far_on = across(to_far)
    to_mid = add(t3, [(rest3, t3), (in3, t3)], (to_far,))
    mid_on = across(to_mid)
    done01 = add_all([(t0, [(own0, 0), (in0, 2 * t0), (on0, t0), (out01, 0)]),
                      (t1, [(own1, 0), (in1, 2 * t1), (on1, t1), (out01, t0)])], (to_mid,))
    to_out2 = add(t2, [(rest2, 2 * t2), (on2, 0)], (done01,))
    out2 = outward(to_out2)
    to_out3 = add(t3, [(rest3, 2 * t3), (far_on, 0)], (to_out2,))
    out3 = outward(to_out3)
    done2 = add(t2, [(own2, 0), (in2, 2 * t2), (on2, t2), (out2, 0)], (to_out3,))
    return finish([done01, done2], [(own3, 0), (in3, 2 * t3), (mid_on, 0), (out3, 0)])


def solution(mesh):
    return jax.shard_map(
        body,
        mesh=mesh,
        in_specs=(
            P(("replica", "dp"), "tp", None),
            P(("replica", "dp"), "tp"),
            P(("replica", "dp"), None),
            P(("replica", "dp"), None),
            P(("replica", "dp"), None, None),
            P(("replica", "dp"), None),
            P("tp", None, None),
            P("tp", None, None),
            P("tp", "dp"),
            P(("replica", "dp"), None, None),
            P(("replica", "dp"), None),
            P(("replica", "dp")),
            P(("replica", "dp"), None),
            P(("replica", "dp")),
        ),
        out_specs=P(("replica", "tp"), "dp"),
        check_vma=False,
    )
```

```python
import functools

import jax
import jax.numpy as jnp
import numpy as np
from jax import lax
from jax.experimental import pallas as pl
from jax.experimental.pallas import tpu as pltpu
from jax.sharding import PartitionSpec as P

HIDDEN = -1e30
LANES = 128
MIB = 1024 * 1024
PIECES = 4

SMEM = pl.BlockSpec(memory_space=pltpu.SMEM)
VMEM = pl.BlockSpec(memory_space=pltpu.VMEM)
HBM = pl.BlockSpec(memory_space=pltpu.HBM)
ANY = pl.BlockSpec(memory_space=pl.ANY)


def params(mib):
    return pltpu.CompilerParams(vmem_limit_bytes=mib * MIB)


def dot_nt(a, b):
    return lax.dot_general(a, b, (((1,), (1,)), ((), ())), preferred_element_type=jnp.float32)


def dot(a, b):
    return jnp.dot(a, b, preferred_element_type=jnp.float32)


def chunk_sizes(tok_group):
    if tok_group == 256:
        return (48, 64, 80, 64)
    return (tok_group,)


def rope_rows(rope_t):
    rows = jnp.transpose(rope_t.astype(jnp.float32), (1, 0))
    return jnp.concatenate(
        [rows, jnp.zeros((rows.shape[0], LANES - rows.shape[1]), jnp.float32)], axis=1
    ).astype(jnp.bfloat16)


def build_queries(q, q_nope, q_rope, first, wk, ready=None):
    heads = q_nope.shape[0]
    t = q.shape[0] // heads
    latent = wk.shape[2]
    rope_dim = q_rope.shape[1] // heads
    lane = lax.broadcasted_iota(jnp.int32, (t, LANES), 1)
    one = jnp.where(lane == rope_dim, 1.0, 0.0)
    per_tile = LANES // rope_dim
    for h in range(heads):
        pair = q_rope[first:first + t, h // per_tile * LANES:(h // per_tile + 1) * LANES].astype(jnp.float32)
        turn = h % per_tile * rope_dim
        if turn:
            pair = pltpu.roll(pair, LANES - turn, 1)
        q[h * t:(h + 1) * t, latent:] = jnp.where(lane < rope_dim, pair, one).astype(jnp.bfloat16)
    for h in range(heads):
        if ready is not None:
            ready(h)
        q[h * t:(h + 1) * t, :latent] = dot(q_nope[h, first:first + t, :], wk[h]).astype(jnp.bfloat16)


def prefill(q, keys, att, heads, t, first, prior, fresh, exp_scale):
    latent = att.shape[1]
    together = 1
    while together * 2 <= heads and together * 2 * t <= 384:
        together *= 2
    tile = together * t
    token = first + lax.broadcasted_iota(jnp.int32, (t, fresh), 0)
    key_token = lax.broadcasted_iota(jnp.int32, (t, fresh), 1)
    causal = (key_token <= token)[None]
    end = prior + fresh

    def scores_of(i):
        rows = q[i * tile:(i + 1) * tile, :]
        return dot_nt(rows, keys[:prior, :]), dot_nt(rows, keys[prior:end, :])

    steps = heads // together
    ahead = scores_of(0)
    for i in range(steps):
        s_old, s_new = ahead
        if i + 1 < steps:
            ahead = scores_of(i + 1)
        s_new = jnp.where(causal, s_new.reshape(together, t, fresh), HIDDEN).reshape(tile, fresh)
        top = jnp.maximum(jnp.max(s_old, axis=1, keepdims=True), jnp.max(s_new, axis=1, keepdims=True))
        p_old = jnp.exp2((s_old - top) * exp_scale)
        p_new = jnp.exp2((s_new - top) * exp_scale)
        total = jnp.sum(p_old, axis=1, keepdims=True) + jnp.sum(p_new, axis=1, keepdims=True)
        mixed = dot(p_old.astype(jnp.bfloat16), keys[:prior, :latent]) + dot(
            p_new.astype(jnp.bfloat16), keys[prior:end, :latent])
        att[i * tile:(i + 1) * tile, :] = (mixed / total).astype(jnp.bfloat16)


def head_outputs(out, att, wv, t):
    heads, _, dv = wv.shape
    for h in range(heads):
        out[:, h * dv:(h + 1) * dv] = dot(att[h * t:(h + 1) * t, :], wv[h]).astype(jnp.bfloat16)


def pieces(source, target, sems, first):
    size = source.shape[0] // PIECES
    return [pltpu.make_async_copy(source.at[pl.ds(i * size, size)], target.at[pl.ds(i * size, size)],
                                  sems.at[first + i]) for i in range(PIECES)]


def first_kernel(fresh, exp_scale, me, z, table, offset, q_nope, q_rope_hbm, wk_hbm, wv_hbm, cache_latent,
                 cache_rope, new_latent, new_rope_t, out, keys, wk, wv, q_rope, q, att, sems, wsems):
    heads = q_nope.shape[0]
    t = out.shape[0]
    block_len, latent = cache_latent.shape[1:]
    rope_dim = new_rope_t.shape[0]
    blocks = table.shape[1]
    prior = blocks * block_len
    tok_group = new_latent.shape[0]

    rope_copies = [pltpu.make_async_copy(
        q_rope_hbm.at[pl.ds(at, size)], q_rope.at[pl.ds(at, size)], wsems.at[n])
        for n, (at, size) in enumerate(((0, t), (t, tok_group - t))) if size]
    wk_copies = pieces(wk_hbm, wk, wsems, 2)
    later = pieces(wv_hbm, wv, wsems, 2 + PIECES) + rope_copies[1:]
    for c in wk_copies + rope_copies[:1]:
        c.start()
    copies = []
    for i in range(blocks):
        copies.append(pltpu.make_async_copy(
            cache_latent.at[table[0, i]],
            keys.at[pl.ds(i * block_len, block_len), pl.ds(0, latent)], sems.at[i]))
    copies.append(pltpu.make_async_copy(
        new_latent, keys.at[pl.ds(prior, tok_group), pl.ds(0, latent)], sems.at[blocks]))
    for c in copies:
        c.start(priority=1)

    keys[prior:, latent:] = rope_rows(new_rope_t[...])
    lane = lax.broadcasted_iota(jnp.int32, (block_len, LANES), 1)
    pos = lax.broadcasted_iota(jnp.int32, (block_len, LANES), 0)
    for i in range(blocks):
        hide = jnp.where((lane == rope_dim) & (pos >= offset[0] - i * block_len), HIDDEN, 0.0)
        rope = cache_rope[table[0, i]].astype(jnp.float32) + hide
        keys[i * block_len:(i + 1) * block_len, latent:] = rope.astype(jnp.bfloat16)

    rope_copies[0].wait()

    def ready(h):
        if h * PIECES % heads == 0:
            wk_copies[h * PIECES // heads].wait()

    build_queries(q, q_nope, q_rope, 0, wk, ready)
    for c in copies:
        c.wait()
    for c in later:
        c.start()
    prefill(q, keys, att, heads, t, 0, prior, fresh, exp_scale)
    for c in later:
        c.wait()
    head_outputs(out, att, wv, t)


def pack_kernel(n_after, plan, me, ids, cache_latent, cache_rope, *rest):
    outs, sems = rest[n_after:-1], rest[-1]
    block_len, latent = cache_latent.shape[1:]
    copies = []
    places = []
    for out, targets in zip(outs, plan):
        row = 0
        for target in targets:
            to = target(me[0])
            for k in range(ids.shape[1]):
                places.append((out, row, ids[0, k, to]))
                row += block_len
    for n, (out, row, b) in enumerate(places):
        copies.append(pltpu.make_async_copy(
            cache_latent.at[b], out.at[pl.ds(row, block_len), pl.ds(0, latent)], sems.at[n]))
        copies[-1].start()
    for out, row, b in places:
        out[row:row + block_len, latent:] = cache_rope[b]
    for c in copies:
        c.wait()


def later_kernel(first, fresh, prior, exp_scale, n_after, q_nope, q_rope, wk, wv, keys, *rest):
    out, q, att = rest[n_after:]
    heads = q_nope.shape[0]
    t = out.shape[0]
    build_queries(q, q_nope, q_rope, first, wk)
    prefill(q, keys, att, heads, t, first, prior, fresh, exp_scale)
    head_outputs(out, att, wv, t)


def last_kernel(first, fresh, prior, prefill_len, exp_scale, n_after, spots, got, me, q_nope, q_rope, wk, wv, keys,
                flat_latent, cache_rope, decode_table, decode_length, *rest):
    received = rest[:-5 - n_after]
    out, q, att, dkeys, sems = rest[-5:]
    groups = len(spots)
    heads = q_nope.shape[0]
    t = out.shape[0]
    pool, block_len, _ = cache_rope.shape
    latent = flat_latent.shape[1]
    ext = pool * block_len + groups * got
    tail = dkeys.shape[0] - ext
    start = keys.shape[0] - tail
    copies = []
    for i in range(PIECES):
        rows = pl.ds(i * pool * block_len // PIECES, pool * block_len // PIECES)
        copies.append(pltpu.make_async_copy(
            flat_latent.at[rows], dkeys.at[rows, pl.ds(0, latent)], sems.at[i]))
    for c in copies:
        c.start()
    for i in range(pool):
        dkeys[i * block_len:(i + 1) * block_len, latent:] = cache_rope[i]
    for n, row, source in spots:
        at = pl.multiple_of(pool * block_len + source(me[0]) * got, block_len)
        dkeys[pl.ds(at, got), :] = received[n][row:row + got, :]
    dkeys[ext:, :] = keys[start:, :]

    build_queries(q, q_nope, q_rope, first, wk)
    prefill(q, keys, att, heads, t, first, prior, fresh, exp_scale)

    slots, decodes = decode_table.shape
    for c in copies:
        c.wait()
    span = dkeys.shape[0]
    key = lax.broadcasted_iota(jnp.int32, (decodes, span), 1)
    request = lax.broadcasted_iota(jnp.int32, (decodes, span), 0)
    block = key // block_len
    pos = key % block_len
    own_key = key - ext + (start - prior) == request + prefill_len
    count = jnp.where(own_key, 1.0, 0.0)
    row = lax.broadcasted_iota(jnp.int32, (decodes, LANES), 0)

    def column(read):
        value = jnp.zeros((decodes, LANES), jnp.int32)
        for r in range(decodes):
            value = jnp.where(row == r, read(r), value)
        return value[:, :1]

    length = column(lambda r: decode_length[r])
    for m in range(slots):
        hit = (block == column(lambda r: decode_table[m, r])) & (pos + m * block_len < length) & (
            key < ext)
        count = count + jnp.where(hit, 1.0, 0.0)
    count = count[None]
    at = prefill_len - first
    half = heads // 2 if heads % 2 == 0 else heads
    for lo in range(0, heads, half):
        rows = jnp.concatenate(
            [q[h * t + at:h * t + at + decodes, :] for h in range(lo, lo + half)], axis=0)
        s = dot_nt(rows, dkeys[...]).reshape(half, decodes, span)
        s = jnp.where(count > 0.0, s, HIDDEN)
        top = jnp.max(s, axis=2, keepdims=True)
        p = count * jnp.exp2((s - top) * exp_scale)
        total = jnp.sum(p, axis=2, keepdims=True).reshape(half * decodes, 1)
        p = p.reshape(half * decodes, span).astype(jnp.bfloat16)
        mixed = (dot(p, dkeys[:, :latent]) / total).astype(jnp.bfloat16)
        for h in range(lo, lo + half):
            att[h * t + at:h * t + at + decodes, :] = mixed[(h - lo) * decodes:(h - lo + 1) * decodes]
    head_outputs(out, att, wv, t)


COST = pl.CostEstimate(flops=1000, bytes_accessed=1000, transcendentals=0)
LONG = pl.CostEstimate(flops=40_000_000_000, bytes_accessed=1000, transcendentals=0)
SHORT = pl.CostEstimate(flops=6_000_000_000, bytes_accessed=1000, transcendentals=0)


def in_hbm(x):
    return pltpu.with_memory_space_constraint(x, pltpu.HBM)


def project_kernel(n_parts, tails, places, me, z, w, *rest):
    parts, rest, x = rest[:n_parts], rest[n_parts:], rest[-1]
    own, outs = rest[-2 - len(tails)], rest[-1 - len(tails):-1]
    t = own.shape[0]
    lead = outs[-1].shape[0] - tails[-1] * t
    if lead:
        outs[-1][:lead, :] = rest[0][...]
    for i, part in enumerate(parts):
        place = 0
        for g, row in enumerate(places):
            for p, column in enumerate(row):
                place = jnp.where((me[0] == g) & (z[0] == p), column[i], place)
        x[pl.ds(pl.multiple_of(place * t, t), t), :] = part[...]
    columns = w.shape[1]
    step = 256 if columns % 256 == 0 else columns
    for at in range(0, columns, step):
        y = dot(x[...], w[:, at:at + step]).astype(jnp.bfloat16)
        own[:, at:at + step] = y[:t]
        row = t
        for i, n in enumerate(tails):
            skip = lead if i == len(tails) - 1 else 0
            outs[i][skip:skip + n * t, at:at + step] = y[row:row + n * t]
            row += n * t


def project(where, parts, w, tails, earlier=(), after=()):
    depth, columns = w.shape
    rows = sum(p.shape[0] for p in parts)
    t = rows // (1 + sum(tails))
    sizes = [t] + [n * t for n in tails]
    sizes[-1] += sum(e.shape[0] for e in earlier)
    places, me, z = where
    return pl.pallas_call(
        functools.partial(project_kernel, len(parts), tails, places),
        out_shape=[jax.ShapeDtypeStruct((n, columns), jnp.bfloat16) for n in sizes],
        in_specs=[SMEM, SMEM, VMEM] + [VMEM] * (len(parts) + len(earlier)) + [ANY] * len(after),
        out_specs=[VMEM] * len(sizes),
        scratch_shapes=[pltpu.VMEM((rows, depth), jnp.bfloat16)],
        name="project",
        compiler_params=params(12),
        cost_estimate=COST,
    )(me[None], z[None], w, *parts, *earlier, *after)


def add_kernel(sums, *refs):
    out = refs[-1]
    row = i = 0
    for rows, spans in sums:
        total = None
        for at in spans:
            x = refs[i][at:at + rows, :].astype(jnp.float32)
            total = x if total is None else total + x
            i += 1
        out[row:row + rows, :] = total.astype(jnp.bfloat16)
        row += rows


def add_all(sums, after=()):
    terms = [x for _, parts in sums for x, _ in parts]
    return pl.pallas_call(
        functools.partial(add_kernel, [(rows, [at for _, at in parts]) for rows, parts in sums]),
        out_shape=jax.ShapeDtypeStruct((sum(rows for rows, _ in sums), terms[0].shape[1]), jnp.bfloat16),
        in_specs=[VMEM] * len(terms) + [ANY] * len(after),
        out_specs=VMEM,
        name="add",
        compiler_params=params(8),
        cost_estimate=COST,
    )(*terms, *after)


def add(rows, terms, after=()):
    return add_all([(rows, terms)], after)


def finish_kernel(n_ready, spans, *refs):
    out = refs[-1]
    row = 0
    for ref in refs[:n_ready]:
        out[row:row + ref.shape[0], :] = ref[...]
        row += ref.shape[0]
    add_kernel([(out.shape[0] - row, spans)], *refs[n_ready:-1], out.at[row:, :])


def finish(ready, terms):
    rows = sum(r.shape[0] for r in ready) + terms[0][0].shape[0]
    return pl.pallas_call(
        functools.partial(finish_kernel, len(ready), [at for _, at in terms]),
        out_shape=jax.ShapeDtypeStruct((rows, terms[0][0].shape[1]), jnp.bfloat16),
        in_specs=[VMEM] * (len(ready) + len(terms)),
        out_specs=VMEM,
        name="finish",
        compiler_params=params(8),
        cost_estimate=COST,
    )(*ready, *[x for x, _ in terms])


def gathered_ids(groups, me):
    if groups % 2:
        return [(me - s) % groups for s in range(groups)]
    return [(who - 2 * s) % groups for who in (me, me ^ 1) for s in range(groups // 2)]


def shift_groups(x):
    groups = lax.axis_size("dp")
    step = 1 if groups % 2 else 2
    return [x] + [lax.ppermute(x, "dp", [(i, (i + s) % groups) for i in range(groups)])
                  for s in range(step, groups, step)]


def stack_kernel(firsts, *refs):
    out, at = refs[-1], 0
    for ref, first in zip(refs, firsts):
        n = ref.shape[0] - first
        out[at:at + n, :] = ref[first:, :]
        at += n


def stack(parts, after=()):
    parts = [p if isinstance(p, tuple) else (p, 0) for p in parts]
    rows = sum(p.shape[0] - first for p, first in parts)
    return pl.pallas_call(
        functools.partial(stack_kernel, [first for _, first in parts]),
        out_shape=jax.ShapeDtypeStruct((rows, parts[0][0].shape[1]), jnp.bfloat16),
        in_specs=[VMEM] * len(parts) + [ANY] * len(after),
        out_specs=VMEM,
        name="stack",
        compiler_params=params(4),
        cost_estimate=COST,
    )(*[p for p, _ in parts], *after)


def swap_cores(x):
    return lax.ppermute(x, "dp", [(i, i ^ 1) for i in range(lax.axis_size("dp"))])


LINE_ORDER = ((0, 3, 2, 1), (1, 3, 2, 0), (2, 0, 1, 3), (3, 0, 1, 2))
INWARD = [(0, 1), (3, 2)]
ACROSS = [(1, 2), (2, 1)]
OUTWARD = [(1, 0), (2, 3)]


def body(
    query_nope,
    query_rope,
    new_latent,
    new_rope,
    cache_latent,
    cache_rope,
    absorb_key,
    absorb_value,
    output_weight,
    send_blocks,
    prefill_table,
    prefill_offset,
    decode_table,
    decode_length,
):
    tok_group, heads, nope_dim = query_nope.shape
    pool, block_len, latent = cache_latent.shape
    rope_dim = new_rope.shape[1]
    capacity = send_blocks.shape[2]
    groups = lax.axis_size("dp")
    decodes = decode_length.shape[0]
    prefill_len = tok_group - decodes
    dv = absorb_value.shape[2]
    columns = output_weight.shape[1]
    exp_scale = float((nope_dim + rope_dim) ** (-0.5) * 1.4426950408889634)
    blocks = prefill_table.shape[1]
    prior = blocks * block_len
    width = latent + LANES
    on_line = lax.axis_size("tp") == 4 and groups == 4
    bf16 = jnp.bfloat16

    me = lax.axis_index("dp")
    z = lax.axis_index("tp")
    places = []
    for g in range(groups):
        came = gathered_ids(groups, g)
        if on_line:
            places.append([[order.index(k) for k in came] for order in LINE_ORDER])
        else:
            places.append([came])
    where = (places, me, z if on_line else z * 0)

    padded_rope = jnp.pad(
        cache_rope.reshape(pool, block_len, rope_dim), ((0, 0), (0, 0), (0, LANES - rope_dim)))
    q_nope = query_nope.transpose(1, 0, 2)
    sizes = chunk_sizes(tok_group)
    starts = [sum(sizes[:i]) for i in range(len(sizes))]

    def fresh_of(n):
        seen = min(starts[n] + sizes[n], prefill_len)
        return min(-(-seen // LANES) * LANES, tok_group)

    def scratch(t):
        return [pltpu.VMEM((heads * t, width), bf16), pltpu.VMEM((heads * t, latent), bf16)]

    def first_chunk():
        t = sizes[0]
        return pl.pallas_call(
            functools.partial(first_kernel, fresh_of(0), exp_scale),
            out_shape=[jax.ShapeDtypeStruct((t, heads * dv), bf16),
                       jax.ShapeDtypeStruct((prior + tok_group, width), bf16),
                       jax.ShapeDtypeStruct(absorb_key.shape, bf16),
                       jax.ShapeDtypeStruct(absorb_value.shape, bf16),
                       jax.ShapeDtypeStruct(query_rope.shape, bf16)],
            in_specs=[SMEM] * 4 + [VMEM, HBM, HBM, HBM, HBM, VMEM, HBM, VMEM],
            out_specs=[VMEM] * 5,
            scratch_shapes=[
                *scratch(t),
                pltpu.SemaphoreType.DMA((blocks + 1,)),
                pltpu.SemaphoreType.DMA((2 * PIECES + 2,)),
            ],
            name="attend_first",
            compiler_params=params(20),
            cost_estimate=LONG,
        )(me[None], z[None], prefill_table, prefill_offset, q_nope, in_hbm(query_rope), in_hbm(absorb_key),
          in_hbm(absorb_value), in_hbm(cache_latent), padded_rope,
          in_hbm(new_latent), new_rope.T)

    def attend(n, held, after, brought=None):
        keys, wk, wv, q_rope = held
        t = sizes[n]
        args = [q_nope, q_rope, wk, wv, keys]
        specs = [VMEM] * 5
        scratches = scratch(t)
        limit = 20
        static = (starts[n], fresh_of(n), prior)
        if n == len(sizes) - 1:
            brought, spots = brought
            kernel = functools.partial(
                last_kernel, *static, prefill_len, exp_scale, len(after), spots, capacity * block_len)
            args = [me[None]] + args + [
                in_hbm(cache_latent.reshape(pool * block_len, latent)), padded_rope, decode_table.T, decode_length, *brought]
            specs = [SMEM] + specs + [HBM, VMEM, SMEM, SMEM] + [VMEM] * len(brought)
            span = pool * block_len + groups * capacity * block_len + min(LANES, tok_group)
            scratches += [pltpu.VMEM((span, width), bf16), pltpu.SemaphoreType.DMA((PIECES,))]
            limit = 26
        else:
            kernel = functools.partial(later_kernel, *static, exp_scale, len(after))
        return pl.pallas_call(
            kernel,
            out_shape=jax.ShapeDtypeStruct((t, heads * dv), bf16),
            in_specs=specs + [ANY] * len(after),
            out_specs=VMEM,
            scratch_shapes=scratches,
            name="attend",
            compiler_params=params(limit),
            cost_estimate=SHORT if n == len(sizes) - 1 else LONG,
        )(*args, *after)

    def pack(plan, after):
        return pl.pallas_call(
            functools.partial(pack_kernel, len(after), plan),
            out_shape=[jax.ShapeDtypeStruct((len(p) * capacity * block_len, width), bf16) for p in plan],
            in_specs=[SMEM, SMEM, HBM, VMEM] + [ANY] * len(after),
            out_specs=[VMEM] * len(plan),
            scratch_shapes=[pltpu.SemaphoreType.DMA((groups * capacity,))],
            name="pack",
            compiler_params=params(8),
            cost_estimate=COST,
        )(me[None], send_blocks.transpose(0, 2, 1), in_hbm(cache_latent), padded_rope, *after)

    def migrate():
        packed = pack([(lambda g, s=s: lax.rem(g + s, groups),) for s in range(groups)], ())
        return [packed[0]] + [
            lax.ppermute(packed[s], "dp", [(i, (i + s) % groups) for i in range(groups)])
            for s in range(1, groups)
        ], [(s, 0, lambda g, s=s: lax.rem(g + groups - s, groups)) for s in range(groups)]

    w = output_weight
    x0, *held = first_chunk()
    if not on_line:
        outs = []
        brought = migrate()
        for n, t in enumerate(sizes):
            x = attend(n, held, (), brought) if n else x0
            mine = shift_groups(x)
            if groups % 2 == 0:
                mine += [swap_cores(y) for y in mine]
            own, others = project(where, mine, w, (groups - 1,))
            partials = jnp.concatenate([own, others], axis=0).reshape(groups, t, columns)
            outs.append(lax.psum_scatter(partials, "tp", scatter_dimension=0, tiled=False))
        return jnp.concatenate(outs, axis=0)

    def inward(x):
        return lax.ppermute(x, "tp", INWARD)

    def across(x):
        return lax.ppermute(x, "tp", ACROSS)

    def outward(x):
        return lax.ppermute(x, "tp", OUTWARD)

    def gather(x, after):
        came = shift_groups(x)[1]
        return [x, came, swap_cores(x), swap_cores(stack([came], after))]

    t0, t1, t2, t3 = sizes
    apart = [lambda g, k=k: g ^ k for k in range(4)]
    own_blocks, core_blocks, far_blocks = pack([(apart[0],), (apart[1],), (apart[2], apart[3])], ())
    x_blocks = lax.ppermute(far_blocks, "dp", [(i, i ^ 2) for i in range(groups)])
    x1 = attend(1, held, (x0,))
    half = capacity * block_len
    on_blocks = swap_cores(stack([core_blocks, (x_blocks, half)], (x0,)))
    brought = ((own_blocks, x_blocks, on_blocks), [(0, 0, apart[0]), (1, 0, apart[2]), (2, 0, apart[1]), (2, half, apart[3])])
    own0, rest0 = project(where, gather(x0, (x1,)), w, (3,), (), (x1,))
    in0 = inward(rest0)
    x2 = attend(2, held, (own0, on_blocks))
    own1, rest1 = project(where, gather(x1, (x2,)), w, (3,), (), (x2,))
    in1 = inward(rest1)
    to_across0 = add(2 * t0, [(rest0, 0), (in0, 0)], (own1,))
    x3 = attend(3, held, (to_across0,), brought)
    own2, rest2, near2 = project(where, gather(x2, (x3,)), w, (2, 1), (), (x3,))
    in2 = inward(rest2)
    on0 = across(stack([to_across0], (own2,)))
    to_across1 = add(2 * t1, [(rest1, 0), (in1, 0)], (own2,))
    on1 = across(to_across1)
    own3, rest3, near = project(
        where, gather(x3, (own2,)), w, (2, 1), (near2,), (to_across1,))
    in3 = inward(rest3)
    to_far2 = add(t2, [(rest2, 0), (in2, 0)], (own3, on0))
    far2_on = across(to_far2)
    near_in = inward(near)
    to_out01 = add_all([(t0, [(rest0, 2 * t0), (on0, 0)]), (t1, [(rest1, 2 * t1), (on1, 0)])],
                       (to_far2,))
    out01 = outward(to_out01)
    to_out2 = add(t2, [(near2, 0), (far2_on, 0)], (to_out01,))
    out2 = outward(to_out2)
    to_far3 = add(t3, [(rest3, 0), (in3, 0)], (to_out2,))
    far3_on = across(to_far3)
    to_mids = add_all([(t2, [(rest2, t2), (in2, t2)]), (t3, [(rest3, t3), (in3, t3)])], (to_far3,))
    mids_on = across(to_mids)
    done01 = add_all([(t0, [(own0, 0), (in0, 2 * t0), (on0, t0), (out01, 0)]),
                      (t1, [(own1, 0), (in1, 2 * t1), (on1, t1), (out01, t0)])], (to_mids,))
    to_out3 = add(t3, [(near, t2), (far3_on, 0)], (done01,))
    out3 = outward(to_out3)
    done2 = add(t2, [(own2, 0), (near_in, 0), (mids_on, 0), (out2, 0)], (to_out3,))
    return finish([done01, done2], [(own3, 0), (near_in, t2), (mids_on, t2), (out3, 0)])


def solution(mesh):
    return jax.shard_map(
        body,
        mesh=mesh,
        in_specs=(
            P(("replica", "dp"), "tp", None),
            P(("replica", "dp"), "tp"),
            P(("replica", "dp"), None),
            P(("replica", "dp"), None),
            P(("replica", "dp"), None, None),
            P(("replica", "dp"), None),
            P("tp", None, None),
            P("tp", None, None),
            P("tp", "dp"),
            P(("replica", "dp"), None, None),
            P(("replica", "dp"), None),
            P(("replica", "dp")),
            P(("replica", "dp"), None),
            P(("replica", "dp")),
        ),
        out_specs=P(("replica", "tp"), "dp"),
        check_vma=False,
    )
```
